128 devices in a mesh: ctx: 16 (over y, x_hi, core), wt: 8 (over x_lo, z).
Axes of the slice: x: 4 (x_hi: 2, x_lo: 2; x = x_hi * 2 + x_lo), y: 4, z: 4, core: 2. Of those that a mesh axis runs over, the one named last changes fastest.
Arguments:
- inputs: bfloat16 [8, 4096, 512], P('wt', 'ctx'), may hold values from -6 to 6
- lengths: int32 [8], P('wt'), may hold values from 1024 to 4096, as said below
- cotangent: bfloat16 [8, 4096, 512], P('wt', 'ctx'), may hold values from -6 to 6
- glu_gain: bfloat16 [512], P('wt'), may hold values from 0.5 to 1.5
- glu_value: bfloat16 [512, 512], P('wt'), may hold values from -0.25 to 0.25
- glu_gate: bfloat16 [512, 512], P('wt'), may hold values from -0.25 to 0.25
- conv_gain: bfloat16 [512], P('wt'), may hold values from 0.5 to 1.5
- wide_weight: bfloat16 [512, 2048], P('wt'), may hold values from -0.25 to 0.25
- narrow_weight: bfloat16 [3, 512, 256], P(None, 'wt'), may hold values from -0.15625 to 0.15625
- mid_gain: bfloat16 [2048], P('wt'), may hold values from 0.5 to 1.5
- depth_weight: bfloat16 [9, 2048], P(None, 'wt'), may hold values from -2 to 2
- point_weight: bfloat16 [2048, 256], P('wt'), may hold values from -0.125 to 0.125
- attn_gain: bfloat16 [512], P('wt'), may hold values from 0.5 to 1.5
- query_weight: bfloat16 [512, 512], P('wt'), may hold values from -0.5 to 0.5
- key_weight: bfloat16 [512, 512], P('wt'), may hold values from -0.25 to 0.25
- value_weight: bfloat16 [512, 512], P('wt'), may hold values from -0.25 to 0.25
- output_weight: bfloat16 [512, 512], P('wt'), may hold values from -1.5 to 1.5
- ffn_gain: bfloat16 [512], P('wt'), may hold values from 0.5 to 1.5
- ffn_in: bfloat16 [512, 2048], P('wt'), may hold values from -0.25 to 0.25
- ffn_out: bfloat16 [2048, 512], P('wt'), may hold values from -0.125 to 0.125
Outputs:
- output: bfloat16 [8, 4096, 512], P('wt', 'ctx')
- input_grad: float32 [8, 4096, 512], P('wt', 'ctx')
- grad_glu_gain: float32 [512], P('wt')
- grad_glu_value: float32 [512, 512], P('wt')
- grad_glu_gate: float32 [512, 512], P('wt')
- grad_conv_gain: float32 [512], P('wt')
- grad_wide_weight: float32 [512, 2048], P('wt')
- grad_narrow_weight: float32 [3, 512, 256], P(None, 'wt')
- grad_mid_gain: float32 [2048], P('wt')
- grad_depth_weight: float32 [9, 2048], P(None, 'wt')
- grad_point_weight: float32 [2048, 256], P('wt')
- grad_attn_gain: float32 [512], P('wt')
- grad_query_weight: float32 [512, 512], P('wt')
- grad_key_weight: float32 [512, 512], P('wt')
- grad_value_weight: float32 [512, 512], P('wt')
- grad_output_weight: float32 [512, 512], P('wt')
- grad_ffn_gain: float32 [512], P('wt')
- grad_ffn_in: float32 [512, 2048], P('wt')
- grad_ffn_out: float32 [2048, 512], P('wt')
The draws below stay inside these ranges and needn't reach their ends.
Inputs may be any that keep to these rules, and one draw needn't show every extreme that they name: `lengths`: valid slots of each sequence, which are its first slots; one sequence has exactly 4096 and one exactly 1024.
All inputs are finite; a program needn't handle non-finite values.
Results may differ from the reference program's by a relative error of at most 0.03.
Values may be sent and summed in bfloat16 or wider, within the bound.
No kernel may reach another device: no remote copies, remote signals or barrier semaphores. Data moves between devices by JAX's collectives and lax.ppermute only.
A program may use at most 256 MiB of HBM per device.

```python
import jax
import jax.numpy as jnp
from jax import lax

D = 512
HEADS = 8
HEAD = 64
FF = 2048
HALF = 256
SEQ = 4096
SEQS = 8


def draw_lengths(key, part):
    drawn = jax.random.randint(key, (SEQS,), SEQ // 4, SEQ + 1, dtype=jnp.int32)
    order = jax.random.permutation(jax.random.fold_in(key, 11), SEQS)
    drawn = drawn.at[order[0]].set(SEQ)
    return drawn.at[order[1]].set(SEQ // 4)


def shard_levels(own_key, extent, cuts, least, high):
    level, own = 1.0, jax.random.fold_in(own_key, 6)
    for axis_at, blocks in cuts:
        heights = jnp.exp(jax.random.uniform(jax.random.fold_in(own, axis_at), (blocks,), jnp.float32, least / len(cuts), high / len(cuts)))
        level = level * jnp.repeat(heights, extent[axis_at] // blocks).reshape([-1 if axis == axis_at else 1 for axis in range(len(extent))])
    return level


def noise(key, shape, deviation, bound, shards=(), kind=jnp.bfloat16):
    values = jax.random.normal(key, shape, jnp.float32) * deviation
    if len(shards) > 0:
        values = shard_levels(key, shape, shards, -0.22, 0.18) * values
    return jnp.clip(values, min=-bound, max=bound).astype(kind)


def setup_inputs(seed: int = 0) -> dict:
    splits = jax.random.split(jax.random.key(seed), 21)
    return {
        "inputs": noise(splits[0], (SEQS, SEQ, D), 1.0, 6.0, ((0, 8), (1, 16))),
        "lengths": draw_lengths(jax.random.fold_in(splits[20], 71), 0),
        "cotangent": noise(splits[2], (SEQS, SEQ, D), 1.0, 6.0, ((0, 8), (1, 16))),
        "glu_gain": jnp.clip(1.0 + 0.1 * jax.random.normal(splits[3], (D,), jnp.float32), 0.5, 1.5).astype(jnp.bfloat16),
        "glu_value": noise(splits[4], (D, D), D ** -0.5, 0.25, ((0, 8),)),
        "glu_gate": noise(splits[5], (D, D), D ** -0.5, 0.25, ((0, 8),)),
        "conv_gain": jnp.clip(1.0 + 0.1 * jax.random.normal(splits[6], (D,), jnp.float32), 0.5, 1.5).astype(jnp.bfloat16),
        "wide_weight": noise(splits[7], (D, FF), D ** -0.5, 0.25, ((0, 8),)),
        "narrow_weight": noise(splits[8], (3, D, HALF), (3 * D) ** -0.5, 0.15625, ((1, 8),)),
        "mid_gain": jnp.clip(1.0 + 0.1 * jax.random.normal(splits[9], (FF,), jnp.float32), 0.5, 1.5).astype(jnp.bfloat16),
        "depth_weight": noise(splits[10], (9, FF), 9 ** -0.5, 2.0, ((1, 8),)),
        "point_weight": noise(splits[11], (FF, HALF), FF ** -0.5, 0.125, ((0, 8),)),
        "attn_gain": jnp.clip(1.0 + 0.1 * jax.random.normal(splits[12], (D,), jnp.float32), 0.5, 1.5).astype(jnp.bfloat16),
        "query_weight": noise(splits[13], (D, D), (D // 4) ** -0.5, 0.5, ((0, 8),)),
        "key_weight": noise(splits[14], (D, D), D ** -0.5, 0.25, ((0, 8),)),
        "value_weight": noise(splits[15], (D, D), D ** -0.5, 0.25, ((0, 8),)),
        "output_weight": noise(splits[16], (D, D), (D // 32) ** -0.5, 1.5, ((0, 8),)),
        "ffn_gain": jnp.clip(1.0 + 0.1 * jax.random.normal(splits[17], (D,), jnp.float32), 0.5, 1.5).astype(jnp.bfloat16),
        "ffn_in": noise(splits[18], (D, FF), D ** -0.5, 0.25, ((0, 8),)),
        "ffn_out": noise(splits[19], (FF, D), FF ** -0.5, 0.125, ((0, 8),)),
    }


@jax.custom_vjp
def low(v):
    return lax.optimization_barrier(v.astype(jnp.bfloat16)).astype(jnp.float32)

@jax.custom_vjp
def low_back(v):
    return v

def low_keep(v):
    return (low(v), None)

def low_pass(kept, grad):
    return (grad,)

def back_keep(v):
    return (v, None)

def back_low(kept, grad):
    return (low(grad),)
low.defvjp(low_keep, low_pass)
low_back.defvjp(back_keep, back_low)
EPSILON = 1e-06

def matmul(left, right):
    return jnp.dot(left, right, precision=lax.Precision.HIGHEST)

def layer_norm(value, gain):
    average = lax.optimization_barrier(jnp.mean(value, -1, keepdims=True))
    centred = value - average
    spread = lax.optimization_barrier(jnp.mean(centred * centred, -1, keepdims=True))
    return centred * lax.rsqrt(spread + EPSILON) * gain

def shift_rows(value, offset):
    if offset > 0:
        return jnp.concatenate([value[offset:], jnp.zeros((offset, value.shape[1]), jnp.float32)], 0)
    if offset < 0:
        return jnp.concatenate([jnp.zeros((-offset, value.shape[1]), jnp.float32), value[:offset]], 0)
    return value

def smooth_unit(value):
    return value * jax.nn.sigmoid(value)

def attention(queries, keys, values, key_valid):
    block = min(512, SEQ)
    factor = HEAD ** (-0.5)

    def one_block(part):
        logits = jnp.einsum('rhe,she->hrs', part, keys, precision=lax.Precision.HIGHEST) * factor
        logits = low_back(logits)
        logits = jnp.where(key_valid[None, None, :], logits, -1e+30)
        highest = lax.optimization_barrier(jnp.max(logits, -1, keepdims=True))
        expo = jnp.exp(logits - highest)
        probs = expo / lax.optimization_barrier(jnp.sum(expo, -1, keepdims=True))
        return jnp.einsum('hrs,she->rhe', low(probs), values, precision=lax.Precision.HIGHEST)
    blocks = queries.reshape(SEQ // block, block, HEADS, HEAD)
    return lax.map(jax.checkpoint(one_block), blocks).reshape(SEQ, D)

def forward(hidden, weights, valid):
    glu_gain, glu_value, glu_gate, conv_gain, wide_weight, narrow_weight, mid_gain, depth_weight, point_weight, attn_gain, query_weight, key_weight, value_weight, output_weight, ffn_gain, ffn_in, ffn_out = weights
    row_mask = valid[:, None]
    first_in = low(layer_norm(hidden, glu_gain))
    value_part = low_back(matmul(first_in, glu_value))
    gate_part = low_back(matmul(first_in, glu_gate))
    after_glu = hidden + value_part * jax.nn.sigmoid(gate_part)
    conv_in = low(layer_norm(after_glu, conv_gain) * row_mask)
    wide = smooth_unit(low_back(matmul(conv_in, wide_weight)))
    stacked = jnp.concatenate([shift_rows(conv_in, -1), conv_in, shift_rows(conv_in, 1)], 1)
    narrow = smooth_unit(low_back(matmul(stacked, narrow_weight.reshape(3 * D, HALF))))
    mixed = wide + jnp.pad(narrow, ((0, 0), (0, FF - HALF)))
    mid_in = low(layer_norm(mixed, mid_gain) * row_mask)
    spread = sum((shift_rows(mid_in, tap - 4) * depth_weight[tap] for tap in range(9)))
    spread = low(low_back(spread))
    separable = low_back(matmul(spread, point_weight))
    after_conv = after_glu + jnp.pad(separable, ((0, 0), (0, D - HALF)))
    attn_in = low(layer_norm(after_conv, attn_gain))
    queries = low(low_back(matmul(attn_in, query_weight))).reshape(SEQ, HEADS, HEAD)
    keys = low(low_back(matmul(attn_in, key_weight))).reshape(SEQ, HEADS, HEAD)
    values = low(low_back(matmul(attn_in, value_weight))).reshape(SEQ, HEADS, HEAD)
    heads_out = low(low_back(attention(queries, keys, values, valid > 0)))
    after_attn = after_conv + low_back(matmul(heads_out, output_weight))
    ffn_input = low(layer_norm(after_attn, ffn_gain))
    activated = low(smooth_unit(low_back(matmul(ffn_input, ffn_in))))
    ffn_result = low_back(matmul(activated, ffn_out))
    return (after_attn + ffn_result) * row_mask

def reference(inputs, lengths, cotangent, glu_gain, glu_value, glu_gate, conv_gain, wide_weight, narrow_weight, mid_gain, depth_weight, point_weight, attn_gain, query_weight, key_weight, value_weight, output_weight, ffn_gain, ffn_in, ffn_out):
    weights = tuple((weight.astype(jnp.float32) for weight in (glu_gain, glu_value, glu_gate, conv_gain, wide_weight, narrow_weight, mid_gain, depth_weight, point_weight, attn_gain, query_weight, key_weight, value_weight, output_weight, ffn_gain, ffn_in, ffn_out)))
    positions = jnp.arange(SEQ, dtype=jnp.int32)

    def one_sequence(totals, item):
        sequence, length, cot_rows = item
        valid = (positions < length).astype(jnp.float32)

        def run(hidden, *params):
            return forward(hidden, params, valid)
        result, pull = jax.vjp(run, sequence.astype(jnp.float32), *weights)
        grads = pull(cot_rows.astype(jnp.float32))
        totals = tuple((total + grad_one for total, grad_one in zip(totals, grads[1:])))
        return (totals, (result.astype(jnp.bfloat16), grads[0]))
    zeros = tuple((jnp.zeros(weight.shape, jnp.float32) for weight in weights))
    totals, (outputs, input_grads) = lax.scan(one_sequence, zeros, (inputs, lengths, cotangent))
    return (outputs, input_grads, totals[0], totals[1], totals[2], totals[3], totals[4], totals[5], totals[6], totals[7], totals[8], totals[9], totals[10], totals[11], totals[12], totals[13], totals[14], totals[15], totals[16])
```

```python
import functools

import jax
import jax.numpy as jnp
import numpy as np
from jax import lax
from jax.experimental import pallas as pl
from jax.experimental.pallas import tpu as pltpu
from jax.sharding import Mesh
from jax.sharding import PartitionSpec as P

HEADS = 8
HEAD = 64
EPSILON = 1e-06
AXES = ("y", "xh", "core", "xl", "z")
SIZES = (4, 2, 2, 2, 4)
CTX = ("y", "xh", "core")
CHIPS = ("y", "xh")
WT = ("xl", "z")
LOG2E = 1.4426950408889634
BF = jnp.bfloat16
F32 = jnp.float32


def moves(target):
    pairs = []
    for source in range(int(np.prod(SIZES))):
        place = [int(v) for v in np.unravel_index(source, SIZES)]
        goal = target(*place)
        if goal is not None:
            pairs.append((source, int(np.ravel_multi_index(tuple(goal), SIZES))))
    return pairs


def shift(dy=0, dxh=0, dc=0, dxl=0, dz=0):
    return moves(
        lambda y, xh, c, xl, z: (
            (y + dy) % 4, (xh + dxh) % 2, (c + dc) % 2, (xl + dxl) % 2, (z + dz) % 4,
        )
    )


def along(step):
    def target(y, xh, c, xl, z):
        place = y * 4 + xh * 2 + c + step
        if place < 0 or place > 15:
            return None
        return (place // 4, place // 2 % 2, place % 2, xl, z)
    return moves(target)


def send(value, pairs):
    return lax.ppermute(value, AXES, pairs)


def matmul(left, right):
    return jnp.dot(left, right, preferred_element_type=F32)


def contract(left, right, ldim, rdim):
    return lax.dot_general(
        left, right, (((ldim,), (rdim,)), ((), ())), preferred_element_type=F32
    )


def inner_rows(left, right):
    return contract(left, right, 0, 0)


def outer_cols(left, right):
    return contract(left, right, 1, 1)


def smooth_unit(value):
    return value * jax.nn.sigmoid(value)


def smooth_slope(value):
    sigma = jax.nn.sigmoid(value)
    return sigma * (1.0 + value * (1.0 - sigma))


def layer_norm(value, gain):
    average = jnp.mean(value, -1, keepdims=True)
    centred = value - average
    scale = lax.rsqrt(jnp.mean(centred * centred, -1, keepdims=True) + EPSILON)
    normal = centred * scale
    return (normal * gain, normal, scale)


def norm_back(incoming, normal, scale, gain):
    scaled = incoming * gain
    gain_grad = jnp.sum(incoming * normal, 0)
    value_grad = scale * (
        scaled
        - jnp.mean(scaled, -1, keepdims=True)
        - normal * jnp.mean(scaled * normal, -1, keepdims=True)
    )
    return (value_grad, gain_grad)


def with_halo(block, width):
    low = send(block[block.shape[0] - width:], along(1))
    high = send(block[:width], along(-1))
    return jnp.concatenate([low, block, high], axis=0)


def rotate(stacked, amount):
    count = stacked.shape[0]
    return lax.dynamic_slice_in_dim(
        jnp.concatenate([stacked, stacked], 0), (count - amount) % count, count, 0
    )


def gather(own):
    core, xl, z = (lax.axis_index(a) for a in ("core", "xl", "z"))
    rows, cols = own.shape
    half, quarter = rows // 2, rows // 4
    mine = lax.dynamic_slice_in_dim(own, core * half, half, 0)
    other = send(mine, shift(dxl=1))
    two = jnp.where(xl == 0, jnp.stack([mine, other]), jnp.stack([other, mine]))
    up = send(two, shift(dz=1))
    down = send(two, shift(dz=-1))
    up2 = send(up[:, :quarter], shift(dz=1))
    down2 = send(down[:, quarter:], shift(dz=-1))
    far = jnp.concatenate([up2, down2], 1)
    placed = rotate(jnp.stack([two, down, far, up]), z)
    passed = send(placed, shift(dc=1))
    both = jnp.where(core == 0, jnp.stack([placed, passed]), jnp.stack([passed, placed]))
    return both.transpose(2, 1, 0, 3, 4).reshape(8, rows, cols)


def reduce_all(grads):
    y, core, xl, z = (lax.axis_index(a) for a in ("y", "core", "xl", "z"))
    _, rows, cols = grads.shape
    half, part = rows // 2, rows // 8
    work = grads.reshape(2, 4, rows, cols)
    give = lax.dynamic_slice_in_dim(work, (1 - core) * half, half, 2).astype(BF)
    work = lax.dynamic_slice_in_dim(work, core * half, half, 2) + send(give, shift(dc=1)).astype(F32)

    def pick(array, index, dim, size=1):
        return lax.dynamic_slice_in_dim(array, index * size, size, dim)

    parts = [
        send(pick(work, (z + d) % 4, 1)[:, 0].astype(BF), shift(dz=d)) for d in (1, 3, 2)
    ]
    work = pick(work, z, 1)[:, 0] + sum(p.astype(F32) for p in parts)
    give = pick(work, 1 - xl, 0)[0].astype(BF)
    work = pick(work, xl, 0)[0] + send(give, shift(dxl=1)).astype(F32)
    parts = [
        send(pick(work, (y + d) % 4, 0, part).astype(BF), shift(dy=d)) for d in (1, 3, 2)
    ]
    work = pick(work, y, 0, part) + sum(p.astype(F32) for p in parts)
    own = work.astype(BF)
    total = (own.astype(F32) + send(own, shift(dxh=1)).astype(F32)).astype(BF)
    rest = [send(total, shift(dy=-d)) for d in (1, 2, 3)]
    placed = rotate(jnp.stack([total] + rest), y).reshape(half, cols)
    passed = send(placed, shift(dc=1))
    return jnp.where(
        core == 0, jnp.concatenate([placed, passed], 0), jnp.concatenate([passed, placed], 0)
    )


def attend_kernel(chips, rows, length_ref, core_ref, near_ref, far_ref, o_ref, e_ref, l_ref,
                  keys_ref, values_ref):
    step = pl.program_id(0)
    span = chips * rows
    aug = 2 * HEAD

    @pl.when(step == 0)
    def _():
        length = length_ref[0]
        core = core_ref[0]
        ones = jnp.ones((16, rows), F32)
        for side in range(2):
            source = near_ref if side == 0 else far_ref
            base = HEAD if side == 0 else 0
            owner = core if side == 0 else 1 - core
            for chip in range(chips):
                cols = slice(side * span + chip * rows, side * span + (chip + 1) * rows)
                key = source[chip, base:base + HEAD, :]
                keys_ref[0:HEAD, cols] = key
                keys_ref[HEAD:aug, cols] = key
                place = (chip * 2 + owner) * rows + lax.broadcasted_iota(jnp.int32, (16, rows), 1)
                row = lax.broadcasted_iota(jnp.int32, (16, rows), 0)
                bias = jnp.where((place < length) | (row > 0), 0.0, -1e30)
                keys_ref[aug:aug + 16, cols] = bias.astype(BF)
                value = source[chip, base + HEAD:base + 2 * HEAD, :].astype(F32)
                stacked = jnp.concatenate([value, ones, jnp.zeros((48, rows), F32)], 0)
                values_ref[cols, :] = stacked.T.astype(BF)

    query = near_ref[step, 0:HEAD, :].astype(F32) * (LOG2E * HEAD ** -0.5)
    high = query.astype(BF)
    low = (query - high.astype(F32)).astype(BF)
    query = jnp.concatenate([high, low, jnp.ones((16, rows), BF)], 0)
    scores = contract(query, keys_ref[...], 0, 0)
    top = jnp.max(scores, 1, keepdims=True)
    expo = jnp.exp2(scores - top).astype(BF)
    e_ref[...] = expo
    out = matmul(expo, values_ref[...]).T
    inverse = 1.0 / out[HEAD:HEAD + 8]
    o_ref[0] = (out[0:HEAD] * inverse[0:1]).astype(BF)
    l_ref[0] = inverse


def attend(near, far, length, core):
    chips, _, rows = near.shape
    tokens = 2 * chips * rows
    return pl.pallas_call(
        functools.partial(attend_kernel, chips, rows),
        grid=(chips,),
        in_specs=[
            pl.BlockSpec(memory_space=pltpu.SMEM),
            pl.BlockSpec(memory_space=pltpu.SMEM),
            pl.BlockSpec(near.shape, lambda i: (0, 0, 0)),
            pl.BlockSpec(far.shape, lambda i: (0, 0, 0)),
        ],
        out_specs=[
            pl.BlockSpec((1, HEAD, rows), lambda i: (i, 0, 0)),
            pl.BlockSpec((rows, tokens), lambda i: (i, 0)),
            pl.BlockSpec((1, 8, rows), lambda i: (i, 0, 0)),
        ],
        out_shape=[
            jax.ShapeDtypeStruct((chips, HEAD, rows), BF),
            jax.ShapeDtypeStruct((chips * rows, tokens), BF),
            jax.ShapeDtypeStruct((chips, 8, rows), F32),
        ],
        scratch_shapes=[
            pltpu.VMEM((2 * HEAD + 16, tokens), BF),
            pltpu.VMEM((tokens, 2 * HEAD), BF),
        ],
        compiler_params=pltpu.CompilerParams(vmem_limit_bytes=48 * 2**20),
        name="attend",
    )(length, core, near, far)


def attend_back_kernel(chips, rows, near_ref, far_ref, e_ref, o_ref, l_ref, do_ref,
                       dq_ref, dk_ref, dv_ref, keys_ref, values_ref, dk_acc, dv_acc):
    step = pl.program_id(0)
    span = chips * rows

    @pl.when(step == 0)
    def _():
        row = lax.broadcasted_iota(jnp.int32, (16, rows), 0)
        ones = jnp.where(row < 3, 1.0, 0.0).astype(BF)
        for side in range(2):
            source = near_ref if side == 0 else far_ref
            base = HEAD if side == 0 else 0
            for chip in range(chips):
                cols = slice(side * span + chip * rows, side * span + (chip + 1) * rows)
                key = source[chip, base:base + HEAD, :].astype(F32)
                stacked = jnp.concatenate([key, jnp.zeros((HEAD, rows), F32)], 0)
                keys_ref[cols, :] = stacked.T.astype(BF)
                values_ref[0:HEAD, cols] = source[chip, base + HEAD:base + 2 * HEAD, :]
                values_ref[HEAD:HEAD + 16, cols] = ones
        dk_acc[...] = jnp.zeros_like(dk_acc)
        dv_acc[...] = jnp.zeros_like(dv_acc)

    inverse = l_ref[0, 0:1, :]
    grad = do_ref[0].astype(F32) * inverse
    total = -jnp.sum(grad * o_ref[0].astype(F32), 0, keepdims=True)
    high = total.astype(BF).astype(F32)
    mid = (total - high).astype(BF).astype(F32)
    low = total - high - mid
    grad_low = grad.astype(BF)
    row = lax.broadcasted_iota(jnp.int32, (16, rows), 0)
    extra = jnp.where(row == 0, high, jnp.where(row == 1, mid, jnp.where(row == 2, low, 0.0)))
    grads = jnp.concatenate([grad_low, extra.astype(BF)], 0)
    query = near_ref[step, 0:HEAD, :]
    block = 1024
    dq = jnp.zeros((rows, 2 * HEAD), F32)
    for start in range(0, 2 * span, block):
        cols = slice(start, start + block)
        expo = e_ref[:, cols]
        d_probs = contract(grads, values_ref[:, cols], 0, 0)
        d_scores = (expo.astype(F32) * d_probs).astype(BF)
        dq = dq + matmul(d_scores, keys_ref[cols, :])
        dk_acc[:, cols] += matmul(query, d_scores)
        dv_acc[:, cols] += matmul(grad_low, expo)
    dq_ref[0] = (dq.T[0:HEAD] * HEAD ** -0.5).astype(BF)

    @pl.when(step == chips - 1)
    def _():
        for side in range(2):
            for chip in range(chips):
                cols = slice(side * span + chip * rows, side * span + (chip + 1) * rows)
                dk_ref[side, chip] = (dk_acc[:, cols] * HEAD ** -0.5).astype(BF)
                dv_ref[side, chip] = dv_acc[:, cols].astype(BF)


def attend_back(near, far, expo, out, inverse, d_out):
    chips, _, rows = near.shape
    tokens = 2 * chips * rows
    whole = lambda i: (0, 0, 0)
    one = lambda i: (i, 0, 0)
    return pl.pallas_call(
        functools.partial(attend_back_kernel, chips, rows),
        grid=(chips,),
        in_specs=[
            pl.BlockSpec(near.shape, whole),
            pl.BlockSpec(far.shape, whole),
            pl.BlockSpec((rows, tokens), lambda i: (i, 0)),
            pl.BlockSpec((1, HEAD, rows), one),
            pl.BlockSpec((1, 8, rows), one),
            pl.BlockSpec((1, HEAD, rows), one),
        ],
        out_specs=[
            pl.BlockSpec((1, HEAD, rows), one),
            pl.BlockSpec((2, chips, HEAD, rows), lambda i: (0, 0, 0, 0)),
            pl.BlockSpec((2, chips, HEAD, rows), lambda i: (0, 0, 0, 0)),
        ],
        out_shape=[
            jax.ShapeDtypeStruct((chips, HEAD, rows), BF),
            jax.ShapeDtypeStruct((2, chips, HEAD, rows), BF),
            jax.ShapeDtypeStruct((2, chips, HEAD, rows), BF),
        ],
        scratch_shapes=[
            pltpu.VMEM((tokens, 2 * HEAD), BF),
            pltpu.VMEM((HEAD + 16, tokens), BF),
            pltpu.VMEM((HEAD, tokens), F32),
            pltpu.VMEM((HEAD, tokens), F32),
        ],
        compiler_params=pltpu.CompilerParams(vmem_limit_bytes=48 * 2**20),
        name="attend_back",
    )(near, far, expo, out, inverse, d_out)


def shards(
    inputs, lengths, cotangent, glu_gain, glu_value, glu_gate, conv_gain, wide_weight,
    narrow_weight, mid_gain, depth_weight, point_weight, attn_gain, query_weight, key_weight,
    value_weight, output_weight, ffn_gain, ffn_in, ffn_out,
):
    rows, width = inputs.shape[1], inputs.shape[2]
    half = narrow_weight.shape[2]
    units = wide_weight.shape[1]
    core = lax.axis_index("core")
    first = (lax.axis_index("y") * 4 + lax.axis_index("xh") * 2 + core) * rows
    valid = (first + jnp.arange(rows, dtype=jnp.int32) < lengths[0]).astype(F32)[:, None]
    hidden = inputs[0].astype(F32)

    gains = jnp.concatenate([glu_gain, conv_gain, attn_gain, ffn_gain])[None]
    small = jnp.concatenate([gains, mid_gain[None], depth_weight], 0)
    small = jnp.pad(small, ((0, 32 - small.shape[0]), (0, 0)))
    pack1 = jnp.concatenate(
        [glu_value, glu_gate, jnp.concatenate([small[:16], small[16:]], 1)], 0
    )
    full1 = gather(pack1)
    w_val = full1[:, 0:64].reshape(width, width)
    w_gat = full1[:, 64:128].reshape(width, width)
    small = full1[:, 128:144, :256].astype(F32)
    g_glu, g_conv, g_att, g_ffn = (small[:, 0, 64 * i:64 * i + 64].reshape(-1) for i in range(4))
    g_mid = small[:, 1].reshape(-1)
    depth_float = small[:, 2:11].transpose(1, 0, 2).reshape(9, units)

    narrow_flat = narrow_weight.reshape(-1, half)
    cut = narrow_flat.shape[0] // 2
    pack2 = jnp.concatenate(
        [wide_weight[:, 512 * i:512 * i + 512] for i in range(4)]
        + [jnp.concatenate([narrow_flat[:cut], narrow_flat[cut:]], 1)]
        + [jnp.concatenate([point_weight[:128], point_weight[128:]], 1)]
        + [query_weight, key_weight, value_weight], 0,
    )
    full2 = gather(pack2)
    w_wid = full2[:, 0:256].reshape(8, 4, 64, 512).transpose(0, 2, 1, 3).reshape(width, units)
    nar = full2[:, 256:352]
    nar = jnp.concatenate([nar[:, :, :half], nar[:, :, half:]], 1).reshape(8, 3, 64, half)
    w_nar = nar.transpose(1, 0, 2, 3).reshape(3, width, half)
    pnt = full2[:, 352:480]
    w_pnt = jnp.concatenate([pnt[:, :, :half], pnt[:, :, half:]], 1).reshape(units, half)
    w_qry, w_key, w_vls = (
        full2[:, 480 + 64 * i:544 + 64 * i].reshape(width, width) for i in range(3)
    )

    pack3 = jnp.concatenate(
        [output_weight] + [ffn_in[:, 512 * i:512 * i + 512] for i in range(4)] + [ffn_out], 0
    )
    full3 = gather(pack3)
    w_outp = full3[:, 0:64].reshape(width, width)
    w_upper = full3[:, 64:320].reshape(8, 4, 64, 512).transpose(0, 2, 1, 3).reshape(width, units)
    w_lower = full3[:, 320:576].reshape(units, width)

    normed, glu_hat, glu_scale = layer_norm(hidden, g_glu)
    glu_in = normed.astype(BF)
    value_part = matmul(glu_in, w_val)
    sigma = jax.nn.sigmoid(matmul(glu_in, w_gat))
    after_glu = hidden + value_part * sigma

    normed, conv_hat, conv_scale = layer_norm(after_glu, g_conv)
    conv_in = (normed * valid).astype(BF)
    wide_pre = matmul(conv_in, w_wid)
    conv_rim = with_halo(conv_in, 1)
    stacked = jnp.concatenate(
        [conv_rim[0:rows], conv_rim[1:rows + 1], conv_rim[2:rows + 2]], axis=1
    )
    narrow_pre = matmul(stacked, w_nar.reshape(3 * width, half))
    mixed = smooth_unit(wide_pre) + jnp.pad(smooth_unit(narrow_pre), ((0, 0), (0, units - half)))
    normed, mid_hat, mid_scale = layer_norm(mixed, g_mid)
    mid_in = (normed * valid).astype(BF)
    mid_rim = with_halo(mid_in, 4)
    spread = sum((mid_rim[tap:tap + rows].astype(F32) * depth_float[tap] for tap in range(9)))
    spread_in = spread.astype(BF)
    separable = matmul(spread_in, w_pnt)
    after_conv = after_glu + jnp.pad(separable, ((0, 0), (0, width - half)))

    normed, attn_hat, attn_scale = layer_norm(after_conv, g_att)
    attn_in = normed.astype(BF)
    qkv = jnp.concatenate(
        [contract(w, attn_in, 0, 1).astype(BF).reshape(HEADS, HEAD, rows)
         for w in (w_qry, w_key, w_vls)], 1,
    )
    near = lax.all_to_all(qkv, CHIPS, 0, 0, tiled=True)
    far = send(near[:, HEAD:], shift(dc=1))
    head_out, expo, inverse = attend(near, far, lengths, core[None])
    heads_in = lax.all_to_all(head_out, CHIPS, 0, 0, tiled=True).reshape(width, rows)
    after_attn = after_conv + contract(heads_in, w_outp, 0, 0)

    normed, ffn_hat, ffn_scale = layer_norm(after_attn, g_ffn)
    ffn_input = normed.astype(BF)
    ffn_pre = matmul(ffn_input, w_upper)
    activated = smooth_unit(ffn_pre).astype(BF)
    result = (after_attn + matmul(activated, w_lower)) * valid
    grad = cotangent[0].astype(F32) * valid
    grad_low = grad.astype(BF)
    d_lower = inner_rows(activated, grad_low)
    d_pre = (outer_cols(grad_low, w_lower) * smooth_slope(ffn_pre)).astype(BF)
    d_upper = inner_rows(ffn_input, d_pre)
    back, d_gffn = norm_back(outer_cols(d_pre, w_upper), ffn_hat, ffn_scale, g_ffn)
    grad = grad + back
    grad_low = grad.astype(BF)
    d_outp = contract(heads_in, grad_low, 1, 0)
    d_heads = contract(w_outp, grad_low, 1, 1).astype(BF).reshape(HEADS, HEAD, rows)
    d_near = lax.all_to_all(d_heads, CHIPS, 0, 0, tiled=True)

    def by_shard(array, count=8):
        return array.reshape((count, array.shape[0] // count) + array.shape[1:])

    def columns(array):
        return by_shard(array).reshape(8, 64, 4, 512).transpose(0, 2, 1, 3).reshape(8, 256, 512)

    early = jnp.concatenate([by_shard(d_outp), columns(d_upper), by_shard(d_lower)], 1)
    early = reduce_all(early)

    dq, dk, dv = attend_back(near, far, expo, head_out, inverse, d_near)
    d_far = send(jnp.concatenate([dk[1], dv[1]], 1), shift(dc=1)).astype(F32)
    d_near = jnp.concatenate([dk[0], dv[0]], 1).astype(F32)
    d_qkv = jnp.concatenate([dq, (d_near + d_far).astype(BF)], 1)
    d_qkv = lax.all_to_all(d_qkv, CHIPS, 0, 0, tiled=True)
    dq_low, dk_low, dv_low = (
        d_qkv[:, HEAD * i:HEAD * i + HEAD].reshape(width, rows) for i in range(3)
    )
    d_qry = contract(attn_in, dq_low, 0, 1)
    d_key = contract(attn_in, dk_low, 0, 1)
    d_vls = contract(attn_in, dv_low, 0, 1)
    d_norm = (
        contract(dq_low, w_qry, 0, 1) + contract(dk_low, w_key, 0, 1)
        + contract(dv_low, w_vls, 0, 1)
    )
    back, d_gatt = norm_back(d_norm, attn_hat, attn_scale, g_att)
    grad = grad + back

    sep_grad = grad[:, :half].astype(BF)
    d_pnt = inner_rows(spread_in, sep_grad)
    d_spread = outer_cols(sep_grad, w_pnt).astype(BF)
    spread_float = d_spread.astype(F32)
    d_dep = jnp.stack(
        [jnp.sum(mid_rim[tap:tap + rows].astype(F32) * spread_float, 0) for tap in range(9)]
    )
    spread_rim = with_halo(d_spread, 4)
    d_mid = sum(
        (spread_rim[8 - tap:8 - tap + rows].astype(F32) * depth_float[tap] for tap in range(9))
    )
    back_mid, d_gmid = norm_back(d_mid * valid, mid_hat, mid_scale, g_mid)
    d_wide_pre = (back_mid * smooth_slope(wide_pre)).astype(BF)
    d_nar_pre = (back_mid[:, :half] * smooth_slope(narrow_pre)).astype(BF)
    d_wid = inner_rows(conv_in, d_wide_pre)
    d_nar = inner_rows(stacked, d_nar_pre).reshape(3, width, half)
    nar_rim = with_halo(d_nar_pre, 1)
    back_stack = jnp.concatenate(
        [nar_rim[2:rows + 2], nar_rim[1:rows + 1], nar_rim[0:rows]], axis=1
    )
    d_conv = outer_cols(d_wide_pre, w_wid) + outer_cols(
        back_stack, w_nar.transpose(1, 0, 2).reshape(width, 3 * half)
    )
    back, d_gconv = norm_back(d_conv * valid, conv_hat, conv_scale, g_conv)
    grad = grad + back

    d_value = (grad * sigma).astype(BF)
    d_gate = (grad * value_part * sigma * (1.0 - sigma)).astype(BF)
    d_wval = inner_rows(glu_in, d_value)
    d_wgat = inner_rows(glu_in, d_gate)
    d_norm = outer_cols(d_value, w_val) + outer_cols(d_gate, w_gat)
    back, d_gglu = norm_back(d_norm, glu_hat, glu_scale, g_glu)
    grad = grad + back

    gains = jnp.concatenate([by_shard(g) for g in (d_gglu, d_gconv, d_gatt, d_gffn)], 1)[:, None]
    small = jnp.concatenate(
        [gains, by_shard(d_gmid)[:, None], d_dep.reshape(9, 8, 256).transpose(1, 0, 2)], 1
    )
    small = jnp.pad(small, ((0, 0), (0, 64 - small.shape[1]), (0, 0)))
    nar = d_nar.reshape(3, 8, 64, half).transpose(1, 0, 2, 3).reshape(8, 192, half)
    pnt = by_shard(d_pnt)
    late = jnp.concatenate(
        [by_shard(d_wval), by_shard(d_wgat), columns(d_wid),
         jnp.concatenate([nar[:, :96], nar[:, 96:]], 2),
         jnp.concatenate([pnt[:, :128], pnt[:, 128:]], 2),
         by_shard(d_qry), by_shard(d_key), by_shard(d_vls),
         jnp.concatenate([small[:, :32], small[:, 32:]], 2)], 1,
    )
    late = reduce_all(late).astype(F32)
    early = early.astype(F32)

    def wide_of(array):
        return array.reshape(4, 64, 512).transpose(1, 0, 2).reshape(64, 2048)

    s_wval, s_wgat = late[0:64], late[64:128]
    s_wid = wide_of(late[128:384])
    nar = late[384:480]
    s_nar = jnp.concatenate([nar[:, :half], nar[:, half:]], 0).reshape(3, 64, half)
    pnt = late[480:608]
    s_pnt = jnp.concatenate([pnt[:, :half], pnt[:, half:]], 0)
    s_qry, s_key, s_vls = late[608:672], late[672:736], late[736:800]
    small = late[800:832, :256]
    s_gglu, s_gconv, s_gatt, s_gffn = (small[0, 64 * i:64 * i + 64] for i in range(4))
    s_outp, s_upper, s_lower = early[0:64], wide_of(early[64:320]), early[320:576]
    return (
        result.astype(BF)[None], grad[None], s_gglu, s_wval, s_wgat, s_gconv, s_wid, s_nar,
        small[1], small[2:11], s_pnt, s_gatt, s_qry, s_key, s_vls, s_outp, s_gffn, s_upper,
        s_lower,
    )


def solution(mesh):
    fine = Mesh(mesh.devices.reshape(SIZES), AXES)
    flat, row, mid = P(WT), P(WT, None), P(None, WT, None)
    col = P(None, WT)
    tokens = P(WT, CTX, None)
    weights = (
        flat, row, row, flat, row, mid, flat, col, row, flat, row, row, row, row, flat, row, row,
    )
    return jax.shard_map(
        shards, mesh=fine, in_specs=(tokens, flat, tokens) + weights,
        out_specs=(tokens, tokens) + weights, check_vma=False,
    )
```

```python
import functools

import jax
import jax.numpy as jnp
import numpy as np
from jax import lax
from jax.experimental import pallas as pl
from jax.experimental.pallas import tpu as pltpu
from jax.sharding import Mesh
from jax.sharding import PartitionSpec as P

HEADS = 8
HEAD = 64
EPSILON = 1e-06
AXES = ("y", "xh", "core", "xl", "z")
SIZES = (4, 2, 2, 2, 4)
CTX = ("y", "xh", "core")
CHIPS = ("y", "xh")
WT = ("xl", "z")
LOG2E = 1.4426950408889634
BF = jnp.bfloat16
F32 = jnp.float32


def moves(target):
    pairs = []
    for source in range(int(np.prod(SIZES))):
        place = [int(v) for v in np.unravel_index(source, SIZES)]
        goal = target(*place)
        if goal is not None:
            pairs.append((source, int(np.ravel_multi_index(tuple(goal), SIZES))))
    return pairs


def shift(dy=0, dxh=0, dc=0, dxl=0, dz=0):
    return moves(
        lambda y, xh, c, xl, z: (
            (y + dy) % 4, (xh + dxh) % 2, (c + dc) % 2, (xl + dxl) % 2, (z + dz) % 4,
        )
    )


def along(step):
    def target(y, xh, c, xl, z):
        place = y * 4 + xh * 2 + c + step
        if place < 0 or place > 15:
            return None
        return (place // 4, place // 2 % 2, place % 2, xl, z)
    return moves(target)


def send(value, pairs):
    return lax.ppermute(value, AXES, pairs)


def matmul(left, right):
    return jnp.dot(left, right, preferred_element_type=F32)


def contract(left, right, ldim, rdim):
    return lax.dot_general(
        left, right, (((ldim,), (rdim,)), ((), ())), preferred_element_type=F32
    )


def smooth_unit(value):
    return value * jax.nn.sigmoid(value)


def smooth_slope(value):
    sigma = jax.nn.sigmoid(value)
    return sigma * (1.0 + value * (1.0 - sigma))


def attend_kernel(chips, rows, length_ref, core_ref, near_ref, far_ref, o_ref, e_ref, l_ref,
                  keys_ref, values_ref):
    step = pl.program_id(0)
    span = chips * rows
    aug = 2 * HEAD

    @pl.when(step == 0)
    def _():
        length = length_ref[0]
        core = core_ref[0]
        ones = jnp.ones((16, rows), F32)
        for side in range(2):
            source = near_ref if side == 0 else far_ref
            base = HEAD if side == 0 else 0
            owner = core if side == 0 else 1 - core
            for chip in range(chips):
                cols = slice(side * span + chip * rows, side * span + (chip + 1) * rows)
                key = source[chip, base:base + HEAD, :]
                keys_ref[0:HEAD, cols] = key
                keys_ref[HEAD:aug, cols] = key
                place = (chip * 2 + owner) * rows + lax.broadcasted_iota(jnp.int32, (16, rows), 1)
                row = lax.broadcasted_iota(jnp.int32, (16, rows), 0)
                bias = jnp.where((place < length) | (row > 0), 0.0, -1e30)
                keys_ref[aug:aug + 16, cols] = bias.astype(BF)
                value = source[chip, base + HEAD:base + 2 * HEAD, :].astype(F32)
                stacked = jnp.concatenate([value, ones, jnp.zeros((48, rows), F32)], 0)
                values_ref[cols, :] = stacked.T.astype(BF)

    query = near_ref[step, 0:HEAD, :].astype(F32) * (LOG2E * HEAD ** -0.5)
    high = query.astype(BF)
    low = (query - high.astype(F32)).astype(BF)
    query = jnp.concatenate([high, low, jnp.ones((16, rows), BF)], 0)
    scores = contract(query, keys_ref[...], 0, 0)
    top = jnp.max(scores, 1, keepdims=True)
    expo = jnp.exp2(scores - top).astype(BF)
    e_ref[...] = expo
    out = matmul(expo, values_ref[...]).T
    inverse = 1.0 / out[HEAD:HEAD + 8]
    o_ref[0] = (out[0:HEAD] * inverse[0:1]).astype(BF)
    l_ref[0] = inverse


def attend(near, far, length, core):
    chips, _, rows = near.shape
    tokens = 2 * chips * rows
    return pl.pallas_call(
        functools.partial(attend_kernel, chips, rows),
        grid=(chips,),
        in_specs=[
            pl.BlockSpec(memory_space=pltpu.SMEM),
            pl.BlockSpec(memory_space=pltpu.SMEM),
            pl.BlockSpec(near.shape, lambda i: (0, 0, 0)),
            pl.BlockSpec(far.shape, lambda i: (0, 0, 0)),
        ],
        out_specs=[
            pl.BlockSpec((1, HEAD, rows), lambda i: (i, 0, 0)),
            pl.BlockSpec((rows, tokens), lambda i: (i, 0)),
            pl.BlockSpec((1, 8, rows), lambda i: (i, 0, 0)),
        ],
        out_shape=[
            jax.ShapeDtypeStruct((chips, HEAD, rows), BF),
            jax.ShapeDtypeStruct((chips * rows, tokens), BF),
            jax.ShapeDtypeStruct((chips, 8, rows), F32),
        ],
        scratch_shapes=[
            pltpu.VMEM((2 * HEAD + 16, tokens), BF),
            pltpu.VMEM((tokens, 2 * HEAD), BF),
        ],
        compiler_params=pltpu.CompilerParams(vmem_limit_bytes=48 * 2**20),
        cost_estimate=cost(14),
        name="attend",
    )(length, core, near, far)


def attend_back_kernel(chips, rows, near_ref, far_ref, e_ref, o_ref, l_ref, do_ref,
                       dq_ref, dk_ref, dv_ref, keys_ref, values_ref, dk_acc, dv_acc):
    step = pl.program_id(0)
    span = chips * rows

    @pl.when(step == 0)
    def _():
        row = lax.broadcasted_iota(jnp.int32, (16, rows), 0)
        ones = jnp.where(row < 3, 1.0, 0.0).astype(BF)
        for side in range(2):
            source = near_ref if side == 0 else far_ref
            base = HEAD if side == 0 else 0
            for chip in range(chips):
                cols = slice(side * span + chip * rows, side * span + (chip + 1) * rows)
                key = source[chip, base:base + HEAD, :].astype(F32)
                stacked = jnp.concatenate([key, jnp.zeros((HEAD, rows), F32)], 0)
                keys_ref[cols, :] = stacked.T.astype(BF)
                values_ref[0:HEAD, cols] = source[chip, base + HEAD:base + 2 * HEAD, :]
                values_ref[HEAD:HEAD + 16, cols] = ones
        dk_acc[...] = jnp.zeros_like(dk_acc)
        dv_acc[...] = jnp.zeros_like(dv_acc)

    inverse = l_ref[0, 0:1, :]
    grad = do_ref[0].astype(F32) * inverse
    total = -jnp.sum(grad * o_ref[0].astype(F32), 0, keepdims=True)
    high = total.astype(BF).astype(F32)
    mid = (total - high).astype(BF).astype(F32)
    low = total - high - mid
    grad_low = grad.astype(BF)
    row = lax.broadcasted_iota(jnp.int32, (16, rows), 0)
    extra = jnp.where(row == 0, high, jnp.where(row == 1, mid, jnp.where(row == 2, low, 0.0)))
    grads = jnp.concatenate([grad_low, extra.astype(BF)], 0)
    query = near_ref[step, 0:HEAD, :]
    block = 1024
    dq = jnp.zeros((rows, 2 * HEAD), F32)
    for start in range(0, 2 * span, block):
        cols = slice(start, start + block)
        expo = e_ref[:, cols]
        d_probs = contract(grads, values_ref[:, cols], 0, 0)
        d_scores = (expo.astype(F32) * d_probs).astype(BF)
        dq = dq + matmul(d_scores, keys_ref[cols, :])
        dk_acc[:, cols] += matmul(query, d_scores)
        dv_acc[:, cols] += matmul(grad_low, expo)
    dq_ref[0] = (dq.T[0:HEAD] * HEAD ** -0.5).astype(BF)

    @pl.when(step == chips - 1)
    def _():
        for side in range(2):
            for chip in range(chips):
                cols = slice(side * span + chip * rows, side * span + (chip + 1) * rows)
                dk_ref[side, chip] = (dk_acc[:, cols] * HEAD ** -0.5).astype(BF)
                dv_ref[side, chip] = dv_acc[:, cols].astype(BF)


def attend_back(near, far, expo, out, inverse, d_out):
    chips, _, rows = near.shape
    tokens = 2 * chips * rows
    whole = lambda i: (0, 0, 0)
    one = lambda i: (i, 0, 0)
    return pl.pallas_call(
        functools.partial(attend_back_kernel, chips, rows),
        grid=(chips,),
        in_specs=[
            pl.BlockSpec(near.shape, whole),
            pl.BlockSpec(far.shape, whole),
            pl.BlockSpec((rows, tokens), lambda i: (i, 0)),
            pl.BlockSpec((1, HEAD, rows), one),
            pl.BlockSpec((1, 8, rows), one),
            pl.BlockSpec((1, HEAD, rows), one),
        ],
        out_specs=[
            pl.BlockSpec((1, HEAD, rows), one),
            pl.BlockSpec((2, chips, HEAD, rows), lambda i: (0, 0, 0, 0)),
            pl.BlockSpec((2, chips, HEAD, rows), lambda i: (0, 0, 0, 0)),
        ],
        out_shape=[
            jax.ShapeDtypeStruct((chips, HEAD, rows), BF),
            jax.ShapeDtypeStruct((2, chips, HEAD, rows), BF),
            jax.ShapeDtypeStruct((2, chips, HEAD, rows), BF),
        ],
        scratch_shapes=[
            pltpu.VMEM((tokens, 2 * HEAD), BF),
            pltpu.VMEM((HEAD + 16, tokens), BF),
            pltpu.VMEM((HEAD, tokens), F32),
            pltpu.VMEM((HEAD, tokens), F32),
        ],
        compiler_params=pltpu.CompilerParams(vmem_limit_bytes=48 * 2**20),
        cost_estimate=cost(3),
        name="attend_back",
    )(near, far, expo, out, inverse, d_out)


VMEM = pl.BlockSpec(memory_space=pltpu.VMEM)
SMEM = pl.BlockSpec(memory_space=pltpu.SMEM)
ANY = pl.BlockSpec(memory_space=pl.ANY)
RIM = 8
EARLY = 144
SMALL = 320
LATE = 208


def call(kernel, outs, specs, scratch, name, micros, *args):
    return pl.pallas_call(
        kernel,
        in_specs=specs,
        out_specs=[VMEM] * len(outs),
        out_shape=[jax.ShapeDtypeStruct(shape, kind) for shape, kind in outs],
        scratch_shapes=scratch,
        compiler_params=pltpu.CompilerParams(vmem_limit_bytes=56 * 2**20),
        cost_estimate=cost(micros),
        name=name,
    )(*args)


def cost(micros):
    return pl.CostEstimate(
        flops=int(micros * 1.0e9), bytes_accessed=int(micros * 3.0e6), transcendentals=0
    )


def fetch(core, near_ref, far_ref, both_ref, sems):
    copies = [
        pltpu.make_async_copy(near_ref, both_ref.at[core], sems.at[0]),
        pltpu.make_async_copy(far_ref, both_ref.at[1 - core], sems.at[1]),
    ]
    for copy in copies:
        copy.start()
    return copies


def settle(copies):
    for copy in copies:
        copy.wait()


def gains_of(small_ref):
    total = small_ref[0, SMALL:SMALL + 16, :].astype(F32)
    for w in range(1, 8):
        total = total + small_ref[w, SMALL:SMALL + 16, :].astype(F32)
    return jnp.concatenate([total[0:8], total[8:16]], 1)


def taps_of(small_ref, index):
    small = small_ref[index, SMALL + 16:SMALL + 32, :].astype(F32)
    return small[0:9], small[9:10]


def normal_of(value):
    average = jnp.mean(value, -1, keepdims=True)
    centred = value - average
    scale = lax.rsqrt(jnp.mean(centred * centred, -1, keepdims=True) + EPSILON)
    return centred * scale, scale


def back_of(incoming, normal, scale, gain):
    scaled = incoming * gain
    return scale * (
        scaled
        - jnp.mean(scaled, -1, keepdims=True)
        - normal * jnp.mean(scaled * normal, -1, keepdims=True)
    )


def column_sum(value):
    return jnp.sum(value, 0, keepdims=True)


def mask_of(info_ref, count, before):
    place = info_ref[1] - before + lax.broadcasted_iota(jnp.int32, (count, 1), 0)
    return jnp.where((place >= 0) & (place < info_ref[2]), 1.0, 0.0)


def block_cols(index, size=256):
    return pl.ds(pl.multiple_of(index * size, size), size)


def upper_block(both_ref, index):
    rows = pl.ds(pl.multiple_of(lax.rem(index, 4) * 64, 64), 64)
    if len(both_ref.shape) == 5:
        return both_ref[lax.div(index, 4), :, :, rows, :].reshape(512, 256)
    return both_ref[lax.div(index, 4), :, rows, :].reshape(512, 256)


def narrow_block(both_ref, tap):
    return both_ref[0, :, :, 256 + 64 * tap:320 + 64 * tap, :].reshape(512, 256)


def point_block(both_ref, index):
    return both_ref[1, lax.div(index, 4), lax.rem(index, 4), 256:512, :]


def collect(info_ref, near_refs, far_refs, both_ref, sems):
    core, z = info_ref[0], info_ref[4]
    half = both_ref.shape[3] // 2
    copies = []
    for side, refs in ((core, near_refs), (1 - core, far_refs)):
        own, up, down, up2, down2 = refs
        for ref, step in ((own, 0), (up, 3), (down, 1)):
            copies.append((ref, both_ref.at[side, :, lax.rem(z + step, 4)]))
        opposite = lax.rem(z + 2, 4)
        copies.append((up2, both_ref.at[side, :, opposite, 0:half, :]))
        copies.append((down2, both_ref.at[side, :, opposite, half:2 * half, :]))
    copies = [
        pltpu.make_async_copy(source, target, sems.at[i]) for i, (source, target) in enumerate(copies)
    ]
    for copy in copies:
        copy.start()
    return copies


def glu_of(ref):
    return jnp.concatenate(
        [ref[:, 64 * i:64 * i + 64, :].reshape(512, 256) for i in range(2)], 1
    )


def queries_of(both_ref, side, part):
    return both_ref[side, :, 128 + 64 * part:192 + 64 * part, :].reshape(512, 256)


def glu_kernel(info_ref, low_ref, x_ref, high_ref, near_ref, far_ref, n1_ref, a_ref, sg_ref, h1_ref):
    rows = x_ref.shape[0]
    main = slice(RIM, RIM + rows)
    x = jnp.concatenate(
        [low_ref[...].astype(F32), x_ref[...].astype(F32), high_ref[...].astype(F32)], 0
    )
    normal, _ = normal_of(x)
    normed = normal * gains_of(near_ref)[0:1]
    n1 = normed.astype(BF)
    n1_ref[...] = normed[main].astype(BF)
    first = info_ref[0] == 0
    near = matmul(n1, glu_of(near_ref))
    far = matmul(n1, glu_of(far_ref))
    a = jnp.where(first, near, far)
    sg = jax.nn.sigmoid(jnp.where(first, far, near))
    a_ref[...] = a[main]
    sg_ref[...] = sg[main]
    h1_ref[...] = x + a * sg


def conv_kernel(info_ref, h1_ref, small_ref, *refs):
    near2, far2, rest = refs[0:5], refs[5:10], refs[10:]
    conv_body(info_ref, h1_ref, small_ref, near2, far2, *rest)


def conv_body(info_ref, h1_ref, small_ref, near2, far2, nearq_ref, farq_ref,
                n2_ref, wp_ref, np_ref, nm_ref, mean_ref, scale_ref, sp_ref, h2_ref, n3_ref,
                qkv_ref, w2_ref, wq_ref, mix_ref, sem2, semq):
    core = info_ref[0]
    rim_rows = h1_ref.shape[0]
    rows = rim_rows - 2 * RIM
    copies2 = collect(info_ref, near2, far2, w2_ref, sem2)
    copiesq = fetch(core, nearq_ref, farq_ref, wq_ref, semq)
    gains = gains_of(small_ref)
    valid = mask_of(info_ref, rim_rows, RIM)
    normal, _ = normal_of(h1_ref[...])
    n2f = normal * gains[1:2] * valid
    n2 = n2f.astype(BF)
    n2_ref[...] = n2
    n2f = n2.astype(F32)
    settle(copies2)
    narrow = jnp.zeros((rim_rows, 256), F32)
    for tap in range(3):
        if tap == 1:
            moved = n2
        else:
            moved = pltpu.roll(n2f, 1 if tap == 0 else rim_rows - 1, 0).astype(BF)
        narrow = narrow + matmul(moved, narrow_block(w2_ref, tap))
    np_ref[...] = narrow
    narrow = smooth_unit(narrow)

    def first_pass(index, total):
        cols = block_cols(index)
        wide = matmul(n2_ref[...], upper_block(w2_ref, index))
        wp_ref[:, cols] = wide
        mixed = smooth_unit(wide) + narrow * jnp.where(index == 0, 1.0, 0.0)
        mix_ref[:, cols] = mixed
        return total + jnp.sum(mixed, -1, keepdims=True)

    total = lax.fori_loop(0, 8, first_pass, jnp.zeros((rim_rows, 1), F32))
    mean = total * (1.0 / 2048)

    def second_pass(index, total):
        centred = mix_ref[:, block_cols(index)] - mean
        return total + jnp.sum(centred * centred, -1, keepdims=True)

    total = lax.fori_loop(0, 8, second_pass, jnp.zeros((rim_rows, 1), F32))
    scale = lax.rsqrt(total * (1.0 / 2048) + EPSILON)
    mean_ref[...] = jnp.broadcast_to(mean, mean_ref.shape)
    scale_ref[...] = jnp.broadcast_to(scale, scale_ref.shape)
    h2_ref[...] = h1_ref[RIM:RIM + rows, :]

    def third_pass(index, carry):
        cols = block_cols(index)
        taps, gain = taps_of(small_ref, index)
        nm = ((mix_ref[:, cols] - mean) * scale * gain * valid).astype(BF)
        nm_ref[:, cols] = nm
        mix_ref[:, cols] = nm.astype(F32)
        spread = jnp.zeros((rows, 256), F32)
        for tap in range(9):
            spread = spread + mix_ref[4 + tap:4 + tap + rows, cols] * taps[tap:tap + 1]
        spread = spread.astype(BF)
        sp_ref[:, cols] = spread
        h2_ref[:, 0:256] += matmul(spread, point_block(w2_ref, index))
        return carry

    lax.fori_loop(0, 8, third_pass, 0)
    normal, _ = normal_of(h2_ref[...])
    n3 = (normal * gains[2:3]).astype(BF)
    n3_ref[...] = n3
    settle(copiesq)
    for part in range(3):
        for side in range(2):
            block = matmul(n3, queries_of(wq_ref, side, part))
            qkv_ref[4 * side:4 * side + 4, 64 * part:64 * part + 64, :] = (
                block.T.astype(BF).reshape(4, 64, rows)
            )


def ffn_kernel(info_ref, h2_ref, o_ref, small_ref, cot_ref, near_ref, far_ref,
               out_ref, r_ref, du_ref, n4_ref, gy_ref, ga_ref, g3_ref, dob_ref, gain_ref,
               w_ref, y_ref, dn_ref, sem):
    rows = h2_ref.shape[0]
    copies = fetch(info_ref[0], near_ref, far_ref, w_ref, sem)
    gains = gains_of(small_ref)
    valid = mask_of(info_ref, rows, 0)
    heads = o_ref[...].reshape(512, rows)
    gy = (cot_ref[...].astype(F32) * valid).astype(BF)
    gy_ref[...] = gy
    settle(copies)
    outs = [w_ref[side, :, 512:576, :].reshape(512, 256) for side in range(2)]
    h3 = h2_ref[...] + jnp.concatenate([contract(heads, outs[side], 0, 0) for side in range(2)], 1)
    normal, scale = normal_of(h3)
    n4_ref[...] = (normal * gains[3:4]).astype(BF)
    y_ref[...] = h3
    dn_ref[...] = jnp.zeros_like(dn_ref)

    def step(index, carry):
        cols = block_cols(index)
        upper = upper_block(w_ref, index)
        lower = [w_ref[side, index, 256:512, :] for side in range(2)]
        u = matmul(n4_ref[...], upper)
        sigma = jax.nn.sigmoid(u)
        r = (u * sigma).astype(BF)
        r_ref[:, cols] = r
        y_ref[:, 0:256] += matmul(r, lower[0])
        y_ref[:, 256:512] += matmul(r, lower[1])
        dr = contract(gy_ref[:, 0:256], lower[0], 1, 1) + contract(gy_ref[:, 256:512], lower[1], 1, 1)
        du = (dr * (sigma * (1.0 + u * (1.0 - sigma)))).astype(BF)
        du_ref[:, cols] = du
        dn_ref[...] += contract(du, upper, 1, 1)
        return carry

    lax.fori_loop(0, 8, step, 0)
    out_ref[...] = (y_ref[...] * valid).astype(BF)
    dn = dn_ref[...]
    gain_ref[...] = column_sum(dn * normal)
    g3 = gy.astype(F32) + back_of(dn, normal, scale, gains[3:4])
    g3_ref[...] = g3
    ga = g3.astype(BF)
    ga_ref[...] = ga
    dob = contract(outs[0], ga[:, 0:256], 1, 1) + contract(outs[1], ga[:, 256:512], 1, 1)
    dob_ref[...] = dob.astype(BF).reshape(HEADS, HEAD, rows)


def pair_rows(value):
    split = value.reshape(8, 8, 8, 256)
    return jnp.concatenate([split[..., 0:128], split[..., 128:256]], 2)


def writer(out_ref, add_ref):
    def write(value, *where):
        if add_ref is not None:
            value = value + add_ref[where].astype(F32)
        out_ref[where] = value.astype(BF)
    return write


def early_kernel(keeps, info_ref, r_ref, du_ref, n4_ref, gy_ref, ga_ref, o_ref, *refs):
    rows = r_ref.shape[0]
    side = info_ref[0] if keeps else 1 - info_ref[0]
    write = writer(refs[-1], refs[0] if keeps else None)
    full = slice(None)
    for j in range(4):
        res = contract(n4_ref[...], du_ref[:, block_cols(side * 4 + j)], 0, 0)
        for i in range(2):
            write(res[:, 128 * i:128 * i + 128].reshape(8, 64, 128), full, 2 * j + i, slice(0, 64))
    gy = gy_ref[:, block_cols(side)]
    for w in range(8):
        res = contract(gy, r_ref[:, 256 * w:256 * w + 256], 0, 0).reshape(8, 32, 256)
        for i in range(2):
            write(res[:, :, 128 * i:128 * i + 128], w, full, slice(64 + 32 * i, 96 + 32 * i))
    res = matmul(o_ref[...].reshape(512, rows), ga_ref[:, block_cols(side)])
    write(pair_rows(res), full, full, slice(128, 144))


def attn_in_kernel(info_ref, d_ref, h2_ref, g3_ref, small_ref, near_ref, far_ref,
                   g2_ref, gs_ref, lo_ref, hi_ref, gain_ref, w_ref, sem):
    rows = h2_ref.shape[0]
    copies = fetch(info_ref[0], near_ref, far_ref, w_ref, sem)
    gains = gains_of(small_ref)
    normal, scale = normal_of(h2_ref[...])
    settle(copies)
    dn = jnp.zeros((rows, 512), F32)
    for part in range(3):
        for side in range(2):
            block = d_ref[4 * side:4 * side + 4, 64 * part:64 * part + 64, :].reshape(256, rows)
            dn = dn + contract(block, queries_of(w_ref, side, part), 0, 1)
    gain_ref[...] = column_sum(dn * normal)
    g2 = g3_ref[...] + back_of(dn, normal, scale, gains[2:3])
    g2_ref[...] = g2
    gs = g2[:, 0:256]
    gs_ref[...] = gs.astype(BF)
    lo_ref[...] = gs[0:RIM].astype(BF)
    hi_ref[...] = gs[rows - RIM:rows].astype(BF)


def conv_back_kernel(info_ref, lo_ref, gs_ref, hi_ref, nm_ref, wp_ref, np_ref, mean_ref,
                     scale_ref, small_ref, *refs):
    near2, far2, rest = refs[0:5], refs[5:10], refs[10:]
    conv_back_body(info_ref, lo_ref, gs_ref, hi_ref, nm_ref, wp_ref, np_ref, mean_ref,
                   scale_ref, small_ref, near2, far2, *rest)


def conv_back_body(info_ref, lo_ref, gs_ref, hi_ref, nm_ref, wp_ref, np_ref, mean_ref,
                   scale_ref, small_ref, near2, far2, dw_ref, dnar_ref, table_ref,
                   w2_ref, nmf_ref, dsp_ref, sc_ref, hat_ref, sem2):
    rim_rows = wp_ref.shape[0]
    rows = rim_rows - 2 * RIM
    main = slice(RIM, RIM + rows)
    copies = collect(info_ref, near2, far2, w2_ref, sem2)
    valid = mask_of(info_ref, rim_rows, RIM)
    gs = jnp.concatenate(
        [lo_ref[...].astype(F32), gs_ref[...].astype(F32), hi_ref[...].astype(F32)], 0
    ).astype(BF)
    mean = mean_ref[:, 0:1]
    scale = scale_ref[:, 0:1]
    table_ref[...] = jnp.zeros_like(table_ref)
    dsp_ref[0:RIM, :] = jnp.zeros((RIM, 256), F32)
    dsp_ref[RIM + rim_rows:, :] = jnp.zeros((RIM, 256), F32)
    settle(copies)

    def first_pass(index, carry):
        one, two = carry
        cols = block_cols(index)
        taps, gain = taps_of(small_ref, index)
        dsp = contract(gs, point_block(w2_ref, index), 1, 1).astype(BF).astype(F32)
        dsp_ref[RIM:RIM + rim_rows, :] = dsp
        nmf_ref[...] = nm_ref[:, cols].astype(F32)
        inner = dsp[main]
        dn = jnp.zeros((rim_rows, 256), F32)
        for tap in range(9):
            dn = dn + dsp_ref[12 - tap:12 - tap + rim_rows, :] * taps[tap:tap + 1]
            table_ref[tap:tap + 1, cols] = column_sum(nmf_ref[4 + tap:4 + tap + rows, :] * inner)
        dn = dn * valid
        mixed = smooth_unit(wp_ref[:, cols]) + smooth_unit(np_ref[...]) * jnp.where(index == 0, 1.0, 0.0)
        hat = (mixed - mean) * scale
        hat_ref[:, cols] = hat
        table_ref[9:10, cols] = column_sum((dn * hat)[main])
        scaled = dn * gain
        sc_ref[:, cols] = scaled
        return (one + jnp.sum(scaled, -1, keepdims=True),
                two + jnp.sum(scaled * hat, -1, keepdims=True))

    zero = jnp.zeros((rim_rows, 1), F32)
    one, two = lax.fori_loop(0, 8, first_pass, (zero, zero))
    one = one * (1.0 / 2048)
    two = two * (1.0 / 2048)
    back = scale * (sc_ref[:, 0:256] - one - hat_ref[:, 0:256] * two)
    dnar_ref[...] = (back * smooth_slope(np_ref[...])).astype(BF)

    def second_pass(index, carry):
        cols = block_cols(index)
        back = scale[main] * (
            sc_ref[main, cols] - one[main] - hat_ref[main, cols] * two[main]
        )
        dw_ref[:, cols] = (back * smooth_slope(wp_ref[main, cols])).astype(BF)
        return carry

    lax.fori_loop(0, 8, second_pass, 0)


def glu_back_kernel(info_ref, dw_ref, dnar_ref, h1_ref, small_ref, *refs):
    near2, far2, rest = refs[0:5], refs[5:10], refs[10:]
    glu_back_body(info_ref, dw_ref, dnar_ref, h1_ref, small_ref, near2, far2, *rest)


def glu_back_body(info_ref, dw_ref, dnar_ref, h1_ref, small_ref, near2, far2, far1_ref, g2_ref,
                  a_ref, sg_ref, x_ref, dx_ref, da_ref, db_ref, gconv_ref, gglu_ref,
                  w2_ref, dn_ref, nar_ref, sem2):
    rows = g2_ref.shape[0]
    main = slice(RIM, RIM + rows)
    copies = collect(info_ref, near2, far2, w2_ref, sem2)
    gains = gains_of(small_ref)
    valid = mask_of(info_ref, rows, 0)
    nar_ref[...] = dnar_ref[...].astype(F32)
    dn_ref[...] = jnp.zeros_like(dn_ref)
    normal, scale1 = normal_of(h1_ref[main, :])
    settle(copies)
    for tap in range(3):
        moved = nar_ref[9 - tap:9 - tap + rows, :].astype(BF)
        dn_ref[...] += contract(moved, narrow_block(w2_ref, tap), 1, 1)

    def step(index, carry):
        dn_ref[...] += contract(dw_ref[:, block_cols(index)], upper_block(w2_ref, index), 1, 1)
        return carry

    lax.fori_loop(0, 8, step, 0)
    dn = dn_ref[...] * valid
    gconv_ref[...] = column_sum(dn * normal)
    g1 = g2_ref[...] + back_of(dn, normal, scale1, gains[1:2])
    sg = sg_ref[...]
    da = g1 * sg
    db = g1 * a_ref[...] * sg * (1.0 - sg)
    da_ref[...] = da.astype(BF)
    db_ref[...] = db.astype(BF)
    first = info_ref[0] == 0
    dn = contract(jnp.where(first, da, db).astype(BF), glu_of(small_ref), 1, 1)
    dn = dn + contract(jnp.where(first, db, da).astype(BF), glu_of(far1_ref), 1, 1)
    normal, scale0 = normal_of(x_ref[...].astype(F32))
    gglu_ref[...] = column_sum(dn * normal)
    dx_ref[...] = g1 + back_of(dn, normal, scale0, gains[0:1])


FULL = slice(None)


def conv_grads(side, write, n2_ref, dw_ref, dnar_ref, sp_ref, gs_ref, n3_ref, d_ref, n2f_ref):
    rows = dw_ref.shape[0]
    n2f_ref[...] = n2_ref[...].astype(F32)
    shifted = [n2f_ref[7 + tap:7 + tap + rows, :].astype(BF) for tap in range(3)]
    for j in range(4):
        res = contract(shifted[1], dw_ref[:, block_cols(side * 4 + j)], 0, 0)
        for i in range(2):
            write(res[:, 128 * i:128 * i + 128].reshape(8, 64, 128), 2 * j + i, FULL, slice(0, 64))
    gs = gs_ref[:, block_cols(side, 128)]
    for w in range(8):
        res = contract(gs, sp_ref[:, 256 * w:256 * w + 256], 0, 0).reshape(8, 16, 256)
        for i in range(2):
            write(res[:, :, 128 * i:128 * i + 128], FULL, w, slice(64 + 16 * i, 80 + 16 * i))
    for part in range(3):
        d = d_ref[pl.ds(side * 4, 4), 64 * part:64 * part + 64, :].reshape(256, rows)
        packed = pair_rows(contract(n3_ref[...], d, 0, 1))
        for w in range(8):
            write(packed[w], FULL, w, slice(96 + 16 * part, 112 + 16 * part))
    return shifted


def main_rows(rows):
    return slice(RIM, RIM + rows)


def narrow_grads(side, shifted, dnar_ref, narf_ref):
    rows = shifted[0].shape[0]
    narf_ref[...] = dnar_ref[...].astype(F32)
    dnar = narf_ref[main_rows(rows), block_cols(side, 128)].astype(BF)
    return [contract(piece, dnar, 0, 0) for piece in shifted]


def narrow_rows(narrow, c, w):
    return [n[64 * w + 8 * c:64 * w + 8 * c + 8] for n in narrow]


def glu_grads(side, write, base, n1_ref, da_ref, db_ref):
    for place, d_ref in enumerate((da_ref, db_ref)):
        packed = pair_rows(contract(n1_ref[...], d_ref[:, block_cols(side)], 0, 0))
        for w in range(8):
            write(packed[w], FULL, w, slice(base + 16 * place, base + 16 * place + 16))


def small_rows(side, table_ref, gain_refs, w):
    lanes = pl.ds(pl.multiple_of(w * 256 + side * 128, 128), 128)
    pair = slice(128 * (w // 2), 128 * (w // 2) + 128)
    return jnp.concatenate(
        [table_ref[0:10, lanes]] + [ref[:, pair] for ref in gain_refs] + [table_ref[14:16, lanes]], 0
    )


def conv_give_kernel(info_ref, n2_ref, dw_ref, dnar_ref, sp_ref, gs_ref, n3_ref, d_ref, out_ref,
                     n2f_ref, narf_ref):
    side = 1 - info_ref[0]
    shifted = conv_grads(side, writer(out_ref, None), n2_ref, dw_ref, dnar_ref, sp_ref, gs_ref,
                         n3_ref, d_ref, n2f_ref)
    narrow = narrow_grads(side, shifted, dnar_ref, narf_ref)
    for w in range(8):
        for c in range(8):
            rows = jnp.concatenate(narrow_rows(narrow, c, w) + [jnp.zeros((8, 128), F32)], 0)
            out_ref[c, w, 144:176, :] = rows.astype(BF)


def glu_give_kernel(info_ref, n1_ref, da_ref, db_ref, table_ref, gglu_ref, gconv_ref, gattn_ref,
                    gffn_ref, out_ref):
    side = 1 - info_ref[0]
    glu_grads(side, writer(out_ref, None), 0, n1_ref, da_ref, db_ref)
    for w in range(8):
        table = small_rows(side, table_ref, (gglu_ref, gconv_ref, gattn_ref, gffn_ref), w)
        for c in range(8):
            rows = jnp.concatenate([table[2 * c:2 * c + 2], jnp.zeros((14, 128), F32)], 0)
            out_ref[c, w, 32:48, :] = rows.astype(BF)


def late_keep_kernel(info_ref, n2_ref, dw_ref, dnar_ref, sp_ref, gs_ref, n3_ref, d_ref, n1_ref,
                     da_ref, db_ref, table_ref, gglu_ref, gconv_ref, gattn_ref, gffn_ref,
                     conv_ref, glu_ref, out_ref, n2f_ref, narf_ref):
    side = info_ref[0]

    def write(value, *where):
        out_ref[where] = (value + conv_ref[where].astype(F32)).astype(BF)

    shifted = conv_grads(side, write, n2_ref, dw_ref, dnar_ref, sp_ref, gs_ref, n3_ref, d_ref, n2f_ref)
    narrow = narrow_grads(side, shifted, dnar_ref, narf_ref)

    def write_glu(value, *where):
        start = where[2].start
        added = value + glu_ref[where[0], where[1], start - 176:start - 160, :].astype(F32)
        out_ref[where] = added.astype(BF)

    glu_grads(side, write_glu, 176, n1_ref, da_ref, db_ref)
    for w in range(8):
        table = small_rows(side, table_ref, (gglu_ref, gconv_ref, gattn_ref, gffn_ref), w)
        for c in range(8):
            other = glu_ref[c, w, 32:48, :].astype(F32)
            small = jnp.concatenate([table[2 * c:2 * c + 2], jnp.zeros((6, 128), F32)], 0) + other[0:8]
            rows = jnp.concatenate(narrow_rows(narrow, c, w) + [jnp.zeros((8, 128), F32)], 0)
            rows = rows + conv_ref[c, w, 144:176, :].astype(F32)
            out_ref[c, w, 144:176, :] = jnp.concatenate([rows[0:24], small], 0).astype(BF)


def unpack_kernel(info_ref, near_ref, far_ref, gglu_ref, val_ref, gat_ref, gconv_ref, wid_ref, nar_ref,
                  gmid_ref, dep_ref, pnt_ref, gatt_ref, qry_ref, key_ref, vls_ref, outp_ref,
                  gffn_ref, upper_ref, lower_ref, fin_ref, low_ref, pt_ref, table_ref, sem):
    settle(fetch(info_ref[0], near_ref, far_ref, fin_ref, sem))
    for c in range(8):
        for k in range(2):
            fin = fin_ref[k, c].astype(F32)
            lanes = slice(k * 1024 + c * 128, k * 1024 + c * 128 + 128)
            upper_ref[:, lanes] = fin[0:64]
            wid_ref[:, lanes] = fin[EARLY:EARLY + 64]
            late = EARLY
            for i in range(2):
                low_ref[k * 256 + c * 32:k * 256 + c * 32 + 32, 128 * i:128 * i + 128] = (
                    fin[64 + 32 * i:96 + 32 * i]
                )
                pt_ref[k * 128 + c * 16:k * 128 + c * 16 + 16, 128 * i:128 * i + 128] = (
                    fin[late + 64 + 16 * i:late + 80 + 16 * i]
                )
            for tap in range(3):
                nar_ref[tap, 8 * c:8 * c + 8, 128 * k:128 * k + 128] = (
                    fin[late + 144 + 8 * tap:late + 152 + 8 * tap]
                )
            table_ref[2 * c:2 * c + 2, 128 * k:128 * k + 128] = fin[late + 168:late + 170]
            bases = [128] + [late + 96 + 16 * i for i in range(3)] + [late + 176, late + 192]
            targets = [outp_ref, qry_ref, key_ref, vls_ref, val_ref, gat_ref]
            for base, target in zip(bases, targets):
                for i in range(2):
                    target[8 * c:8 * c + 8, k * 256 + 128 * i:k * 256 + 128 * i + 128] = (
                        fin[base + 8 * i:base + 8 * i + 8]
                    )
    lower_ref[...] = low_ref[...].T
    pnt_ref[...] = pt_ref[...].T
    dep_ref[...] = table_ref[0:9, :]
    gmid_ref[...] = table_ref[9:10, :]
    even = info_ref[3] == 0
    gains = jnp.where(even, table_ref[10:14, 0:64], table_ref[10:14, 64:128])
    gglu_ref[...] = gains[0:1]
    gconv_ref[...] = gains[1:2]
    gatt_ref[...] = gains[2:3]
    gffn_ref[...] = gains[3:4]


def spread_out(own, axes, count):
    copies = jnp.broadcast_to(own[None], (count,) + own.shape)
    return lax.all_to_all(copies, axes, 0, 0, tiled=True)


def shards(
    inputs, lengths, cotangent, glu_gain, glu_value, glu_gate, conv_gain, wide_weight,
    narrow_weight, mid_gain, depth_weight, point_weight, attn_gain, query_weight, key_weight,
    value_weight, output_weight, ffn_gain, ffn_in, ffn_out,
):
    rows, width = inputs.shape[1], inputs.shape[2]
    units = wide_weight.shape[1]
    rim_rows = rows + 2 * RIM
    core = lax.axis_index("core")
    shard = lax.axis_index("xl") * 4 + lax.axis_index("z")
    first = (lax.axis_index("y") * 4 + lax.axis_index("xh") * 2 + core) * rows
    z = lax.axis_index("z")
    info = jnp.stack([core, first, lengths[0], shard % 2, z]).astype(jnp.int32)
    flip = shift(dc=1)

    def own_half(weight):
        cols = weight.shape[-1] // 2
        return lax.dynamic_slice_in_dim(weight, core * cols, cols, weight.ndim - 1)

    def blocks(weight):
        return [weight[:, 256 * i:256 * i + 256] for i in range(weight.shape[1] // 256)]

    narrow_rows = jnp.pad(narrow_weight.reshape(192, 256), ((0, 64), (0, 0)))
    pack2 = jnp.concatenate(
        blocks(own_half(wide_weight)) + [jnp.where(core == 0, narrow_rows, point_weight)], 0
    )
    half = pack2.shape[0] // 2
    other = send(pack2, shift(dxl=1))
    pair = jnp.where(shard < 4, jnp.stack([pack2, other]), jnp.stack([other, pack2]))
    up, down = send(pair, shift(dz=1)), send(pair, shift(dz=-1))
    up2, down2 = send(up[:, :half], shift(dz=1)), send(down[:, half:], shift(dz=-1))
    near2 = [pair, up, down, up2, down2]
    far2 = [send(piece, flip) for piece in near2]

    place = lax.broadcasted_iota(jnp.int32, (1, width), 1) // 64 == shard
    gains = jnp.stack([glu_gain, conv_gain, attn_gain, ffn_gain])
    gains = jnp.where(place, jnp.tile(gains, (1, 8)), jnp.zeros((), BF))
    gains = jnp.pad(gains, ((0, 4), (0, 0)))
    taps = jnp.pad(jnp.concatenate([depth_weight, mid_gain[None]], 0), ((0, 6), (0, 0)))
    pack1 = jnp.concatenate(
        blocks(jnp.where(core == 0, glu_value, glu_gate))
        + [own_half(w) for w in (query_weight, key_weight, value_weight)]
        + blocks(gains) + [taps], 0,
    )
    near1 = spread_out(pack1, WT, 8)
    near1, up, down = lax.optimization_barrier((near1, near2[1], near2[2]))
    far1 = send(near1[:, :SMALL], flip)
    x = inputs[0]
    low_x = send(x[rows - RIM:], along(1))
    high_x = send(x[:RIM], along(-1))
    pack3 = jnp.concatenate(
        blocks(own_half(ffn_in)) + [own_half(ffn_out), own_half(output_weight)], 0
    )
    pack3, _, _ = lax.optimization_barrier((pack3, near2[3], near2[4]))
    near3 = lax.all_gather(pack3, WT, axis=0)
    far3 = send(near3, flip)

    tall, wide, narrow = (rows, width), (rows, units), (rows, 256)
    dma = pltpu.SemaphoreType.DMA
    ring = pltpu.VMEM((2, 2, 4) + pack2.shape, BF)
    n1, a, sg, h1 = call(
        glu_kernel, [(tall, BF), (tall, F32), (tall, F32), ((rim_rows, width), F32)],
        [SMEM] + [VMEM] * 5, [], "glu", 3, info, low_x, x, high_x, near1, far1,
    )
    n2, wp, np_, nm, mean, scale, sp, h2, n3, qkv = call(
        conv_kernel,
        [((rim_rows, width), BF), ((rim_rows, units), F32), ((rim_rows, 256), F32),
         ((rim_rows, units), BF), ((rim_rows, 128), F32), ((rim_rows, 128), F32),
         (wide, BF), (tall, F32), (tall, BF), ((HEADS, 3 * HEAD, rows), BF)],
        [SMEM, VMEM, VMEM] + [ANY] * 12,
        [ring, pltpu.VMEM((2, 8, SMALL, 256), BF), pltpu.VMEM((rim_rows, units), F32),
         dma((10,)), dma((2,))],
        "conv", 15, info, h1, near1, *near2, *far2, near1[:, :SMALL], far1,
    )
    near = lax.all_to_all(qkv, CHIPS, 0, 0, tiled=True)
    far = send(near[:, HEAD:], flip)
    head_out, expo, inverse = attend(near, far, lengths, info[:1])
    heads_in = lax.all_to_all(head_out, CHIPS, 0, 0, tiled=True)
    output, r, du, n4, gy, ga, g3, dob, d_gffn = call(
        ffn_kernel,
        [(tall, BF), (wide, BF), (wide, BF), (tall, BF), (tall, BF), (tall, BF), (tall, F32),
         ((HEADS, HEAD, rows), BF), ((1, width), F32)],
        [SMEM, VMEM, VMEM, VMEM, VMEM, ANY, ANY],
        [pltpu.VMEM((2,) + near3.shape, BF), pltpu.VMEM(tall, F32), pltpu.VMEM(tall, F32), dma((2,))],
        "ffn", 11, info, h2, heads_in, near1, cotangent[0], near3, far3,
    )

    d_near = lax.all_to_all(dob, CHIPS, 0, 0, tiled=True)
    early = [((8, 8, EARLY, 128), BF)]
    given = (info, r, du, n4, gy, ga, heads_in)
    give = call(
        functools.partial(early_kernel, False), early, [SMEM] + [VMEM] * 6, [], "early_give", 0.3,
        *given,
    )[0]
    early = call(
        functools.partial(early_kernel, True), early, [SMEM] + [VMEM] * 7, [], "early_keep", 0.3,
        *given, send(give, flip),
    )[0]
    d_near, early = lax.optimization_barrier((d_near, early))
    early = lax.psum_scatter(early, WT, scatter_dimension=0, tiled=True)
    early = early[0]
    dq, dk, dv = attend_back(near, far, expo, head_out, inverse, d_near)
    d_far = send(jnp.concatenate([dk[1], dv[1]], 1), flip).astype(F32)
    d_own = jnp.concatenate([dk[0], dv[0]], 1).astype(F32)
    d_qkv = jnp.concatenate([dq, (d_own + d_far).astype(BF)], 1)
    d_qkv = lax.all_to_all(d_qkv, CHIPS, 0, 0, tiled=True)
    g2, gs, lo, hi, d_gatt = call(
        attn_in_kernel,
        [(tall, F32), (narrow, BF), ((RIM, 256), BF), ((RIM, 256), BF), ((1, width), F32)],
        [SMEM] + [VMEM] * 4 + [ANY] * 2,
        [pltpu.VMEM((2, 8, SMALL, 256), BF), dma((2,))],
        "attn_in", 0.5, info, d_qkv, h2, g3, near1, near1[:, :SMALL], far1,
    )
    low_gs = send(hi, along(1))
    high_gs = send(lo, along(-1))
    rim_narrow = ((rim_rows, 256), BF)
    dw, dnar, table = call(
        conv_back_kernel, [(wide, BF), rim_narrow, ((16, units), F32)],
        [SMEM] + [VMEM] * 9 + [ANY] * 10,
        [ring, pltpu.VMEM((rim_rows, 256), F32), pltpu.VMEM((rim_rows + 2 * RIM, 256), F32),
         pltpu.VMEM((rim_rows, units), F32), pltpu.VMEM((rim_rows, units), F32), dma((10,))],
        "conv_back", 2, info, low_gs, gs, high_gs, nm, wp, np_, mean, scale, near1, *near2, *far2,
    )
    shapes = [pltpu.VMEM((rim_rows, width), F32), pltpu.VMEM((rim_rows, 256), F32)]
    conv_given = (n2, dw, dnar, sp, gs, n3, d_qkv)
    give1 = call(
        conv_give_kernel, [((8, 8, 176, 128), BF)], [SMEM] + [VMEM] * 7, shapes, "conv_give", 0.5,
        info, *conv_given,
    )[0]
    take1 = send(give1, flip)
    g2, _, early = lax.optimization_barrier((g2, give1, early))
    early = lax.all_to_all(early, CHIPS, 0, 0, tiled=True)
    dx, da, db, d_gconv, d_gglu = call(
        glu_back_kernel,
        [(tall, F32), (tall, BF), (tall, BF), ((1, width), F32), ((1, width), F32)],
        [SMEM] + [VMEM] * 4 + [ANY] * 10 + [VMEM] * 5,
        [ring, pltpu.VMEM(tall, F32), pltpu.VMEM((rim_rows, 256), F32), dma((10,))],
        "glu_back", 1, info, dw, dnar, h1, near1, *near2, *far2, far1, g2, a, sg, x,
    )
    glu_given = (n1, da, db, table, d_gglu, d_gconv, d_gatt, d_gffn)
    give2 = call(
        glu_give_kernel, [((8, 8, 48, 128), BF)], [SMEM] + [VMEM] * 8, [], "glu_give", 0.3,
        info, *glu_given,
    )[0]
    late = call(
        late_keep_kernel, [((8, 8, LATE, 128), BF)], [SMEM] + [VMEM] * 17, shapes, "late_keep", 0.5,
        info, *conv_given, *glu_given, take1, send(give2, flip),
    )[0]
    late, early = lax.optimization_barrier((late, early))
    early = jnp.sum(early.astype(F32), 0).astype(BF)
    late = lax.all_to_all(late.reshape(64, LATE, 128), CHIPS + WT, 0, 0, tiled=True)
    late = jnp.sum(late.astype(F32), 0).astype(BF)
    final = spread_out(jnp.concatenate([early, late], 0), CHIPS, 8)
    square, broad = ((64, 512), F32), ((64, 2048), F32)
    line = ((1, 64), F32)
    grads = call(
        unpack_kernel,
        [line, square, square, line, broad, ((3, 64, 256), F32), ((1, 256), F32),
         ((9, 256), F32), ((256, 256), F32), line, square, square, square, square, line, broad,
         ((256, 512), F32)],
        [SMEM, ANY, ANY],
        [pltpu.VMEM((2, 8, EARLY + LATE, 128), BF), pltpu.VMEM((512, 256), F32),
         pltpu.VMEM((256, 256), F32), pltpu.VMEM((16, 256), F32), dma((2,))],
        "unpack", 3, info, final, send(final, flip),
    )
    grads = [g[0] if g.shape[0] == 1 else g for g in grads]
    return (output[None], dx[None]) + tuple(grads)


def solution(mesh):
    fine = Mesh(mesh.devices.reshape(SIZES), AXES)
    flat, row, mid = P(WT), P(WT, None), P(None, WT, None)
    col = P(None, WT)
    tokens = P(WT, CTX, None)
    weights = (
        flat, row, row, flat, row, mid, flat, col, row, flat, row, row, row, row, flat, row, row,
    )
    return jax.shard_map(
        shards, mesh=fine, in_specs=(tokens, flat, tokens) + weights,
        out_specs=(tokens, tokens) + weights, check_vma=False,
    )
```

```python
import functools

import jax
import jax.numpy as jnp
import numpy as np
from jax import lax
from jax.experimental import pallas as pl
from jax.experimental.pallas import tpu as pltpu
from jax.sharding import Mesh
from jax.sharding import PartitionSpec as P

HEADS = 8
HEAD = 64
EPSILON = 1e-06
AXES = ("y", "xh", "core", "xl", "z")
SIZES = (4, 2, 2, 2, 4)
CTX = ("y", "xh", "core")
CHIPS = ("y", "xh")
WT = ("xl", "z")
LOG2E = 1.4426950408889634
BF = jnp.bfloat16
F32 = jnp.float32


def moves(target):
    pairs = []
    for source in range(int(np.prod(SIZES))):
        place = [int(v) for v in np.unravel_index(source, SIZES)]
        goal = target(*place)
        if goal is not None:
            pairs.append((source, int(np.ravel_multi_index(tuple(goal), SIZES))))
    return pairs


def shift(dy=0, dxh=0, dc=0, dxl=0, dz=0):
    return moves(
        lambda y, xh, c, xl, z: (
            (y + dy) % 4, (xh + dxh) % 2, (c + dc) % 2, (xl + dxl) % 2, (z + dz) % 4,
        )
    )


def along(step):
    def target(y, xh, c, xl, z):
        place = y * 4 + xh * 2 + c + step
        if place < 0 or place > 15:
            return None
        return (place // 4, place // 2 % 2, place % 2, xl, z)
    return moves(target)


def send(value, pairs):
    return lax.ppermute(value, AXES, pairs)


def matmul(left, right):
    return jnp.dot(left, right, preferred_element_type=F32)


def contract(left, right, ldim, rdim):
    return lax.dot_general(
        left, right, (((ldim,), (rdim,)), ((), ())), preferred_element_type=F32
    )


def smooth_unit(value):
    return value * jax.nn.sigmoid(value)


def smooth_slope(value):
    sigma = jax.nn.sigmoid(value)
    return sigma * (1.0 + value * (1.0 - sigma))


VMEM = pl.BlockSpec(memory_space=pltpu.VMEM)
SMEM = pl.BlockSpec(memory_space=pltpu.SMEM)
HBM = pl.BlockSpec(memory_space=pltpu.HBM)
ANY = pl.BlockSpec(memory_space=pl.ANY)
FREE = "free"


def attend_kernel(chips, rows, length_ref, core_ref, near_ref, far_ref, o_ref, e_ref, l_ref,
                  near_out, far_out, keys_ref, values_ref, sem):
    step = pl.program_id(0)
    span = chips * rows
    aug = 2 * HEAD
    pairs = [(near_ref, near_out), (far_ref, far_out)]

    @pl.when(step == chips - 1)
    def _():
        for i, (source, target) in enumerate(pairs):
            pltpu.make_async_copy(source, target, sem.at[i]).wait()

    @pl.when(step == 0)
    def _():
        launch(pairs, sem)
        length = length_ref[0]
        core = core_ref[0]
        ones = jnp.ones((16, rows), F32)
        for side in range(2):
            source = near_ref if side == 0 else far_ref
            base = HEAD if side == 0 else 0
            owner = core if side == 0 else 1 - core
            for chip in range(chips):
                cols = slice(side * span + chip * rows, side * span + (chip + 1) * rows)
                key = source[chip, base:base + HEAD, :]
                keys_ref[0:HEAD, cols] = key
                keys_ref[HEAD:aug, cols] = key
                place = (chip * 2 + owner) * rows + lax.broadcasted_iota(jnp.int32, (16, rows), 1)
                row = lax.broadcasted_iota(jnp.int32, (16, rows), 0)
                bias = jnp.where((place < length) | (row > 0), 0.0, -1e30)
                keys_ref[aug:aug + 16, cols] = bias.astype(BF)
                value = source[chip, base + HEAD:base + 2 * HEAD, :].astype(F32)
                stacked = jnp.concatenate([value, ones, jnp.zeros((48, rows), F32)], 0)
                values_ref[cols, :] = stacked.T.astype(BF)

    query = near_ref[step, 0:HEAD, :].astype(F32) * (LOG2E * HEAD ** -0.5)
    high = query.astype(BF)
    low = (query - high.astype(F32)).astype(BF)
    query = jnp.concatenate([high, low, jnp.ones((16, rows), BF)], 0)
    scores = contract(query, keys_ref[...], 0, 0)
    top = jnp.max(scores, 1, keepdims=True)
    expo = jnp.exp2(scores - top).astype(BF)
    e_ref[...] = expo
    out = matmul(expo, values_ref[...]).T
    inverse = 1.0 / out[HEAD:HEAD + 8]
    o_ref[0] = (out[0:HEAD] * inverse[0:1]).astype(BF)
    l_ref[0] = inverse


def attend(near, far, length, core):
    chips, _, rows = near.shape
    tokens = 2 * chips * rows
    return pl.pallas_call(
        functools.partial(attend_kernel, chips, rows),
        grid=(chips,),
        in_specs=[
            pl.BlockSpec(memory_space=pltpu.SMEM),
            pl.BlockSpec(memory_space=pltpu.SMEM),
            pl.BlockSpec(near.shape, lambda i: (0, 0, 0)),
            pl.BlockSpec(far.shape, lambda i: (0, 0, 0)),
        ],
        out_specs=[
            pl.BlockSpec((1, HEAD, rows), lambda i: (i, 0, 0)),
            pl.BlockSpec((rows, tokens), lambda i: (i, 0)),
            pl.BlockSpec((1, 8, rows), lambda i: (i, 0, 0)),
            HBM,
            HBM,
        ],
        out_shape=[
            pltpu.HBM((chips, HEAD, rows), BF),
            pltpu.HBM((chips * rows, tokens), BF),
            pltpu.HBM((chips, 8, rows), F32),
            pltpu.HBM(near.shape, BF),
            pltpu.HBM(far.shape, BF),
        ],
        scratch_shapes=[
            pltpu.VMEM((2 * HEAD + 16, tokens), BF),
            pltpu.VMEM((tokens, 2 * HEAD), BF),
            pltpu.SemaphoreType.DMA((2,)),
        ],
        compiler_params=pltpu.CompilerParams(vmem_limit_bytes=32 * 2**20),
        cost_estimate=cost(14),
        name="attend",
    )(length, core, near, far)


def attend_back_kernel(chips, rows, near_ref, far_ref, e_ref, o_ref, l_ref, do_ref,
                       dq_ref, dk_ref, dv_ref, keys_ref, values_ref, dk_acc, dv_acc):
    step = pl.program_id(0)
    span = chips * rows

    @pl.when(step == 0)
    def _():
        row = lax.broadcasted_iota(jnp.int32, (16, rows), 0)
        ones = jnp.where(row < 3, 1.0, 0.0).astype(BF)
        for side in range(2):
            source = near_ref if side == 0 else far_ref
            base = HEAD if side == 0 else 0
            for chip in range(chips):
                cols = slice(side * span + chip * rows, side * span + (chip + 1) * rows)
                key = source[chip, base:base + HEAD, :].astype(F32)
                stacked = jnp.concatenate([key, jnp.zeros((HEAD, rows), F32)], 0)
                keys_ref[cols, :] = stacked.T.astype(BF)
                values_ref[0:HEAD, cols] = source[chip, base + HEAD:base + 2 * HEAD, :]
                values_ref[HEAD:HEAD + 16, cols] = ones
        dk_acc[...] = jnp.zeros_like(dk_acc)
        dv_acc[...] = jnp.zeros_like(dv_acc)

    inverse = l_ref[0, 0:1, :]
    grad = do_ref[0].astype(F32) * inverse
    total = -jnp.sum(grad * o_ref[0].astype(F32), 0, keepdims=True)
    high = total.astype(BF).astype(F32)
    mid = (total - high).astype(BF).astype(F32)
    low = total - high - mid
    grad_low = grad.astype(BF)
    row = lax.broadcasted_iota(jnp.int32, (16, rows), 0)
    extra = jnp.where(row == 0, high, jnp.where(row == 1, mid, jnp.where(row == 2, low, 0.0)))
    grads = jnp.concatenate([grad_low, extra.astype(BF)], 0)
    query = near_ref[step, 0:HEAD, :]
    block = 1024
    dq = jnp.zeros((rows, 2 * HEAD), F32)
    for start in range(0, 2 * span, block):
        cols = slice(start, start + block)
        expo = e_ref[:, cols]
        d_probs = contract(grads, values_ref[:, cols], 0, 0)
        d_scores = (expo.astype(F32) * d_probs).astype(BF)
        dq = dq + matmul(d_scores, keys_ref[cols, :])
        dk_acc[:, cols] += matmul(query, d_scores)
        dv_acc[:, cols] += matmul(grad_low, expo)
    dq_ref[0] = (dq.T[0:HEAD] * HEAD ** -0.5).astype(BF)

    @pl.when(step == chips - 1)
    def _():
        for side in range(2):
            for chip in range(chips):
                cols = slice(side * span + chip * rows, side * span + (chip + 1) * rows)
                dk_ref[side, chip] = (dk_acc[:, cols] * HEAD ** -0.5).astype(BF)
                dv_ref[side, chip] = dv_acc[:, cols].astype(BF)


def attend_back(near, far, expo, out, inverse, d_out):
    chips, _, rows = near.shape
    tokens = 2 * chips * rows
    whole = lambda i: (0, 0, 0)
    one = lambda i: (i, 0, 0)
    return pl.pallas_call(
        functools.partial(attend_back_kernel, chips, rows),
        grid=(chips,),
        in_specs=[
            pl.BlockSpec(near.shape, whole),
            pl.BlockSpec(far.shape, whole),
            pl.BlockSpec((rows, tokens), lambda i: (i, 0)),
            pl.BlockSpec((1, HEAD, rows), one),
            pl.BlockSpec((1, 8, rows), one),
            pl.BlockSpec((1, HEAD, rows), one),
        ],
        out_specs=[
            pl.BlockSpec((1, HEAD, rows), one),
            pl.BlockSpec((2, chips, HEAD, rows), lambda i: (0, 0, 0, 0)),
            pl.BlockSpec((2, chips, HEAD, rows), lambda i: (0, 0, 0, 0)),
        ],
        out_shape=[
            pltpu.HBM((chips, HEAD, rows), BF),
            jax.ShapeDtypeStruct((2, chips, HEAD, rows), BF),
            jax.ShapeDtypeStruct((2, chips, HEAD, rows), BF),
        ],
        scratch_shapes=[
            pltpu.VMEM((tokens, 2 * HEAD), BF),
            pltpu.VMEM((HEAD + 16, tokens), BF),
            pltpu.VMEM((HEAD, tokens), F32),
            pltpu.VMEM((HEAD, tokens), F32),
        ],
        compiler_params=pltpu.CompilerParams(vmem_limit_bytes=32 * 2**20),
        cost_estimate=cost(3),
        name="attend_back",
    )(in_hbm(near), in_hbm(far), in_hbm(expo), in_hbm(out), in_hbm(inverse), d_out)


RIM = 8
ACT_N4 = slice(4096, 4608)
ACT_GY = slice(4608, 5120)
ACT_GA = slice(5120, 5632)
EARLY = 144
SMALL = 320
MIDDLE = 80
LATE = 128


def call(kernel, outs, specs, scratch, name, micros, *args):
    args = [arg if spec in (SMEM, FREE, ANY) else in_hbm(arg) for arg, spec in zip(args, specs)]
    kinds = [out[2] if len(out) > 2 else VMEM for out in outs]
    return pl.pallas_call(
        kernel,
        in_specs=[VMEM if spec is FREE else spec for spec in specs],
        out_specs=[VMEM if kind is FREE else kind for kind in kinds],
        out_shape=[
            (jax.ShapeDtypeStruct if kind is FREE else pltpu.HBM)(out[0], out[1])
            for kind, out in zip(kinds, outs)
        ],
        scratch_shapes=scratch,
        compiler_params=pltpu.CompilerParams(vmem_limit_bytes=32 * 2**20),
        cost_estimate=cost(micros),
        name=name,
    )(*args)


def in_hbm(value):
    return pltpu.with_memory_space_constraint(value, pltpu.HBM)


def cost(micros):
    return pl.CostEstimate(
        flops=int(micros * 1.0e9), bytes_accessed=int(micros * 3.0e6), transcendentals=0
    )


def launch(pairs, sems):
    copies = [
        pltpu.make_async_copy(source, target, sems.at[i]) for i, (source, target) in enumerate(pairs)
    ]
    for copy in copies:
        copy.start()
    return copies


def fetch(core, near_ref, far_ref, both_ref, sems):
    return launch([(near_ref, both_ref.at[core]), (far_ref, both_ref.at[1 - core])], sems)


def settle(copies):
    for copy in copies:
        copy.wait()


def gains_of(small_ref):
    total = small_ref[0, 0:16, :].astype(F32)
    for w in range(1, 8):
        total = total + small_ref[w, 0:16, :].astype(F32)
    return jnp.concatenate([total[0:8], total[8:16]], 1)


def taps_of(small_ref, index):
    small = small_ref[index, 16:32, :].astype(F32)
    return small[0:9], small[9:10]


def normal_of(value):
    average = jnp.mean(value, -1, keepdims=True)
    centred = value - average
    scale = lax.rsqrt(jnp.mean(centred * centred, -1, keepdims=True) + EPSILON)
    return centred * scale, scale


def back_of(incoming, normal, scale, gain):
    scaled = incoming * gain
    return scale * (
        scaled
        - jnp.mean(scaled, -1, keepdims=True)
        - normal * jnp.mean(scaled * normal, -1, keepdims=True)
    )


def column_sum(value):
    return jnp.sum(value, 0, keepdims=True)


def mask_of(info_ref, count, before):
    place = info_ref[1] - before + lax.broadcasted_iota(jnp.int32, (count, 1), 0)
    return jnp.where((place >= 0) & (place < info_ref[2]), 1.0, 0.0)


def block_cols(index, size=256):
    return pl.ds(pl.multiple_of(index * size, size), size)


def upper_block(both_ref, index):
    rows = pl.ds(pl.multiple_of(lax.rem(index, 4) * 64, 64), 64)
    if len(both_ref.shape) == 5:
        return both_ref[lax.div(index, 4), :, :, rows, :].reshape(512, 256)
    return both_ref[lax.div(index, 4), :, rows, :].reshape(512, 256)


def narrow_block(both_ref, tap):
    return both_ref[0, :, :, 256 + 64 * tap:320 + 64 * tap, :].reshape(512, 256)


def point_block(both_ref, index):
    return both_ref[1, lax.div(index, 4), lax.rem(index, 4), 256:512, :]


def collect(info_ref, near_refs, far_refs, both_ref, sems, rows=slice(0, 512)):
    core, x, z = info_ref[0], info_ref[5], info_ref[4]
    copies = []
    for side, refs in ((core, near_refs), (1 - core, far_refs)):
        for i, ref in enumerate(refs):
            place = x if i < 4 else 1 - x
            target = both_ref.at[side, place, lax.rem(z + i % 4, 4), rows]
            copies.append((ref.at[rows], target))
    return launch(copies, sems)


def glu_of(both_ref, side):
    return jnp.concatenate(
        [both_ref[side, :, 64 * i:64 * i + 64, :].reshape(512, 256) for i in range(2)], 1
    )


def queries_of(both_ref, side, part):
    return both_ref[side, :, 64 * part:64 * part + 64, :].reshape(512, 256)


def small_pair(one_ref, small_ref):
    return (one_ref.at[0, :, SMALL:SMALL + 32, :], small_ref)


def glu_kernel(info_ref, low_ref, x_ref, high_ref, near_ref, far_ref, n1_ref, a_ref, sg_ref, h1_ref,
               main_ref, one_ref, w_ref, sem):
    rows = x_ref.shape[0]
    main = slice(RIM, RIM + rows)
    copies = fetch(info_ref[0], near_ref, far_ref, w_ref, sem)
    x = jnp.concatenate(
        [low_ref[...].astype(F32), x_ref[...].astype(F32), high_ref[...].astype(F32)], 0
    )
    normal, _ = normal_of(x)
    settle(copies)
    copies = launch([(w_ref, one_ref)], sem)
    normed = normal * gains_of(w_ref.at[0, :, SMALL:SMALL + 32, :])[0:1]
    n1 = normed.astype(BF)
    n1_ref[...] = normed[main].astype(BF)
    a = matmul(n1, glu_of(w_ref, 0))
    sg = jax.nn.sigmoid(matmul(n1, glu_of(w_ref, 1)))
    a_ref[...] = a[main]
    sg_ref[...] = sg[main]
    h1 = x + a * sg
    h1_ref[...] = h1
    main_ref[...] = h1[main]
    settle(copies)


def conv_kernel(info_ref, h1_ref, *refs):
    near2, far2, rest = refs[0:8], refs[8:16], refs[16:]
    conv_body(info_ref, h1_ref, near2, far2, *rest)


def conv_body(info_ref, h1_ref, near2, far2, one_ref,
              n2_ref, wp_out, np_ref, nm_out, mean_ref, scale_ref, sp_out, h2_ref, n3_ref,
              qkv_ref, two_ref, w2_ref, wq_ref, small_ref, mix_ref, wp_ref, nm_ref, sp_ref,
              sem2, semq, sems):
    core = info_ref[0]
    rim_rows = h1_ref.shape[0]
    rows = rim_rows - 2 * RIM
    copiesq = launch(
        [small_pair(one_ref, small_ref), (one_ref.at[:, :, 128:SMALL, :], wq_ref)], semq
    )
    copies2 = collect(info_ref, near2, far2, w2_ref, sem2)
    settle(copiesq[:1])

    def leaving(which, index):
        source, target = ((wp_ref, wp_out), (nm_ref, nm_out), (sp_ref, sp_out))[which]
        cols = block_cols(index)
        return pltpu.make_async_copy(source.at[:, cols], target.at[:, cols], sems.at[which, index])

    gains = gains_of(small_ref)
    valid = mask_of(info_ref, rim_rows, RIM)
    normal, _ = normal_of(h1_ref[...])
    n2f = normal * gains[1:2] * valid
    n2 = n2f.astype(BF)
    n2_ref[...] = n2
    n2f = n2.astype(F32)
    settle(copies2)
    copies2 = launch([(w2_ref, two_ref)], sem2)
    narrow = jnp.zeros((rim_rows, 256), F32)
    for tap in range(3):
        if tap == 1:
            moved = n2
        else:
            moved = pltpu.roll(n2f, 1 if tap == 0 else rim_rows - 1, 0).astype(BF)
        narrow = narrow + matmul(moved, narrow_block(w2_ref, tap))
    np_ref[...] = narrow
    narrow = smooth_unit(narrow)

    def first_pass(index, total):
        cols = block_cols(index)
        wide = matmul(n2_ref[...], upper_block(w2_ref, index))
        wp_ref[:, cols] = wide
        leaving(0, index).start()
        mixed = smooth_unit(wide) + narrow * jnp.where(index == 0, 1.0, 0.0)
        mix_ref[:, cols] = mixed
        return total + jnp.sum(mixed, -1, keepdims=True)

    total = lax.fori_loop(0, 8, first_pass, jnp.zeros((rim_rows, 1), F32))
    mean = total * (1.0 / 2048)

    def second_pass(index, total):
        centred = mix_ref[:, block_cols(index)] - mean
        return total + jnp.sum(centred * centred, -1, keepdims=True)

    total = lax.fori_loop(0, 8, second_pass, jnp.zeros((rim_rows, 1), F32))
    scale = lax.rsqrt(total * (1.0 / 2048) + EPSILON)
    mean_ref[...] = jnp.broadcast_to(mean, mean_ref.shape)
    scale_ref[...] = jnp.broadcast_to(scale, scale_ref.shape)
    h2_ref[...] = h1_ref[RIM:RIM + rows, :]

    def third_pass(index, carry):
        cols = block_cols(index)
        taps, gain = taps_of(small_ref, index)
        nm = ((mix_ref[:, cols] - mean) * scale * gain * valid).astype(BF)
        nm_ref[:, cols] = nm
        leaving(1, index).start()
        mix_ref[:, cols] = nm.astype(F32)
        spread = jnp.zeros((rows, 256), F32)
        for tap in range(9):
            spread = spread + mix_ref[4 + tap:4 + tap + rows, cols] * taps[tap:tap + 1]
        spread = spread.astype(BF)
        sp_ref[:, cols] = spread
        leaving(2, index).start()
        h2_ref[:, 0:256] += matmul(spread, point_block(w2_ref, index))
        return carry

    lax.fori_loop(0, 8, third_pass, 0)
    normal, _ = normal_of(h2_ref[...])
    n3 = (normal * gains[2:3]).astype(BF)
    n3_ref[...] = n3
    settle(copiesq[1:])
    for part in range(3):
        for side in range(2):
            block = matmul(n3, queries_of(wq_ref, side, part))
            qkv_ref[4 * side:4 * side + 4, 64 * part:64 * part + 64, :] = (
                block.T.astype(BF).reshape(4, 64, rows)
            )
    settle(copies2)
    for which in range(3):
        for index in range(8):
            leaving(which, index).wait()


def ffn_kernel(info_ref, h2_ref, o_ref, cot_ref, one_ref, near_ref, far_ref,
               out_ref, acts_ref, g3_ref, dob_ref, gain_ref, heads_ref,
               w_ref, small_ref, y_ref, dn_ref, sem):
    rows = h2_ref.shape[0]
    core = info_ref[0]
    x = info_ref[5]
    pairs = [small_pair(one_ref, small_ref)]
    for side, ref in ((core, near_ref), (1 - core, far_ref)):
        pairs += [(ref.at[:, 0], w_ref.at[side, x]), (ref.at[:, 1], w_ref.at[side, 1 - x])]
    copies = launch(pairs, sem)
    valid = mask_of(info_ref, rows, 0)
    heads_ref[...] = o_ref[...]
    heads = o_ref[...].reshape(512, rows)
    gy = (cot_ref[...].astype(F32) * valid).astype(BF)
    acts_ref[:, ACT_GY] = gy
    settle(copies)
    gains = gains_of(small_ref)
    outs = [w_ref[side, :, :, 512:576, :].reshape(512, 256) for side in range(2)]
    h3 = h2_ref[...] + jnp.concatenate([contract(heads, outs[side], 0, 0) for side in range(2)], 1)
    normal, scale = normal_of(h3)
    acts_ref[:, ACT_N4] = (normal * gains[3:4]).astype(BF)
    y_ref[...] = h3
    dn_ref[...] = jnp.zeros_like(dn_ref)

    def step(index, carry):
        cols = block_cols(index)
        upper = upper_block(w_ref, index)
        lower = [w_ref[side, lax.div(index, 4), lax.rem(index, 4), 256:512, :] for side in range(2)]
        u = matmul(acts_ref[:, ACT_N4], upper)
        sigma = jax.nn.sigmoid(u)
        r = (u * sigma).astype(BF)
        acts_ref[:, cols] = r
        y_ref[:, 0:256] += matmul(r, lower[0])
        y_ref[:, 256:512] += matmul(r, lower[1])
        dr = contract(acts_ref[:, 4608:4864], lower[0], 1, 1) + contract(acts_ref[:, 4864:5120], lower[1], 1, 1)
        du = (dr * (sigma * (1.0 + u * (1.0 - sigma)))).astype(BF)
        acts_ref[:, block_cols(index + 8)] = du
        dn_ref[...] += contract(du, upper, 1, 1)
        return carry

    lax.fori_loop(0, 8, step, 0)
    out_ref[...] = (y_ref[...] * valid).astype(BF)
    dn = dn_ref[...]
    gain_ref[...] = column_sum(dn * normal)
    g3 = gy.astype(F32) + back_of(dn, normal, scale, gains[3:4])
    g3_ref[...] = g3
    ga = g3.astype(BF)
    acts_ref[:, ACT_GA] = ga
    dob = contract(outs[0], ga[:, 0:256], 1, 1) + contract(outs[1], ga[:, 256:512], 1, 1)
    dob_ref[...] = dob.astype(BF).reshape(HEADS, HEAD, rows)


def pair_rows(value):
    split = value.reshape(8, 8, 8, 256)
    return jnp.concatenate([split[..., 0:128], split[..., 128:256]], 2)


FULL = slice(None)


def by_chip(out_ref, c, rows, value):
    out_ref[c % 2, :, :, c // 2, rows, :] = value.astype(BF).reshape((2, 4) + value.shape[1:])


def by_shard(out_ref, w, rows, value):
    value = value.astype(BF).reshape((4, 2) + value.shape[1:])
    for xh in range(2):
        out_ref[xh, w // 4, w % 4, :, rows, :] = value[:, xh]


def both(product, pairs):
    return sum((product(*pair) for pair in pairs[1:]), product(*pairs[0]))


def early_kernel(info_ref, acts_ref, heads_ref, acts2_ref, heads2_ref, out_ref):
    rows = acts_ref.shape[0]
    side = info_ref[0]
    refs = (acts_ref, acts2_ref)
    for j in range(4):
        cols = block_cols(side * 4 + j + 8)
        res = both(lambda n, d: contract(n, d, 0, 0), [(ref[:, ACT_N4], ref[:, cols]) for ref in refs])
        for i in range(2):
            by_chip(out_ref, 2 * j + i, slice(0, 64), res[:, 128 * i:128 * i + 128].reshape(8, 64, 128))
    gy = [ref[:, block_cols(side + 18)] for ref in refs]
    for w in range(8):
        cols = slice(256 * w, 256 * w + 256)
        res = both(lambda g, r: contract(g, r, 0, 0), [(g, ref[:, cols]) for g, ref in zip(gy, refs)])
        res = res.reshape(8, 32, 256)
        for i in range(2):
            by_shard(out_ref, w, slice(64 + 32 * i, 96 + 32 * i), res[:, :, 128 * i:128 * i + 128])
    ga = block_cols(side + 20)
    res = both(matmul, [(h[...].reshape(512, rows), ref[:, ga])
                        for h, ref in zip((heads_ref, heads2_ref), refs)])
    packed = pair_rows(res)
    for c in range(8):
        by_chip(out_ref, c, slice(128, 144), packed[:, c])


def attn_in_kernel(info_ref, d_ref, h2_ref, g3_ref, one_ref,
                   g2_ref, gs_ref, lo_ref, hi_ref, gain_ref, w_ref, small_ref, sem):
    rows = h2_ref.shape[0]
    copies = launch(
        [small_pair(one_ref, small_ref), (one_ref.at[:, :, 128:SMALL, :], w_ref)], sem
    )
    normal, scale = normal_of(h2_ref[...])
    settle(copies)
    gains = gains_of(small_ref)
    dn = jnp.zeros((rows, 512), F32)
    for part in range(3):
        for side in range(2):
            block = d_ref[4 * side:4 * side + 4, 64 * part:64 * part + 64, :].reshape(256, rows)
            dn = dn + contract(block, queries_of(w_ref, side, part), 0, 1)
    gain_ref[...] = column_sum(dn * normal)
    g2 = g3_ref[...] + back_of(dn, normal, scale, gains[2:3])
    g2_ref[...] = g2
    gs = g2[:, 0:256]
    gs_ref[...] = gs.astype(BF)
    lo_ref[...] = gs[0:RIM].astype(BF)
    hi_ref[...] = gs[rows - RIM:rows].astype(BF)


def conv_back_kernel(info_ref, lo_ref, gs_ref, hi_ref, nm_ref, wp_ref, np_ref, mean_ref,
                     scale_ref, two_ref, one_ref, dw_ref, dnar_ref, table_ref,
                     pt_ref, small_ref, nmf_ref, dsp_ref, sc_ref, hat_ref, sem):
    rim_rows = wp_ref.shape[0]
    rows = rim_rows - 2 * RIM
    main = slice(RIM, RIM + rows)
    copies = launch(
        [small_pair(one_ref, small_ref), (two_ref.at[1, :, :, 256:512, :], pt_ref)], sem
    )
    valid = mask_of(info_ref, rim_rows, RIM)
    gs = jnp.concatenate(
        [lo_ref[...].astype(F32), gs_ref[...].astype(F32), hi_ref[...].astype(F32)], 0
    ).astype(BF)
    mean = mean_ref[:, 0:1]
    scale = scale_ref[:, 0:1]
    table_ref[...] = jnp.zeros_like(table_ref)
    dsp_ref[0:RIM, :] = jnp.zeros((RIM, 256), F32)
    dsp_ref[RIM + rim_rows:, :] = jnp.zeros((RIM, 256), F32)
    settle(copies)

    def first_pass(index, carry):
        one, two = carry
        cols = block_cols(index)
        taps, gain = taps_of(small_ref, index)
        dsp = contract(gs, pt_ref[lax.div(index, 4), lax.rem(index, 4)], 1, 1).astype(BF).astype(F32)
        dsp_ref[RIM:RIM + rim_rows, :] = dsp
        nmf_ref[...] = nm_ref[:, cols].astype(F32)
        inner = dsp[main]
        dn = jnp.zeros((rim_rows, 256), F32)
        for tap in range(9):
            dn = dn + dsp_ref[12 - tap:12 - tap + rim_rows, :] * taps[tap:tap + 1]
            table_ref[tap:tap + 1, cols] = column_sum(nmf_ref[4 + tap:4 + tap + rows, :] * inner)
        dn = dn * valid
        mixed = smooth_unit(wp_ref[:, cols]) + smooth_unit(np_ref[...]) * jnp.where(index == 0, 1.0, 0.0)
        hat = (mixed - mean) * scale
        hat_ref[:, cols] = hat
        table_ref[9:10, cols] = column_sum((dn * hat)[main])
        scaled = dn * gain
        sc_ref[:, cols] = scaled
        return (one + jnp.sum(scaled, -1, keepdims=True),
                two + jnp.sum(scaled * hat, -1, keepdims=True))

    zero = jnp.zeros((rim_rows, 1), F32)
    one, two = lax.fori_loop(0, 8, first_pass, (zero, zero))
    one = one * (1.0 / 2048)
    two = two * (1.0 / 2048)
    back = scale * (sc_ref[:, 0:256] - one - hat_ref[:, 0:256] * two)
    dnar_ref[...] = (back * smooth_slope(np_ref[...])).astype(BF)

    def second_pass(index, carry):
        cols = block_cols(index)
        back = scale[main] * (
            sc_ref[main, cols] - one[main] - hat_ref[main, cols] * two[main]
        )
        dw_ref[:, cols] = (back * smooth_slope(wp_ref[main, cols])).astype(BF)
        return carry

    lax.fori_loop(0, 8, second_pass, 0)


def glu_back_kernel(info_ref, dw_ref, dnar_ref, h1_ref, two_ref, one_ref, g2_ref,
                    a_ref, sg_ref, x_ref, table_ref, gattn_ref, gffn_ref, dx_ref, dab_ref, sums_ref,
                    w2_ref, w1_ref, small_ref, dn_ref, nar_ref, sem):
    rows = g2_ref.shape[0]
    copies = launch([(two_ref, w2_ref)], sem)
    copies1 = launch(
        [small_pair(one_ref, small_ref), (one_ref.at[:, :, 0:128, :], w1_ref)], sem.at[1:3]
    )
    valid = mask_of(info_ref, rows, 0)
    nar_ref[...] = dnar_ref[...].astype(F32)
    dn_ref[...] = jnp.zeros_like(dn_ref)
    normal, scale1 = normal_of(h1_ref[...])
    settle(copies)
    for tap in range(3):
        moved = nar_ref[9 - tap:9 - tap + rows, :].astype(BF)
        dn_ref[...] += contract(moved, narrow_block(w2_ref, tap), 1, 1)

    def step(index, carry):
        dn_ref[...] += contract(dw_ref[:, block_cols(index)], upper_block(w2_ref, index), 1, 1)
        return carry

    lax.fori_loop(0, 8, step, 0)
    settle(copies1)
    gains = gains_of(small_ref)
    dn = dn_ref[...] * valid
    gconv = column_sum(dn * normal)
    g1 = g2_ref[...] + back_of(dn, normal, scale1, gains[1:2])
    sg = sg_ref[...]
    da = (g1 * sg).astype(BF)
    db = (g1 * a_ref[...] * sg * (1.0 - sg)).astype(BF)
    dab_ref[:, 0:512] = da
    dab_ref[:, 512:1024] = db
    sums_ref[0:16, :] = table_ref[...]
    sums_ref[16:24, :] = jnp.zeros((8, 2048), F32)
    sums_ref[17:18, 0:512] = gconv
    sums_ref[18:19, 0:512] = gattn_ref[...]
    sums_ref[19:20, 0:512] = gffn_ref[...]
    dn = contract(da, glu_of(w1_ref, 0), 1, 1) + contract(db, glu_of(w1_ref, 1), 1, 1)
    normal, scale0 = normal_of(x_ref[...].astype(F32))
    sums_ref[16:17, 0:512] = column_sum(dn * normal)
    dx_ref[...] = g1 + back_of(dn, normal, scale0, gains[0:1])


def middle_kernel(info_ref, sp_ref, gs_ref, n3_ref, d_ref, sp2_ref, gs2_ref, n32_ref, d2_ref, out_ref):
    rows = gs_ref.shape[0]
    side = info_ref[0]
    gs = [ref[:, block_cols(side, 128)] for ref in (gs_ref, gs2_ref)]
    for w in range(8):
        cols = slice(256 * w, 256 * w + 256)
        res = both(lambda g, s: contract(g, s, 0, 0),
                   [(g, ref[:, cols]) for g, ref in zip(gs, (sp_ref, sp2_ref))])
        res = res.reshape(8, 16, 256)
        for i in range(2):
            by_shard(out_ref, w, slice(16 * i, 16 * i + 16), res[:, :, 128 * i:128 * i + 128])
    for part in range(3):
        pairs = [(n[...], d[pl.ds(side * 4, 4), 64 * part:64 * part + 64, :].reshape(256, rows))
                 for n, d in ((n3_ref, d_ref), (n32_ref, d2_ref))]
        res = both(lambda n, d: contract(n, d, 0, 1), pairs)
        packed = pair_rows(res)
        for c in range(8):
            by_chip(out_ref, c, slice(32 + 16 * part, 48 + 16 * part), packed[:, c])


def late_kernel(info_ref, n2_ref, dw_ref, dnar_ref, n1_ref, dab_ref, small_ref, n22_ref, dw2_ref,
                dnar2_ref, n12_ref, dab2_ref, small2_ref, out_ref, n2f_ref, narf_ref):
    rows = dw_ref.shape[0]
    side = info_ref[0]
    shifted = []
    dnar = []
    for n_ref, d_ref in ((n2_ref, dnar_ref), (n22_ref, dnar2_ref)):
        n2f_ref[...] = n_ref[...].astype(F32)
        narf_ref[...] = d_ref[...].astype(F32)
        shifted.append([n2f_ref[7 + tap:7 + tap + rows, :].astype(BF) for tap in range(3)])
        dnar.append(narf_ref[RIM:RIM + rows, block_cols(side, 128)].astype(BF))
    for j in range(4):
        cols = block_cols(side * 4 + j)
        res = both(lambda n, d: contract(n, d, 0, 0),
                   [(n[1], ref[:, cols]) for n, ref in zip(shifted, (dw_ref, dw2_ref))])
        for i in range(2):
            part = res[:, 128 * i:128 * i + 128].reshape(8, 64, 128)
            out_ref[2 * j + i, :, 0:64, :] = part.astype(BF)
    narrow = [
        both(lambda n, d: contract(n, d, 0, 0), [(n[tap], d) for n, d in zip(shifted, dnar)])
        for tap in range(3)
    ]
    for w in range(8):
        lanes = pl.ds(pl.multiple_of(w * 256 + side * 128, 128), 128)
        pair = slice(128 * (w // 2), 128 * (w // 2) + 128)
        table = small_ref[0:16, lanes] + small2_ref[0:16, lanes]
        gains = small_ref[16:20, pair] + small2_ref[16:20, pair]
        table = jnp.concatenate([table[0:10], gains, table[14:16]], 0)
        for c in range(8):
            pieces = [n[64 * w + 8 * c:64 * w + 8 * c + 8] for n in narrow]
            pieces += [table[2 * c:2 * c + 2], jnp.zeros((6, 128), F32)]
            out_ref[c, w, 64:96, :] = jnp.concatenate(pieces, 0).astype(BF)
    for place in range(2):
        cols = block_cols(side + 2 * place)
        res = both(lambda n, d: contract(n, d, 0, 0),
                   [(n[...], d[:, cols]) for n, d in ((n1_ref, dab_ref), (n12_ref, dab2_ref))])
        packed = pair_rows(res).astype(BF)
        for w in range(8):
            out_ref[:, w, 96 + 16 * place:112 + 16 * place, :] = packed[w]


def unpack_kernel(info_ref, near_ref, far_ref, gglu_ref, val_ref, gat_ref, gconv_ref, wid_ref, nar_ref,
                  gmid_ref, dep_ref, pnt_ref, gatt_ref, qry_ref, key_ref, vls_ref, outp_ref,
                  gffn_ref, upper_ref, lower_ref, fin_ref, low_ref, pt_ref, table_ref, sem):
    settle(fetch(info_ref[0], near_ref, far_ref, fin_ref, sem))
    for c in range(8):
        for k in range(2):
            fin = fin_ref[k, c].astype(F32)
            lanes = slice(k * 1024 + c * 128, k * 1024 + c * 128 + 128)
            upper_ref[:, lanes] = fin[0:64]
            wid_ref[:, lanes] = fin[EARLY + MIDDLE:EARLY + MIDDLE + 64]
            middle = EARLY
            late = EARLY + MIDDLE
            for i in range(2):
                low_ref[k * 256 + c * 32:k * 256 + c * 32 + 32, 128 * i:128 * i + 128] = (
                    fin[64 + 32 * i:96 + 32 * i]
                )
                pt_ref[k * 128 + c * 16:k * 128 + c * 16 + 16, 128 * i:128 * i + 128] = (
                    fin[middle + 16 * i:middle + 16 * i + 16]
                )
            for tap in range(3):
                nar_ref[tap, 8 * c:8 * c + 8, 128 * k:128 * k + 128] = (
                    fin[late + 64 + 8 * tap:late + 72 + 8 * tap]
                )
            table_ref[2 * c:2 * c + 2, 128 * k:128 * k + 128] = fin[late + 88:late + 90]
            bases = [128] + [middle + 32 + 16 * i for i in range(3)] + [late + 96, late + 112]
            targets = [outp_ref, qry_ref, key_ref, vls_ref, val_ref, gat_ref]
            for base, target in zip(bases, targets):
                for i in range(2):
                    target[8 * c:8 * c + 8, k * 256 + 128 * i:k * 256 + 128 * i + 128] = (
                        fin[base + 8 * i:base + 8 * i + 8]
                    )
    lower_ref[...] = low_ref[...].T
    pnt_ref[...] = pt_ref[...].T
    dep_ref[...] = table_ref[0:9, :]
    gmid_ref[...] = table_ref[9:10, :]
    even = info_ref[3] == 0
    gains = jnp.where(even, table_ref[10:14, 0:64], table_ref[10:14, 64:128])
    gglu_ref[...] = gains[0:1]
    gconv_ref[...] = gains[1:2]
    gatt_ref[...] = gains[2:3]
    gffn_ref[...] = gains[3:4]


def pack_ring_kernel(info_ref, wide_ref, narrow_ref, point_ref, out_ref, sem):
    core = info_ref[0]
    pairs = [
        (wide_ref.at[:, block_cols(core * 4 + j)], out_ref.at[64 * j:64 * j + 64, :]) for j in range(4)
    ]
    copies = launch(pairs, sem)

    @pl.when(core == 0)
    def _():
        settle(launch([(narrow_ref, out_ref.at[256:448, :]),
                       (narrow_ref.at[0:64, :], out_ref.at[448:512, :])], sem.at[4:6]))

    @pl.when(core == 1)
    def _():
        settle(launch([(point_ref, out_ref.at[256:512, :])], sem.at[4:5]))

    settle(copies)


def pack_rest_kernel(info_ref, value_ref, gate_ref, query_ref, key_ref, values_ref, g0_ref, g1_ref,
                     g2_ref, g3_ref, depth_ref, mid_ref, in_ref, out_ref, outw_ref, one_ref,
                     three_ref, pack_ref, g0, g1, g2, g3, depth, mid, sem):
    core = info_ref[0]
    own = block_cols(core)
    small = [(g0_ref, g0), (g1_ref, g1), (g2_ref, g2), (g3_ref, g3), (depth_ref, depth), (mid_ref, mid)]
    small = launch(small, sem)
    weights = launch(
        [(ref.at[:, own], pack_ref.at[128 + 64 * i:192 + 64 * i, :])
         for i, ref in enumerate((query_ref, key_ref, values_ref))], sem.at[6:9],
    )
    later = [(in_ref.at[:, block_cols(core * 4 + j)], three_ref.at[64 * j:64 * j + 64, :]) for j in range(4)]
    later += [(out_ref.at[:, own], three_ref.at[256:512, :]), (outw_ref.at[:, own], three_ref.at[512:576, :])]
    later = launch(later, sem.at[9:15])
    for index, ref in ((0, value_ref), (1, gate_ref)):
        @pl.when(core == index)
        def _():
            settle(launch([(ref.at[:, 256 * i:256 * i + 256], pack_ref.at[64 * i:64 * i + 64, :])
                           for i in range(2)], sem.at[15:17]))
    settle(small)
    gains = jnp.concatenate(
        [ref[...].astype(F32) for ref in (g0, g1, g2, g3)] + [jnp.zeros((4, 64), F32)], 0
    )
    gains = jnp.concatenate([gains] * 8, 1)
    place = lax.broadcasted_iota(jnp.int32, (8, 512), 1)
    start = (info_ref[5] * 4 + info_ref[4]) * 64
    gains = jnp.where((place >= start) & (place < start + 64), gains, 0.0)
    gains = jnp.concatenate([gains[:, 0:256], gains[:, 256:512]], 0)
    pack_ref[SMALL:SMALL + 16, :] = gains.astype(BF)
    taps = jnp.concatenate([depth[...].astype(F32), mid[...].astype(F32), jnp.zeros((6, 256), F32)], 0)
    pack_ref[SMALL + 16:SMALL + 32, :] = taps.astype(BF)
    settle(weights)
    for w in range(8):
        one_ref[w] = pack_ref[...]
    settle(later)


def over_x(value):
    value = value.reshape((4,) + value.shape[2:])
    return lax.psum_scatter(value, ("xh", "xl"), scatter_dimension=0, tiled=True)[0]


def over_z(value):
    return lax.psum_scatter(value, "z", scatter_dimension=0, tiled=True)[0]


def spread_out(own, axes, count):
    copies = jnp.broadcast_to(own[None], (count,) + own.shape)
    return lax.all_to_all(copies, axes, 0, 0, tiled=True)


def shards(
    inputs, lengths, cotangent, glu_gain, glu_value, glu_gate, conv_gain, wide_weight,
    narrow_weight, mid_gain, depth_weight, point_weight, attn_gain, query_weight, key_weight,
    value_weight, output_weight, ffn_gain, ffn_in, ffn_out,
):
    rows, width = inputs.shape[1], inputs.shape[2]
    units = wide_weight.shape[1]
    rim_rows = rows + 2 * RIM
    core = lax.axis_index("core")
    shard = lax.axis_index("xl") * 4 + lax.axis_index("z")
    first = (lax.axis_index("y") * 4 + lax.axis_index("xh") * 2 + core) * rows
    xl, z = lax.axis_index("xl"), lax.axis_index("z")
    info = jnp.stack([core, first, lengths[0], shard % 2, z, xl]).astype(jnp.int32)
    flip = shift(dc=1)
    dma = pltpu.SemaphoreType.DMA

    pack2 = call(
        pack_ring_kernel, [((512, 256), BF, FREE)], [SMEM] + [HBM] * 3, [dma((6,))], "pack_ring", 1,
        info, wide_weight, narrow_weight.reshape(192, 256), point_weight,
    )[0]
    steps = [shift(dz=-1), shift(dz=2), shift(dz=1)]
    other = send(pack2, shift(dxl=1))
    own_pieces = [send(pack2, step) for step in steps]
    other_pieces = [send(other, step) for step in steps]

    line = lambda v: v.reshape(1, -1)
    pack1, pack3 = call(
        pack_rest_kernel, [((8, SMALL + 32, 256), BF, FREE), ((576, 256), BF, FREE)], [SMEM] + [HBM] * 14,
        [pltpu.VMEM((SMALL + 32, 256), BF)] + [pltpu.VMEM((1, 64), BF)] * 4
        + [pltpu.VMEM((9, 256), BF), pltpu.VMEM((1, 256), BF), dma((17,))],
        "pack_rest", 1, info, glu_value, glu_gate, query_weight, key_weight, value_weight,
        line(glu_gain), line(conv_gain), line(attn_gain), line(ffn_gain), depth_weight,
        line(mid_gain), ffn_in, ffn_out, output_weight,
    )

    pack1, *_ = lax.optimization_barrier((pack1, *own_pieces, other))
    near1 = lax.all_to_all(pack1, WT, 0, 0, tiled=True)
    x = inputs[0]
    low_x = send(x[rows - RIM:], along(1))
    high_x = send(x[:RIM], along(-1))
    other3 = send(pack3, shift(dxl=1))
    near1, pack3, other3, low_x, high_x, *ready = lax.optimization_barrier(
        (near1, pack3, other3, low_x, high_x, *own_pieces, *other_pieces)
    )
    near2 = [pack2] + ready[:3] + [other] + ready[3:]
    far2 = [send(piece, flip) for piece in near2]
    far1 = send(near1, flip)
    near3 = lax.all_gather(jnp.stack([pack3, other3]), "z", axis=0)

    tall, wide, narrow = (rows, width), (rows, units), (rows, 256)
    tiny = pltpu.VMEM((8, 32, 256), BF)
    ring = pltpu.VMEM((2, 2, 4) + pack2.shape, BF)
    n1, a, sg, h1, h1m, one = call(
        glu_kernel,
        [(tall, BF), (tall, F32), (tall, F32), ((rim_rows, width), F32, FREE), (tall, F32),
         ((2,) + near1.shape, BF, HBM)],
        [SMEM] + [FREE] * 3 + [ANY] * 2, [pltpu.VMEM((2,) + near1.shape, BF), dma((2,))], "glu", 3,
        info, low_x, x, high_x, near1, far1,
    )
    n2, wp, np_, nm, mean, scale, sp, h2, n3, qkv, two = call(
        conv_kernel,
        [((rim_rows, width), BF), ((rim_rows, units), F32, HBM), ((rim_rows, 256), F32),
         ((rim_rows, units), BF, HBM), ((rim_rows, 128), F32), ((rim_rows, 128), F32),
         (wide, BF, HBM), (tall, F32), (tall, BF), ((HEADS, 3 * HEAD, rows), BF, FREE),
         (ring.shape, BF, HBM)],
        [SMEM, FREE] + [ANY] * 16 + [HBM],
        [ring, pltpu.VMEM((2, 8, SMALL - 128, 256), BF), tiny, pltpu.VMEM((rim_rows, units), F32),
         pltpu.VMEM((rim_rows, units), F32), pltpu.VMEM((rim_rows, units), BF), pltpu.VMEM(wide, BF),
         dma((16,)), dma((2,)), dma((3, 8))],
        "conv", 15, info, h1, *near2, *far2, one,
    )
    near = lax.all_to_all(qkv, CHIPS, 0, 0, tiled=True)
    far = send(near[:, HEAD:], flip)
    head_out, expo, inverse, near, far = attend(near, far, lengths, info[:1])
    near3, _ = lax.optimization_barrier((near3, head_out))
    far3 = send(near3, flip)
    heads_in = lax.all_to_all(head_out, CHIPS, 0, 0, tiled=True)
    output, acts, g3, dob, d_gffn, heads_in = call(
        ffn_kernel,
        [(tall, BF), ((rows, 5632), BF), (tall, F32), ((HEADS, HEAD, rows), BF, FREE),
         ((1, width), F32), ((HEADS, HEAD, rows), BF)],
        [SMEM, VMEM, FREE, VMEM, HBM, HBM, ANY],
        [pltpu.VMEM((2, 2, 4) + pack3.shape, BF), tiny, pltpu.VMEM(tall, F32), pltpu.VMEM(tall, F32),
         dma((5,))],
        "ffn", 11, info, h2, heads_in, cotangent[0], one, near3, far3,
    )

    d_near = lax.all_to_all(dob, CHIPS, 0, 0, tiled=True)
    early = call(
        early_kernel, [((2, 2, 4, 4, EARLY, 128), BF)], [SMEM] + [VMEM] * 2 + [FREE] * 2, [], "early", 0.3,
        info, acts, heads_in, send(acts, flip), send(heads_in, flip),
    )[0]
    d_near, early = lax.optimization_barrier((d_near, early))
    early = over_x(early)
    dq, dk, dv = attend_back(near, far, expo, head_out, inverse, d_near)
    d_far = send(jnp.concatenate([dk[1], dv[1]], 1), flip).astype(F32)
    d_own = jnp.concatenate([dk[0], dv[0]], 1).astype(F32)
    d_qkv = jnp.concatenate([dq, (d_own + d_far).astype(BF)], 1)
    d_qkv = lax.all_to_all(d_qkv, CHIPS, 0, 0, tiled=True)
    early, _ = lax.optimization_barrier((early, d_qkv))
    early = over_z(early)
    g2, gs, lo, hi, d_gatt = call(
        attn_in_kernel,
        [(tall, F32), (narrow, BF), ((RIM, 256), BF), ((RIM, 256), BF), ((1, width), F32)],
        [SMEM, FREE] + [VMEM] * 2 + [HBM],
        [pltpu.VMEM((2, 8, SMALL - 128, 256), BF), tiny, dma((2,))],
        "attn_in", 0.5, info, d_qkv, h2, g3, one,
    )
    low_gs = send(hi, along(1))
    high_gs = send(lo, along(-1))
    middle = call(
        middle_kernel, [((2, 2, 4, 4, MIDDLE, 128), BF)], [SMEM] + [VMEM] * 3 + [FREE] * 5, [], "middle", 0.3,
        info, sp, gs, n3, d_qkv, *[send(v, flip) for v in (sp, gs, n3, d_qkv)],
    )[0]
    low_gs, high_gs, middle = lax.optimization_barrier((low_gs, high_gs, middle))
    middle = over_x(middle)
    rim_narrow = ((rim_rows, 256), BF)
    dw, dnar, table = call(
        conv_back_kernel, [(wide, BF), rim_narrow, ((16, units), F32)],
        [SMEM, FREE, VMEM, FREE] + [VMEM] * 5 + [HBM] * 2,
        [pltpu.VMEM((2, 4, 256, 256), BF), tiny, pltpu.VMEM((rim_rows, 256), F32), pltpu.VMEM((rim_rows + 2 * RIM, 256), F32),
         pltpu.VMEM((rim_rows, units), F32), pltpu.VMEM((rim_rows, units), F32), dma((2,))],
        "conv_back", 2, info, low_gs, gs, high_gs, nm, wp, np_, mean, scale, two, one,
    )
    dw2, dnar2 = send(dw, flip), send(dnar, flip)
    g2, early = lax.optimization_barrier((g2, early))
    dx, dab, sums = call(
        glu_back_kernel, [(tall, F32), ((rows, 2 * width), BF), ((24, units), F32)],
        [SMEM] + [VMEM] * 3 + [HBM] * 2 + [VMEM] * 7,
        [ring, pltpu.VMEM((2, 8, 128, 256), BF), tiny, pltpu.VMEM(tall, F32),
         pltpu.VMEM((rim_rows, 256), F32), dma((3,))],
        "glu_back", 1, info, dw, dnar, h1m, two, one, g2, a, sg, x, table, d_gatt, d_gffn,
    )
    dab2, sums2 = send(dab, flip), send(sums, flip)
    dab2, middle = lax.optimization_barrier((dab2, middle))
    middle = over_z(middle)
    late = call(
        late_kernel, [((8, 8, LATE, 128), BF)], [SMEM] + [VMEM] * 6 + [FREE] * 6,
        [pltpu.VMEM((rim_rows, width), F32), pltpu.VMEM((rim_rows, 256), F32)], "late", 0.5,
        info, n2, dw, dnar, n1, dab, sums, send(n2, flip), dw2, dnar2, send(n1, flip), dab2, sums2,
    )[0]
    _, early, middle = lax.optimization_barrier((late, early, middle))
    y = lax.axis_index("y")
    pieces = jnp.concatenate([early, middle], 1)
    pick = lambda index: lax.dynamic_index_in_dim(pieces, index % 4, 0, keepdims=False)
    parts = [send(pick(y + d), shift(dy=d)) for d in (1, 2, 3)]
    early = sum((part.astype(F32) for part in parts), pick(y).astype(F32)).astype(BF)
    late = lax.all_to_all(late.reshape(64, LATE, 128), CHIPS + WT, 0, 0, tiled=True)
    late = jnp.sum(late.astype(F32), 0).astype(BF)
    final = spread_out(jnp.concatenate([early, late], 0), CHIPS, 8)
    square, broad = ((64, 512), F32), ((64, 2048), F32)
    line = ((1, 64), F32)
    grads = call(
        unpack_kernel,
        [line, square, square, line, broad, ((3, 64, 256), F32), ((1, 256), F32),
         ((9, 256), F32), ((256, 256), F32), line, square, square, square, square, line, broad,
         ((256, 512), F32)],
        [SMEM, ANY, ANY],
        [pltpu.VMEM((2,) + final.shape, BF), pltpu.VMEM((512, 256), F32),
         pltpu.VMEM((256, 256), F32), pltpu.VMEM((16, 256), F32), dma((2,))],
        "unpack", 3, info, final, send(final, flip),
    )
    grads = [g[0] if g.shape[0] == 1 else g for g in grads]
    return (output[None], dx[None]) + tuple(grads)


def solution(mesh):
    fine = Mesh(mesh.devices.reshape(SIZES), AXES)
    flat, row, mid = P(WT), P(WT, None), P(None, WT, None)
    col = P(None, WT)
    tokens = P(WT, CTX, None)
    weights = (
        flat, row, row, flat, row, mid, flat, col, row, flat, row, row, row, row, flat, row, row,
    )
    return jax.shard_map(
        shards, mesh=fine, in_specs=(tokens, flat, tokens) + weights,
        out_specs=(tokens, tokens) + weights, check_vma=False,
    )
```

```python
import functools

import jax
import jax.numpy as jnp
import numpy as np
from jax import lax
from jax.experimental import pallas as pl
from jax.experimental.pallas import tpu as pltpu
from jax.sharding import Mesh
from jax.sharding import PartitionSpec as P

HEADS = 8
HEAD = 64
EPSILON = 1e-06
AXES = ("y", "xh", "core", "xl", "z")
SIZES = (4, 2, 2, 2, 4)
CTX = ("y", "xh", "core")
CHIPS = ("y", "xh")
WT = ("xl", "z")
BLOCK = 1024
LOG2E = 1.4426950408889634
BF = jnp.bfloat16
F32 = jnp.float32


def moves(target):
    pairs = []
    for source in range(int(np.prod(SIZES))):
        place = [int(v) for v in np.unravel_index(source, SIZES)]
        goal = target(*place)
        if goal is not None:
            pairs.append((source, int(np.ravel_multi_index(tuple(goal), SIZES))))
    return pairs


def shift(dy=0, dxh=0, dc=0, dxl=0, dz=0):
    return moves(
        lambda y, xh, c, xl, z: (
            (y + dy) % 4, (xh + dxh) % 2, (c + dc) % 2, (xl + dxl) % 2, (z + dz) % 4,
        )
    )


def along(step):
    def target(y, xh, c, xl, z):
        place = y * 4 + xh * 2 + c + step
        if place < 0 or place > 15:
            return None
        return (place // 4, place // 2 % 2, place % 2, xl, z)
    return moves(target)


def send(value, pairs):
    return lax.ppermute(value, AXES, pairs)


def matmul(left, right):
    return jnp.dot(left, right, preferred_element_type=F32)


def contract(left, right, ldim, rdim):
    return lax.dot_general(
        left, right, (((ldim,), (rdim,)), ((), ())), preferred_element_type=F32
    )


def smooth_unit(value):
    return value * jax.nn.sigmoid(value)


def smooth_slope(value):
    sigma = jax.nn.sigmoid(value)
    return sigma * (1.0 + value * (1.0 - sigma))


VMEM = pl.BlockSpec(memory_space=pltpu.VMEM)
SMEM = pl.BlockSpec(memory_space=pltpu.SMEM)
HBM = pl.BlockSpec(memory_space=pltpu.HBM)
ANY = pl.BlockSpec(memory_space=pl.ANY)
FREE = "free"


def attend_kernel(chips, rows, length_ref, core_ref, near_ref, far_ref, o_ref, e_ref, l_ref,
                  near_out, far_out, keys_ref, values_ref, sem):
    step = pl.program_id(0)
    span = chips * rows
    aug = 2 * HEAD
    pairs = [(near_ref, near_out), (far_ref, far_out)]

    @pl.when(step == chips - 1)
    def _():
        for i, (source, target) in enumerate(pairs):
            pltpu.make_async_copy(source, target, sem.at[i]).wait()

    @pl.when(step == 0)
    def _():
        launch(pairs, sem)
        length = length_ref[0]
        core = core_ref[0]
        ones = jnp.ones((16, rows), F32)
        for side in range(2):
            source = near_ref if side == 0 else far_ref
            base = HEAD if side == 0 else 0
            owner = core if side == 0 else 1 - core
            for chip in range(chips):
                cols = slice(side * span + chip * rows, side * span + (chip + 1) * rows)
                key = source[chip, base:base + HEAD, :]
                keys_ref[0:HEAD, cols] = key
                keys_ref[HEAD:aug, cols] = key
                place = (chip * 2 + owner) * rows + lax.broadcasted_iota(jnp.int32, (16, rows), 1)
                row = lax.broadcasted_iota(jnp.int32, (16, rows), 0)
                bias = jnp.where((place < length) | (row > 0), 0.0, -1e30)
                keys_ref[aug:aug + 16, cols] = bias.astype(BF)
                value = source[chip, base + HEAD:base + 2 * HEAD, :].astype(F32)
                stacked = jnp.concatenate([value, ones, jnp.zeros((48, rows), F32)], 0)
                values_ref[cols, :] = stacked.T.astype(BF)

    query = near_ref[step, 0:HEAD, :].astype(F32) * (LOG2E * HEAD ** -0.5)
    high = query.astype(BF)
    low = (query - high.astype(F32)).astype(BF)
    query = jnp.concatenate([high, low, jnp.ones((16, rows), BF)], 0)
    scores = contract(query, keys_ref[...], 0, 0)
    top = jnp.max(scores, 1, keepdims=True)
    expo = jnp.exp2(scores - top).astype(BF)
    e_ref[...] = expo
    out = matmul(expo, values_ref[...]).T
    inverse = 1.0 / out[HEAD:HEAD + 8]
    o_ref[0] = (out[0:HEAD] * inverse[0:1]).astype(BF)
    l_ref[0] = inverse


def attend(near, far, length, core):
    chips, _, rows = near.shape
    tokens = 2 * chips * rows
    return pl.pallas_call(
        functools.partial(attend_kernel, chips, rows),
        grid=(chips,),
        in_specs=[
            pl.BlockSpec(memory_space=pltpu.SMEM),
            pl.BlockSpec(memory_space=pltpu.SMEM),
            pl.BlockSpec(near.shape, lambda i: (0, 0, 0)),
            pl.BlockSpec(far.shape, lambda i: (0, 0, 0)),
        ],
        out_specs=[
            pl.BlockSpec((1, HEAD, rows), lambda i: (i, 0, 0)),
            pl.BlockSpec((rows, tokens), lambda i: (i, 0)),
            pl.BlockSpec((1, 8, rows), lambda i: (i, 0, 0)),
            HBM,
            HBM,
        ],
        out_shape=[
            pltpu.HBM((chips, HEAD, rows), BF),
            pltpu.HBM((chips * rows, tokens), BF),
            pltpu.HBM((chips, 8, rows), F32),
            pltpu.HBM(near.shape, BF),
            pltpu.HBM(far.shape, BF),
        ],
        scratch_shapes=[
            pltpu.VMEM((2 * HEAD + 16, tokens), BF),
            pltpu.VMEM((tokens, 2 * HEAD), BF),
            pltpu.SemaphoreType.DMA((2,)),
        ],
        compiler_params=pltpu.CompilerParams(vmem_limit_bytes=32 * 2**20),
        cost_estimate=cost(14),
        name="attend",
    )(length, core, near, far)


def attend_back_kernel(chips, rows, near_ref, far_ref, e_ref, o_ref, l_ref, do_ref,
                       dq_ref, dk_ref, dv_ref, keys_ref, values_ref, dk_acc, dv_acc):
    step = pl.program_id(0)
    span = chips * rows

    @pl.when(step == 0)
    def _():
        row = lax.broadcasted_iota(jnp.int32, (16, rows), 0)
        ones = jnp.where(row < 3, 1.0, 0.0).astype(BF)
        for side in range(2):
            source = near_ref if side == 0 else far_ref
            base = HEAD if side == 0 else 0
            for chip in range(chips):
                cols = slice(side * span + chip * rows, side * span + (chip + 1) * rows)
                key = source[chip, base:base + HEAD, :].astype(F32)
                stacked = jnp.concatenate([key, jnp.zeros((HEAD, rows), F32)], 0)
                keys_ref[cols, :] = stacked.T.astype(BF)
                values_ref[0:HEAD, cols] = source[chip, base + HEAD:base + 2 * HEAD, :]
                values_ref[HEAD:HEAD + 16, cols] = ones
        dk_acc[...] = jnp.zeros_like(dk_acc)
        dv_acc[...] = jnp.zeros_like(dv_acc)

    inverse = l_ref[0, 0:1, :]
    grad = do_ref[0].astype(F32) * inverse
    total = -jnp.sum(grad * o_ref[0].astype(F32), 0, keepdims=True)
    high = total.astype(BF).astype(F32)
    mid = (total - high).astype(BF).astype(F32)
    low = total - high - mid
    grad_low = grad.astype(BF)
    row = lax.broadcasted_iota(jnp.int32, (16, rows), 0)
    extra = jnp.where(row == 0, high, jnp.where(row == 1, mid, jnp.where(row == 2, low, 0.0)))
    grads = jnp.concatenate([grad_low, extra.astype(BF)], 0)
    query = near_ref[step, 0:HEAD, :]
    grads = grads.T
    block = BLOCK
    dq = jnp.zeros((rows, 2 * HEAD), F32)
    for start in range(0, 2 * span, block):
        cols = slice(start, start + block)
        expo = e_ref[:, cols]
        d_scores = (expo.astype(F32) * matmul(grads, values_ref[:, cols])).astype(BF)
        dq = dq + matmul(d_scores, keys_ref[cols, :])
        dk_acc[:, cols] += matmul(query, d_scores)
        dv_acc[:, cols] += matmul(grad_low, expo)
    dq_ref[0] = (dq.T[0:HEAD] * HEAD ** -0.5).astype(BF)

    @pl.when(step == chips - 1)
    def _():
        for side in range(2):
            for chip in range(chips):
                cols = slice(side * span + chip * rows, side * span + (chip + 1) * rows)
                dk_ref[side, chip] = (dk_acc[:, cols] * HEAD ** -0.5).astype(BF)
                dv_ref[side, chip] = dv_acc[:, cols].astype(BF)


def attend_back(near, far, expo, out, inverse, d_out):
    chips, _, rows = near.shape
    tokens = 2 * chips * rows
    whole = lambda i: (0, 0, 0)
    one = lambda i: (i, 0, 0)
    return pl.pallas_call(
        functools.partial(attend_back_kernel, chips, rows),
        grid=(chips,),
        in_specs=[
            pl.BlockSpec(near.shape, whole),
            pl.BlockSpec(far.shape, whole),
            pl.BlockSpec((rows, tokens), lambda i: (i, 0)),
            pl.BlockSpec((1, HEAD, rows), one),
            pl.BlockSpec((1, 8, rows), one),
            pl.BlockSpec((1, HEAD, rows), one),
        ],
        out_specs=[
            pl.BlockSpec((1, HEAD, rows), one),
            pl.BlockSpec((2, chips, HEAD, rows), lambda i: (0, 0, 0, 0)),
            pl.BlockSpec((2, chips, HEAD, rows), lambda i: (0, 0, 0, 0)),
        ],
        out_shape=[
            pltpu.HBM((chips, HEAD, rows), BF),
            jax.ShapeDtypeStruct((2, chips, HEAD, rows), BF),
            jax.ShapeDtypeStruct((2, chips, HEAD, rows), BF),
        ],
        scratch_shapes=[
            pltpu.VMEM((tokens, 2 * HEAD), BF),
            pltpu.VMEM((HEAD + 16, tokens), BF),
            pltpu.VMEM((HEAD, tokens), F32),
            pltpu.VMEM((HEAD, tokens), F32),
        ],
        compiler_params=pltpu.CompilerParams(vmem_limit_bytes=32 * 2**20),
        cost_estimate=cost(3),
        name="attend_back",
    )(in_hbm(near), in_hbm(far), in_hbm(expo), in_hbm(out), in_hbm(inverse), d_out)


RIM = 8
FOLD = 15
ACT_N4 = slice(4096, 4608)
ACT_GY = slice(4608, 5120)
ACT_GA = slice(5120, 5632)
EARLY = 144
SMALL = 320
MIDDLE = 80
LATE = 128


def call(kernel, outs, specs, scratch, name, micros, *args):
    args = [arg if spec in (SMEM, FREE, ANY) else in_hbm(arg) for arg, spec in zip(args, specs)]
    kinds = [out[2] if len(out) > 2 else VMEM for out in outs]
    return pl.pallas_call(
        kernel,
        in_specs=[VMEM if spec is FREE else spec for spec in specs],
        out_specs=[VMEM if kind is FREE else kind for kind in kinds],
        out_shape=[
            (jax.ShapeDtypeStruct if kind is FREE else pltpu.HBM)(out[0], out[1])
            for kind, out in zip(kinds, outs)
        ],
        scratch_shapes=scratch,
        compiler_params=pltpu.CompilerParams(vmem_limit_bytes=32 * 2**20),
        cost_estimate=cost(micros),
        name=name,
    )(*args)


def in_hbm(value):
    return pltpu.with_memory_space_constraint(value, pltpu.HBM)


def cost(micros):
    return pl.CostEstimate(
        flops=int(micros * 1.0e9), bytes_accessed=int(micros * 3.0e6), transcendentals=0
    )


def launch(pairs, sems):
    copies = [
        pltpu.make_async_copy(source, target, sems.at[i]) for i, (source, target) in enumerate(pairs)
    ]
    for copy in copies:
        copy.start()
    return copies


def fetch(core, near_ref, far_ref, both_ref, sems):
    return launch([(near_ref, both_ref.at[core]), (far_ref, both_ref.at[1 - core])], sems)


def settle(copies):
    for copy in copies:
        copy.wait()


def gains_of(small_ref):
    total = small_ref[0, 0:16, :].astype(F32)
    for w in range(1, 8):
        total = total + small_ref[w, 0:16, :].astype(F32)
    return jnp.concatenate([total[0:8], total[8:16]], 1)


def taps_of(small_ref, index):
    small = small_ref[index, 16:32, :].astype(F32)
    return small[0:9], small[9:10]


def normal_of(value):
    average = jnp.mean(value, -1, keepdims=True)
    centred = value - average
    scale = lax.rsqrt(jnp.mean(centred * centred, -1, keepdims=True) + EPSILON)
    return centred * scale, scale


def back_of(incoming, normal, scale, gain):
    scaled = incoming * gain
    return scale * (
        scaled
        - jnp.mean(scaled, -1, keepdims=True)
        - normal * jnp.mean(scaled * normal, -1, keepdims=True)
    )


def column_sum(value):
    return jnp.sum(value, 0, keepdims=True)


def mask_of(info_ref, count, before):
    place = info_ref[1] - before + lax.broadcasted_iota(jnp.int32, (count, 1), 0)
    return jnp.where((place >= 0) & (place < info_ref[2]), 1.0, 0.0)


def block_cols(index, size=256):
    return pl.ds(pl.multiple_of(index * size, size), size)


def upper_block(both_ref, index):
    rows = pl.ds(pl.multiple_of(lax.rem(index, 4) * 64, 64), 64)
    if len(both_ref.shape) == 5:
        return both_ref[lax.div(index, 4), :, :, rows, :].reshape(512, 256)
    return both_ref[lax.div(index, 4), :, rows, :].reshape(512, 256)


def narrow_block(both_ref, tap):
    return both_ref[0, :, :, 256 + 64 * tap:320 + 64 * tap, :].reshape(512, 256)


def point_block(both_ref, index):
    return both_ref[1, lax.div(index, 4), lax.rem(index, 4), 256:512, :]


def collect(info_ref, near_refs, far_refs, both_ref, sems, rows=slice(0, 512)):
    core, x, z = info_ref[0], info_ref[5], info_ref[4]
    copies = []
    for side, refs in ((core, near_refs), (1 - core, far_refs)):
        for i, ref in enumerate(refs):
            place = x if i < 4 else 1 - x
            target = both_ref.at[side, place, lax.rem(z + i % 4, 4), rows]
            copies.append((ref.at[rows], target))
    return launch(copies, sems)


def glu_of(both_ref, side):
    return jnp.concatenate(
        [both_ref[side, :, 64 * i:64 * i + 64, :].reshape(512, 256) for i in range(2)], 1
    )


def queries_of(both_ref, side, part):
    return both_ref[side, :, 64 * part:64 * part + 64, :].reshape(512, 256)


def small_pair(one_ref, small_ref):
    return (one_ref.at[0, :, SMALL:SMALL + 32, :], small_ref)


def glu_kernel(info_ref, low_ref, x_ref, high_ref, near_ref, far_ref, n1_ref, a_ref, sg_ref, h1_ref,
               main_ref, w_ref, small_ref, sem):
    rows = x_ref.shape[0]
    main = slice(RIM, RIM + rows)
    core = info_ref[0]
    copies = launch(
        [(near_ref.at[:, SMALL:SMALL + 32, :], small_ref), (near_ref.at[:, 0:128, :], w_ref.at[core]),
         (far_ref.at[:, 0:128, :], w_ref.at[1 - core])], sem
    )
    x = jnp.concatenate(
        [low_ref[...].astype(F32), x_ref[...].astype(F32), high_ref[...].astype(F32)], 0
    )
    normal, _ = normal_of(x)
    settle(copies)
    normed = normal * gains_of(small_ref)[0:1]
    n1 = normed.astype(BF)
    n1_ref[...] = normed[main].astype(BF)
    a = matmul(n1, glu_of(w_ref, 0))
    sg = jax.nn.sigmoid(matmul(n1, glu_of(w_ref, 1)))
    a_ref[...] = a[main].astype(BF)
    sg_ref[...] = sg[main].astype(BF)
    h1 = x + a * sg
    h1_ref[...] = h1
    main_ref[...] = h1[main]


def conv_kernel(info_ref, h1_ref, *refs):
    near2, far2, rest = refs[0:8], refs[8:16], refs[16:]
    conv_body(info_ref, h1_ref, near2, far2, *rest)


def conv_body(info_ref, h1_ref, near2, far2, near1_ref, far1_ref,
              n2_ref, wp_out, np_ref, nm_out, mean_ref, scale_ref, sp_out, h2_ref, n3_ref,
              qkv_ref, two_ref, one_ref, w2_ref, w1_ref, mix_ref, wp_ref, nm_ref, sp_ref, slab_ref,
              sem2, semq, sems):
    core = info_ref[0]
    rim_rows = h1_ref.shape[0]
    rows = rim_rows - 2 * RIM
    copiesq = fetch(core, near1_ref, far1_ref, w1_ref, semq)
    copies2 = collect(info_ref, near2, far2, w2_ref, sem2)
    small_ref = w1_ref.at[0, :, SMALL:SMALL + 32, :]
    settle(copiesq)
    copiesq = launch([(w1_ref, one_ref)], semq)

    def leaving(which, index):
        source, target = ((wp_ref, wp_out), (nm_ref, nm_out), (sp_ref, sp_out))[which]
        cols = block_cols(index)
        return pltpu.make_async_copy(source.at[:, cols], target.at[:, cols], sems.at[which, index])

    gains = gains_of(small_ref)
    valid = mask_of(info_ref, rim_rows, RIM)
    normal, _ = normal_of(h1_ref[...])
    n2f = normal * gains[1:2] * valid
    n2 = n2f.astype(BF)
    n2_ref[...] = n2
    n2f = n2.astype(F32)
    settle(copies2)
    copies2 = launch([(w2_ref, two_ref)], sem2)
    narrow = jnp.zeros((rim_rows, 256), F32)
    for tap in range(3):
        if tap == 1:
            moved = n2
        else:
            moved = pltpu.roll(n2f, 1 if tap == 0 else rim_rows - 1, 0).astype(BF)
        narrow = narrow + matmul(moved, narrow_block(w2_ref, tap))
    np_ref[...] = narrow
    narrow = smooth_unit(narrow)

    def first_pass(index, total):
        weights = jnp.concatenate([upper_block(w2_ref, 2 * index + i) for i in range(2)], 1)
        wide = matmul(n2_ref[...], weights)
        wp_ref[:, block_cols(index, 512)] = wide
        for i in range(2):
            leaving(0, 2 * index + i).start()
        mixed = smooth_unit(wide)
        head = mixed[:, 0:256] + narrow * jnp.where(index == 0, 1.0, 0.0)
        mixed = jnp.concatenate([head, mixed[:, 256:512]], 1)
        mix_ref[:, block_cols(index, 512)] = mixed
        return total + jnp.sum(mixed, -1, keepdims=True)

    total = lax.fori_loop(0, 4, first_pass, jnp.zeros((rim_rows, 1), F32))
    mean = total * (1.0 / 2048)

    total = jnp.zeros((rim_rows, 1), F32)
    for index in range(8):
        centred = mix_ref[:, 256 * index:256 * index + 256] - mean
        total = total + jnp.sum(centred * centred, -1, keepdims=True)
    scale = lax.rsqrt(total * (1.0 / 2048) + EPSILON)
    mean_ref[...] = jnp.broadcast_to(mean, mean_ref.shape)
    scale_ref[...] = jnp.broadcast_to(scale, scale_ref.shape)
    h2_ref[...] = h1_ref[RIM:RIM + rows, :]

    def third_pass(index, carry):
        cols = block_cols(index)
        taps, gain = taps_of(small_ref, index)
        nm = ((mix_ref[:, cols] - mean) * scale * gain * valid).astype(BF)
        nm_ref[:, cols] = nm
        leaving(1, index).start()
        nm = nm.astype(F32)
        halves = []
        for half in range(2):
            lanes = slice(128 * half, 128 * half + 128)
            slab_ref[half] = nm[:, lanes]
            spread = jnp.zeros((rows, 128), F32)
            for tap in range(9):
                spread = spread + slab_ref[half, 4 + tap:4 + tap + rows, :] * taps[tap:tap + 1, lanes]
            halves.append(spread)
        spread = jnp.concatenate(halves, 1).astype(BF)
        sp_ref[:, cols] = spread
        leaving(2, index).start()
        h2_ref[:, 0:256] += matmul(spread, point_block(w2_ref, index))
        return carry

    lax.fori_loop(0, 8, third_pass, 0, unroll=2)
    normal, _ = normal_of(h2_ref[...])
    n3 = (normal * gains[2:3]).astype(BF)
    n3_ref[...] = n3
    for part in range(3):
        for side in range(2):
            block = matmul(n3, w1_ref[side, :, 128 + 64 * part:192 + 64 * part, :].reshape(512, 256))
            qkv_ref[4 * side:4 * side + 4, 64 * part:64 * part + 64, :] = (
                block.T.astype(BF).reshape(4, 64, rows)
            )
    settle(copies2 + copiesq)
    for which in range(3):
        for index in range(8):
            leaving(which, index).wait()


def ffn_kernel(info_ref, h2_ref, o_ref, cot_ref, one_ref, near_ref, far_ref,
               out_ref, acts_ref, g3_ref, dob_ref, gain_ref, heads_ref,
               w_ref, small_ref, y_ref, dn_ref, sem):
    rows = h2_ref.shape[0]
    core = info_ref[0]
    x = info_ref[5]
    pairs = [small_pair(one_ref, small_ref)]
    for side, ref in ((core, near_ref), (1 - core, far_ref)):
        pairs += [(ref.at[:, 0], w_ref.at[side, x]), (ref.at[:, 1], w_ref.at[side, 1 - x])]
    copies = launch(pairs, sem)
    valid = mask_of(info_ref, rows, 0)
    heads_ref[...] = o_ref[...]
    heads = o_ref[...].reshape(512, rows)
    gy = (cot_ref[...].astype(F32) * valid).astype(BF)
    acts_ref[:, ACT_GY] = gy
    settle(copies)
    gains = gains_of(small_ref)
    outs = [w_ref[side, :, :, 512:576, :].reshape(512, 256) for side in range(2)]
    h3 = h2_ref[...] + jnp.concatenate([contract(heads, outs[side], 0, 0) for side in range(2)], 1)
    normal, scale = normal_of(h3)
    acts_ref[:, ACT_N4] = (normal * gains[3:4]).astype(BF)
    y_ref[...] = h3
    dn_ref[...] = jnp.zeros_like(dn_ref)

    gy0, gy1 = acts_ref[:, 4608:4864], acts_ref[:, 4864:5120]

    def step(index, carry):
        upper = jnp.concatenate([upper_block(w_ref, 2 * index + i) for i in range(2)], 1)
        lower = []
        for side in range(2):
            blocks = [2 * index + i for i in range(2)]
            blocks = [w_ref[side, lax.div(k, 4), lax.rem(k, 4), 256:512, :] for k in blocks]
            lower.append(jnp.concatenate(blocks, 0))
        u = matmul(acts_ref[:, ACT_N4], upper)
        sigma = jax.nn.sigmoid(u)
        r = (u * sigma).astype(BF)
        acts_ref[:, block_cols(index, 512)] = r
        dr = contract(gy0, lower[0], 1, 1) + contract(gy1, lower[1], 1, 1)
        du = (dr * (sigma * (1.0 + u * (1.0 - sigma)))).astype(BF)
        acts_ref[:, block_cols(index + 4, 512)] = du
        y_ref[:, 0:256] += matmul(r, lower[0])
        y_ref[:, 256:512] += matmul(r, lower[1])
        dn_ref[...] += contract(du, upper, 1, 1)
        return carry

    lax.fori_loop(0, 4, step, 0)
    out_ref[...] = (y_ref[...] * valid).astype(BF)
    dn = dn_ref[...]
    gain_ref[...] = column_sum(dn * normal)
    g3 = gy.astype(F32) + back_of(dn, normal, scale, gains[3:4])
    g3_ref[...] = g3
    ga = g3.astype(BF)
    acts_ref[:, ACT_GA] = ga
    dob = contract(outs[0], ga[:, 0:256], 1, 1) + contract(outs[1], ga[:, 256:512], 1, 1)
    dob_ref[...] = dob.astype(BF).reshape(HEADS, HEAD, rows)


def pair_rows(value):
    split = value.reshape(8, 8, 8, 256)
    return jnp.concatenate([split[..., 0:128], split[..., 128:256]], 2)


FULL = slice(None)


def by_chip(out_ref, c, rows, value):
    out_ref[c % 2, :, :, c // 2, rows, :] = value.astype(BF).reshape((2, 4) + value.shape[1:])


def by_shard(out_ref, w, rows, value):
    value = value.astype(BF).reshape((4, 2) + value.shape[1:])
    for xh in range(2):
        out_ref[xh, w // 4, w % 4, :, rows, :] = value[:, xh]


def stack_rows(*pieces):
    return jnp.concatenate(pieces, 0)


def early_kernel(info_ref, acts_ref, heads_ref, acts2_ref, heads2_ref, out_ref):
    rows = acts_ref.shape[0]
    side = info_ref[0]

    def tokens(cols):
        return stack_rows(acts_ref[:, cols], acts2_ref[:, cols])

    n4 = tokens(ACT_N4).T
    for j in range(4):
        res = matmul(n4, tokens(block_cols(side * 4 + j + 8)))
        for i in range(2):
            by_chip(out_ref, 2 * j + i, slice(0, 64), res[:, 128 * i:128 * i + 128].reshape(8, 64, 128))
    gy = tokens(block_cols(side + 18)).T
    for w in range(8):
        res = matmul(gy, tokens(slice(256 * w, 256 * w + 256))).reshape(8, 32, 256)
        for i in range(2):
            by_shard(out_ref, w, slice(64 + 32 * i, 96 + 32 * i), res[:, :, 128 * i:128 * i + 128])
    heads = jnp.concatenate([heads_ref[...].reshape(512, rows), heads2_ref[...].reshape(512, rows)], 1)
    packed = pair_rows(matmul(heads, tokens(block_cols(side + 20))))
    for c in range(8):
        by_chip(out_ref, c, slice(128, 144), packed[:, c])


def attn_in_kernel(info_ref, d_ref, h2_in, g3_in, one_ref,
                   g2_ref, gs_ref, lo_ref, hi_ref, gain_ref, w_ref, small_ref, h2_ref, g3_ref, sem):
    rows = h2_ref.shape[0]
    copies = launch(
        [(h2_in, h2_ref), small_pair(one_ref, small_ref), (one_ref.at[:, :, 128:SMALL, :], w_ref),
         (g3_in, g3_ref)], sem
    )
    settle(copies[:1])
    normal, scale = normal_of(h2_ref[...])
    settle(copies[1:])
    gains = gains_of(small_ref)
    parts = [(part, side) for part in range(3) for side in range(2)]
    blocks = [
        d_ref[4 * side:4 * side + 4, 64 * part:64 * part + 64, :].reshape(256, rows) for part, side in parts
    ]
    weights = [queries_of(w_ref, side, part) for part, side in parts]
    dn = contract(stack_rows(*blocks).T, jnp.concatenate(weights, 1), 1, 1)
    gain_ref[...] = column_sum(dn * normal)
    g2 = g3_ref[...] + back_of(dn, normal, scale, gains[2:3])
    g2_ref[...] = g2
    gs = g2[:, 0:256]
    gs_ref[...] = gs.astype(BF)
    lo_ref[...] = gs[0:RIM].astype(BF)
    hi_ref[...] = gs[rows - RIM:rows].astype(BF)


def conv_back_kernel(info_ref, lo_ref, gs_ref, hi_ref, np_ref, mean_ref, scale_ref, nm_in, wp_in,
                     two_ref, one_ref, dw_ref, dnar_ref, table_ref, pt_ref, small_ref, nmf_ref,
                     dsp_ref, sc_ref, hat_ref, nm_ref, wp_ref, sem, sems):
    rim_rows = wp_ref.shape[0]
    rows = rim_rows - 2 * RIM
    main = slice(RIM, RIM + rows)
    copies = launch(
        [small_pair(one_ref, small_ref), (two_ref.at[1, :, :, 256:512, :], pt_ref)], sem
    )

    def arriving(which, index):
        source, target = ((nm_in, nm_ref), (wp_in, wp_ref))[which]
        cols = block_cols(index)
        return pltpu.make_async_copy(source.at[:, cols], target.at[:, cols], sems.at[which, index])

    for index in range(8):
        for which in range(2):
            arriving(which, index).start()
    valid = mask_of(info_ref, rim_rows, RIM)
    gs = jnp.concatenate(
        [lo_ref[...].astype(F32), gs_ref[...].astype(F32), hi_ref[...].astype(F32)], 0
    ).astype(BF)
    mean = mean_ref[:, 0:1]
    scale = scale_ref[:, 0:1]
    table_ref[...] = jnp.zeros_like(table_ref)
    dsp_ref[:, 0:RIM, :] = jnp.zeros((2, RIM, 128), F32)
    dsp_ref[:, RIM + rim_rows:, :] = jnp.zeros((2, RIM, 128), F32)
    settle(copies)

    def first_pass(index, carry):
        one, two = carry
        cols = block_cols(index)
        taps, gain = taps_of(small_ref, index)
        arriving(0, index).wait()
        arriving(1, index).wait()
        dsp = contract(gs, pt_ref[lax.div(index, 4), lax.rem(index, 4)], 1, 1).astype(BF).astype(F32)
        nm = nm_ref[:, cols].astype(F32)
        halves = []
        sums = []
        for half in range(2):
            lanes = slice(128 * half, 128 * half + 128)
            dsp_ref[half, RIM:RIM + rim_rows, :] = dsp[:, lanes]
            nmf_ref[half] = nm[:, lanes]
            inner = dsp[main, lanes]
            dn = jnp.zeros((rim_rows, 128), F32)
            parts = []
            for tap in range(9):
                dn = dn + dsp_ref[half, 12 - tap:12 - tap + rim_rows, :] * taps[tap:tap + 1, lanes]
                parts.append(column_sum(nmf_ref[half, 4 + tap:4 + tap + rows, :] * inner))
            halves.append(dn)
            sums.append(jnp.concatenate(parts, 0))
        table_ref[0:9, cols] = jnp.concatenate(sums, 1)
        dn = jnp.concatenate(halves, 1) * valid
        mixed = smooth_unit(wp_ref[:, cols]) + smooth_unit(np_ref[...]) * jnp.where(index == 0, 1.0, 0.0)
        hat = (mixed - mean) * scale
        hat_ref[:, cols] = hat
        table_ref[9:10, cols] = column_sum((dn * hat)[main])
        scaled = dn * gain
        sc_ref[:, cols] = scaled
        return (one + jnp.sum(scaled, -1, keepdims=True),
                two + jnp.sum(scaled * hat, -1, keepdims=True))

    zero = jnp.zeros((rim_rows, 1), F32)
    one, two = lax.fori_loop(0, 8, first_pass, (zero, zero))
    one = one * (1.0 / 2048)
    two = two * (1.0 / 2048)
    back = scale * (sc_ref[:, 0:256] - one - hat_ref[:, 0:256] * two)
    dnar_ref[...] = (back * smooth_slope(np_ref[...])).astype(BF)

    def second_pass(index, carry):
        cols = block_cols(index)
        back = scale[main] * (
            sc_ref[main, cols] - one[main] - hat_ref[main, cols] * two[main]
        )
        dw_ref[:, cols] = (back * smooth_slope(wp_ref[main, cols])).astype(BF)
        return carry

    lax.fori_loop(0, 8, second_pass, 0)


def glu_back_kernel(info_ref, dw_ref, dnar_ref, h1_in, two_ref, one_ref, g2_ref,
                    a_in, sg_in, x_in, table_ref, gattn_ref, gffn_ref, dx_ref, dab_ref, sums_ref,
                    w2_ref, w1_ref, small_ref, nar_ref, h1_ref, a_ref, sg_ref, x_ref, sem):
    rows = g2_ref.shape[0]
    first = launch([(h1_in, h1_ref)], sem)
    copies = launch(
        [(two_ref.at[0, :, :, 0:448, :], w2_ref.at[0]),
         (two_ref.at[1, :, :, 0:256, :], w2_ref.at[1, :, :, 0:256, :])], sem.at[1:3]
    )
    copies1 = launch(
        [small_pair(one_ref, small_ref), (one_ref.at[:, :, 0:128, :], w1_ref), (a_in, a_ref),
         (sg_in, sg_ref), (x_in, x_ref)], sem.at[3:8]
    )
    valid = mask_of(info_ref, rows, 0)
    nar_ref[...] = dnar_ref[...].astype(F32)
    settle(first)
    normal, scale1 = normal_of(h1_ref[...])
    moved = jnp.concatenate([nar_ref[9 - tap:9 - tap + rows, :].astype(BF) for tap in range(3)], 1)
    dn = jnp.zeros((rows, 512), F32)
    for side in range(2):
        copies[side].wait()
        weights = [w2_ref[side, :, :, 64 * j:64 * j + 64, :].reshape(512, 256) for j in range(4)]
        dn = dn + contract(dw_ref[:, 1024 * side:1024 * side + 1024], jnp.concatenate(weights, 1), 1, 1)
        if side == 0:
            weights = jnp.concatenate([narrow_block(w2_ref, tap) for tap in range(3)], 1)
            dn = dn + contract(moved, weights, 1, 1)
    settle(copies1)
    gains = gains_of(small_ref)
    dn = dn * valid
    gconv = column_sum(dn * normal)
    g1 = g2_ref[...] + back_of(dn, normal, scale1, gains[1:2])
    sg = sg_ref[...].astype(F32)
    da = (g1 * sg).astype(BF)
    db = (g1 * a_ref[...].astype(F32) * sg * (1.0 - sg)).astype(BF)
    dab_ref[:, 0:512] = da
    dab_ref[:, 512:1024] = db
    sums_ref[0:16, :] = table_ref[...]
    sums_ref[16:24, :] = jnp.zeros((8, 2048), F32)
    sums_ref[17:18, 0:512] = gconv
    sums_ref[18:19, 0:512] = gattn_ref[...]
    sums_ref[19:20, 0:512] = gffn_ref[...]
    dn = contract(da, glu_of(w1_ref, 0), 1, 1) + contract(db, glu_of(w1_ref, 1), 1, 1)
    normal, scale0 = normal_of(x_ref[...].astype(F32))
    sums_ref[16:17, 0:512] = column_sum(dn * normal)
    dx_ref[...] = g1 + back_of(dn, normal, scale0, gains[0:1])


def middle_kernel(info_ref, sp_ref, gs_ref, n3_ref, d_ref, sp2_ref, gs2_ref, n32_ref, d2_ref, out_ref):
    rows = gs_ref.shape[0]
    side = info_ref[0]
    gs = stack_rows(gs_ref[:, block_cols(side, 128)], gs2_ref[:, block_cols(side, 128)]).T
    for w in range(8):
        cols = slice(256 * w, 256 * w + 256)
        res = matmul(gs, stack_rows(sp_ref[:, cols], sp2_ref[:, cols])).reshape(8, 16, 256)
        for i in range(2):
            by_shard(out_ref, w, slice(16 * i, 16 * i + 16), res[:, :, 128 * i:128 * i + 128])
    n3 = stack_rows(n3_ref[...], n32_ref[...]).T
    for part in range(3):
        d = [ref[pl.ds(side * 4, 4), 64 * part:64 * part + 64, :].reshape(256, rows) for ref in (d_ref, d2_ref)]
        packed = pair_rows(contract(n3, jnp.concatenate(d, 1), 1, 1))
        for c in range(8):
            by_chip(out_ref, c, slice(32 + 16 * part, 48 + 16 * part), packed[:, c])


def late_kernel(info_ref, n2_ref, dw_ref, dnar_ref, n1_ref, dab_ref, small_ref, n22_ref, dw2_ref,
                dnar2_ref, n12_ref, dab2_ref, small2_ref, out_ref, n2f_ref, narf_ref):
    rows = dw_ref.shape[0]
    side = info_ref[0]
    shifted = []
    dnar = []
    for n_ref, d_ref in ((n2_ref, dnar_ref), (n22_ref, dnar2_ref)):
        n2f_ref[...] = n_ref[...].astype(F32)
        narf_ref[...] = d_ref[...].astype(F32)
        shifted.append([n2f_ref[7 + tap:7 + tap + rows, :].astype(BF) for tap in range(3)])
        dnar.append(narf_ref[RIM:RIM + rows, block_cols(side, 128)].astype(BF))
    shifted = [stack_rows(*pair).T for pair in zip(*shifted)]
    dnar = stack_rows(*dnar)
    for j in range(4):
        cols = block_cols(side * 4 + j)
        res = matmul(shifted[1], stack_rows(dw_ref[:, cols], dw2_ref[:, cols]))
        for i in range(2):
            part = res[:, 128 * i:128 * i + 128].reshape(8, 64, 128)
            out_ref[2 * j + i, :, 0:64, :] = part.astype(BF)
    narrow = [matmul(piece, dnar) for piece in shifted]
    for w in range(8):
        lanes = pl.ds(pl.multiple_of(w * 256 + side * 128, 128), 128)
        pair = slice(128 * (w // 2), 128 * (w // 2) + 128)
        table = small_ref[0:16, lanes] + small2_ref[0:16, lanes]
        gains = small_ref[16:20, pair] + small2_ref[16:20, pair]
        table = jnp.concatenate([table[0:10], gains, table[14:16]], 0)
        for c in range(8):
            pieces = [n[64 * w + 8 * c:64 * w + 8 * c + 8] for n in narrow]
            pieces += [table[2 * c:2 * c + 2], jnp.zeros((6, 128), F32)]
            out_ref[c, w, 64:96, :] = jnp.concatenate(pieces, 0).astype(BF)
    n1 = stack_rows(n1_ref[...], n12_ref[...]).T
    for place in range(2):
        cols = block_cols(side + 2 * place)
        packed = pair_rows(matmul(n1, stack_rows(dab_ref[:, cols], dab2_ref[:, cols]))).astype(BF)
        for w in range(8):
            out_ref[:, w, 96 + 16 * place:112 + 16 * place, :] = packed[w]


def unpack_kernel(info_ref, near_ref, far_ref, gglu_ref, val_ref, gat_ref, gconv_ref, wid_ref, nar_ref,
                  gmid_ref, dep_ref, pnt_ref, gatt_ref, qry_ref, key_ref, vls_ref, outp_ref,
                  gffn_ref, upper_ref, lower_ref, fin_ref, low_ref, pt_ref, table_ref, sem):
    settle(fetch(info_ref[0], near_ref, far_ref, fin_ref, sem))
    for c in range(8):
        for k in range(2):
            fin = fin_ref[k, c].astype(F32)
            lanes = slice(k * 1024 + c * 128, k * 1024 + c * 128 + 128)
            upper_ref[:, lanes] = fin[0:64]
            wid_ref[:, lanes] = fin[EARLY + MIDDLE:EARLY + MIDDLE + 64]
            middle = EARLY
            late = EARLY + MIDDLE
            for i in range(2):
                low_ref[k * 256 + c * 32:k * 256 + c * 32 + 32, 128 * i:128 * i + 128] = (
                    fin[64 + 32 * i:96 + 32 * i]
                )
                pt_ref[k * 128 + c * 16:k * 128 + c * 16 + 16, 128 * i:128 * i + 128] = (
                    fin[middle + 16 * i:middle + 16 * i + 16]
                )
            for tap in range(3):
                nar_ref[tap, 8 * c:8 * c + 8, 128 * k:128 * k + 128] = (
                    fin[late + 64 + 8 * tap:late + 72 + 8 * tap]
                )
            table_ref[2 * c:2 * c + 2, 128 * k:128 * k + 128] = fin[late + 88:late + 90]
            bases = [128] + [middle + 32 + 16 * i for i in range(3)] + [late + 96, late + 112]
            targets = [outp_ref, qry_ref, key_ref, vls_ref, val_ref, gat_ref]
            for base, target in zip(bases, targets):
                for i in range(2):
                    target[8 * c:8 * c + 8, k * 256 + 128 * i:k * 256 + 128 * i + 128] = (
                        fin[base + 8 * i:base + 8 * i + 8]
                    )
    lower_ref[...] = low_ref[...].T
    pnt_ref[...] = pt_ref[...].T
    dep_ref[...] = table_ref[0:9, :]
    gmid_ref[...] = table_ref[9:10, :]
    even = info_ref[3] == 0
    gains = jnp.where(even, table_ref[10:14, 0:64], table_ref[10:14, 64:128])
    gglu_ref[...] = gains[0:1]
    gconv_ref[...] = gains[1:2]
    gatt_ref[...] = gains[2:3]
    gffn_ref[...] = gains[3:4]


def pack_ring_kernel(info_ref, wide_ref, narrow_ref, point_ref, out_ref, sem):
    core = info_ref[0]
    pairs = [
        (wide_ref.at[:, block_cols(core * 4 + j)], out_ref.at[64 * j:64 * j + 64, :]) for j in range(4)
    ]
    copies = launch(pairs, sem)

    @pl.when(core == 0)
    def _():
        settle(launch([(narrow_ref, out_ref.at[256:448, :]),
                       (narrow_ref.at[0:64, :], out_ref.at[448:512, :])], sem.at[4:6]))

    @pl.when(core == 1)
    def _():
        settle(launch([(point_ref, out_ref.at[256:512, :])], sem.at[4:5]))

    settle(copies)


def pack_rest_kernel(info_ref, value_ref, gate_ref, query_ref, key_ref, values_ref, g0_ref, g1_ref,
                     g2_ref, g3_ref, depth_ref, mid_ref, in_ref, out_ref, outw_ref, one_ref,
                     three_ref, pack_ref, g0, g1, g2, g3, depth, mid, sem):
    core = info_ref[0]
    own = block_cols(core)
    small = [(g0_ref, g0), (g1_ref, g1), (g2_ref, g2), (g3_ref, g3), (depth_ref, depth), (mid_ref, mid)]
    small = launch(small, sem)
    weights = launch(
        [(ref.at[:, own], pack_ref.at[128 + 64 * i:192 + 64 * i, :])
         for i, ref in enumerate((query_ref, key_ref, values_ref))], sem.at[6:9],
    )
    later = [(in_ref.at[:, block_cols(core * 4 + j)], three_ref.at[64 * j:64 * j + 64, :]) for j in range(4)]
    later += [(out_ref.at[:, own], three_ref.at[256:512, :]), (outw_ref.at[:, own], three_ref.at[512:576, :])]
    later = launch(later, sem.at[9:15])
    for index, ref in ((0, value_ref), (1, gate_ref)):
        @pl.when(core == index)
        def _():
            settle(launch([(ref.at[:, 256 * i:256 * i + 256], pack_ref.at[64 * i:64 * i + 64, :])
                           for i in range(2)], sem.at[15:17]))
    settle(small)
    gains = jnp.concatenate(
        [ref[...].astype(F32) for ref in (g0, g1, g2, g3)] + [jnp.zeros((4, 64), F32)], 0
    )
    gains = jnp.concatenate([gains] * 8, 1)
    place = lax.broadcasted_iota(jnp.int32, (8, 512), 1)
    start = (info_ref[5] * 4 + info_ref[4]) * 64
    gains = jnp.where((place >= start) & (place < start + 64), gains, 0.0)
    gains = jnp.concatenate([gains[:, 0:256], gains[:, 256:512]], 0)
    pack_ref[SMALL:SMALL + 16, :] = gains.astype(BF)
    taps = jnp.concatenate([depth[...].astype(F32), mid[...].astype(F32), jnp.zeros((6, 256), F32)], 0)
    pack_ref[SMALL + 16:SMALL + 32, :] = taps.astype(BF)
    settle(weights)
    for w in range(8):
        one_ref[w] = pack_ref[...]
    settle(later)


def fold_kernel(*refs):
    total = refs[0][...].astype(F32)
    for ref in refs[1:4]:
        total = total + ref[...].astype(F32)
    refs[4][...] = total.astype(BF)


def over_x(value):
    value = value.reshape((4,) + value.shape[2:])
    return lax.psum_scatter(value, ("xh", "xl"), scatter_dimension=0, tiled=True)[0]


def over_z(value):
    return lax.psum_scatter(value, "z", scatter_dimension=0, tiled=True)[0]


def spread_out(own, axes, count):
    copies = jnp.broadcast_to(own[None], (count,) + own.shape)
    return lax.all_to_all(copies, axes, 0, 0, tiled=True)


def shards(
    inputs, lengths, cotangent, glu_gain, glu_value, glu_gate, conv_gain, wide_weight,
    narrow_weight, mid_gain, depth_weight, point_weight, attn_gain, query_weight, key_weight,
    value_weight, output_weight, ffn_gain, ffn_in, ffn_out,
):
    rows, width = inputs.shape[1], inputs.shape[2]
    units = wide_weight.shape[1]
    rim_rows = rows + 2 * RIM
    core = lax.axis_index("core")
    shard = lax.axis_index("xl") * 4 + lax.axis_index("z")
    first = (lax.axis_index("y") * 4 + lax.axis_index("xh") * 2 + core) * rows
    xl, z = lax.axis_index("xl"), lax.axis_index("z")
    info = jnp.stack([core, first, lengths[0], shard % 2, z, xl]).astype(jnp.int32)
    flip = shift(dc=1)
    dma = pltpu.SemaphoreType.DMA

    pack2 = call(
        pack_ring_kernel, [((512, 256), BF, FREE)], [SMEM] + [HBM] * 3, [dma((6,))], "pack_ring", 1,
        info, wide_weight, narrow_weight.reshape(192, 256), point_weight,
    )[0]
    steps = [shift(dz=-1), shift(dz=2), shift(dz=1)]
    other = send(pack2, shift(dxl=1))
    own_pieces = [send(pack2, step) for step in steps]
    other_pieces = [send(other, step) for step in steps]

    line = lambda v: v.reshape(1, -1)
    pack1, pack3 = call(
        pack_rest_kernel, [((8, SMALL + 32, 256), BF, FREE), ((576, 256), BF, FREE)], [SMEM] + [HBM] * 14,
        [pltpu.VMEM((SMALL + 32, 256), BF)] + [pltpu.VMEM((1, 64), BF)] * 4
        + [pltpu.VMEM((9, 256), BF), pltpu.VMEM((1, 256), BF), dma((17,))],
        "pack_rest", 1, info, glu_value, glu_gate, query_weight, key_weight, value_weight,
        line(glu_gain), line(conv_gain), line(attn_gain), line(ffn_gain), depth_weight,
        line(mid_gain), ffn_in, ffn_out, output_weight,
    )

    pack1, *_ = lax.optimization_barrier((pack1, *own_pieces, other))
    near1 = lax.all_to_all(pack1, WT, 0, 0, tiled=True)
    x = inputs[0]
    low_x = send(x[rows - RIM:], along(1))
    high_x = send(x[:RIM], along(-1))
    other3 = send(pack3, shift(dxl=1))
    near1, pack3, other3, low_x, high_x, *ready = lax.optimization_barrier(
        (near1, pack3, other3, low_x, high_x, *own_pieces, *other_pieces)
    )
    near2 = [pack2] + ready[:3] + [other] + ready[3:]
    far2 = [send(piece, flip) for piece in near2]
    far1 = send(near1, flip)
    near3 = lax.all_gather(jnp.stack([pack3, other3]), "z", axis=0)

    tall, wide, narrow = (rows, width), (rows, units), (rows, 256)
    tiny = pltpu.VMEM((8, 32, 256), BF)
    ring = pltpu.VMEM((2, 2, 4) + pack2.shape, BF)
    n1, a, sg, h1, h1m = call(
        glu_kernel,
        [(tall, BF), (tall, BF), (tall, BF), ((rim_rows, width), F32, FREE), (tall, F32)],
        [SMEM] + [FREE] * 3 + [ANY] * 2, [pltpu.VMEM((2, 8, 128, 256), BF), tiny, dma((3,))], "glu", 3,
        info, low_x, x, high_x, near1, far1,
    )
    n2, wp, np_, nm, mean, scale, sp, h2, n3, qkv, two, one = call(
        conv_kernel,
        [((rim_rows, width), BF), ((rim_rows, units), F32, HBM), ((rim_rows, 256), F32),
         ((rim_rows, units), BF, HBM), ((rim_rows, 128), F32), ((rim_rows, 128), F32),
         (wide, BF, HBM), (tall, F32), (tall, BF), ((HEADS, 3 * HEAD, rows), BF, FREE),
         (ring.shape, BF, HBM), ((2,) + near1.shape, BF, HBM)],
        [SMEM, FREE] + [ANY] * 18,
        [ring, pltpu.VMEM((2,) + near1.shape, BF), pltpu.VMEM((rim_rows, units), F32),
         pltpu.VMEM((rim_rows, units), F32), pltpu.VMEM((rim_rows, units), BF), pltpu.VMEM(wide, BF),
         pltpu.VMEM((2, rim_rows, 128), F32), dma((16,)), dma((2,)), dma((3, 8))],
        "conv", 15, info, h1, *near2, *far2, near1, far1,
    )
    near = lax.all_to_all(qkv, CHIPS, 0, 0, tiled=True)
    far = send(near[:, HEAD:], flip)
    head_out, expo, inverse, near, far = attend(near, far, lengths, info[:1])
    near3, _ = lax.optimization_barrier((near3, head_out))
    far3 = send(near3, flip)
    heads_in = lax.all_to_all(head_out, CHIPS, 0, 0, tiled=True)
    output, acts, g3, dob, d_gffn, heads_in = call(
        ffn_kernel,
        [(tall, BF), ((rows, 5632), BF, FREE), (tall, F32), ((HEADS, HEAD, rows), BF),
         ((1, width), F32), ((HEADS, HEAD, rows), BF, FREE)],
        [SMEM, VMEM, FREE, VMEM, HBM, HBM, ANY],
        [pltpu.VMEM((2, 2, 4) + pack3.shape, BF), tiny, pltpu.VMEM(tall, F32), pltpu.VMEM(tall, F32),
         dma((5,))],
        "ffn", 11, info, h2, heads_in, cotangent[0], one, near3, far3,
    )

    d_near = lax.all_to_all(dob, CHIPS, 0, 0, tiled=True)
    early = call(
        early_kernel, [((2, 2, 4, 4, EARLY, 128), BF)], [SMEM] + [FREE] * 4, [], "early", 0.3,
        info, acts, heads_in, send(acts, flip), send(heads_in, flip),
    )[0]
    d_near, early = lax.optimization_barrier((d_near, early))
    early = over_x(early)
    dq, dk, dv = attend_back(near, far, expo, head_out, inverse, d_near)
    d_far = send(jnp.concatenate([dk[1], dv[1]], 1), flip).astype(F32)
    d_own = jnp.concatenate([dk[0], dv[0]], 1).astype(F32)
    d_qkv = jnp.concatenate([dq, (d_own + d_far).astype(BF)], 1)
    d_qkv = lax.all_to_all(d_qkv, CHIPS, 0, 0, tiled=True)
    early = over_z(early)
    g2, gs, lo, hi, d_gatt = call(
        attn_in_kernel,
        [(tall, F32), (narrow, BF, FREE), ((RIM, 256), BF), ((RIM, 256), BF), ((1, width), F32)],
        [SMEM, FREE] + [HBM] * 3,
        [pltpu.VMEM((2, 8, SMALL - 128, 256), BF), tiny, pltpu.VMEM(tall, F32), pltpu.VMEM(tall, F32),
         dma((4,))],
        "attn_in", 0.5, info, d_qkv, h2, g3, one,
    )
    low_gs = send(hi, along(1))
    high_gs = send(lo, along(-1))
    info_mid, _, _ = lax.optimization_barrier((info, low_gs, high_gs))
    middle = call(
        middle_kernel, [((2, 2, 4, 4, MIDDLE, 128), BF)], [SMEM, VMEM, FREE, VMEM, FREE] + [FREE] * 4, [], "middle", 0.3,
        info_mid, sp, gs, n3, d_qkv, *[send(v, flip) for v in (sp, gs, n3, d_qkv)],
    )[0]
    info_conv, middle = lax.optimization_barrier((info, middle))
    middle = over_x(middle)
    rim_narrow = ((rim_rows, 256), BF)
    dw, dnar, table = call(
        conv_back_kernel, [(wide, BF, FREE), ((rim_rows, 256), BF, FREE), ((16, units), F32, FREE)],
        [SMEM, FREE, FREE, FREE] + [VMEM] * 3 + [HBM] * 4,
        [pltpu.VMEM((2, 4, 256, 256), BF), tiny, pltpu.VMEM((2, rim_rows, 128), F32),
         pltpu.VMEM((2, rim_rows + 2 * RIM, 128), F32), pltpu.VMEM((rim_rows, units), F32),
         pltpu.VMEM((rim_rows, units), F32), pltpu.VMEM((rim_rows, units), BF),
         pltpu.VMEM((rim_rows, units), F32), dma((2,)), dma((2, 8))],
        "conv_back", 2, info_conv, low_gs, gs, high_gs, np_, mean, scale, nm, wp, two, one,
    )
    dw2, dnar2 = send(dw, flip), send(dnar, flip)
    info_glu, early = lax.optimization_barrier((info, early))
    dx, dab, sums = call(
        glu_back_kernel,
        [(tall, F32), ((rows, 2 * width), BF, FREE), ((24, units), F32, FREE)],
        [SMEM, FREE, FREE, HBM, HBM, HBM, VMEM, HBM, HBM, HBM, FREE, VMEM, VMEM],
        [pltpu.VMEM((2, 2, 4, 448, 256), BF), pltpu.VMEM((2, 8, 128, 256), BF), tiny,
         pltpu.VMEM((rim_rows, 256), F32), pltpu.VMEM(tall, F32), pltpu.VMEM(tall, BF),
         pltpu.VMEM(tall, BF), pltpu.VMEM(tall, BF), dma((8,))],
        "glu_back", 1, info_glu, dw, dnar, h1m, two, one, g2, a, sg, x, table, d_gatt, d_gffn,
    )
    dab2, sums2 = send(dab, flip), send(sums, flip)
    info_late, middle = lax.optimization_barrier((info, middle))
    middle = over_z(middle)
    late = call(
        late_kernel, [((8, 8, LATE, 128), BF)], [SMEM, VMEM, FREE, FREE, VMEM, FREE, FREE] + [FREE] * 6,
        [pltpu.VMEM((rim_rows, width), F32), pltpu.VMEM((rim_rows, 256), F32)], "late", 40,
        info_late, n2, dw, dnar, n1, dab, sums, send(n2, flip), dw2, dnar2, send(n1, flip), dab2, sums2,
    )[0]
    _, early, middle = lax.optimization_barrier((late, early, middle))
    y = lax.axis_index("y")
    pieces = jnp.concatenate([early, middle], 1)
    pick = lambda index: lax.dynamic_index_in_dim(pieces, index % 4, 0, keepdims=False)
    parts = [send(pick(y + d), shift(dy=d)) for d in (1, 2, 3)]
    early = call(
        fold_kernel, [((EARLY + MIDDLE, 128), BF, FREE)], [FREE] * 4, [], "fold", FOLD, pick(y), *parts
    )[0]
    late = lax.all_to_all(late.reshape(64, LATE, 128), CHIPS + WT, 0, 0, tiled=True)
    late = jnp.sum(late.astype(F32), 0).astype(BF)
    final = spread_out(jnp.concatenate([early, late], 0), CHIPS, 8)
    square, broad = ((64, 512), F32), ((64, 2048), F32)
    line = ((1, 64), F32)
    grads = call(
        unpack_kernel,
        [line, square, square, line, broad, ((3, 64, 256), F32), ((1, 256), F32),
         ((9, 256), F32), ((256, 256), F32), line, square, square, square, square, line, broad,
         ((256, 512), F32)],
        [SMEM, ANY, ANY],
        [pltpu.VMEM((2,) + final.shape, BF), pltpu.VMEM((512, 256), F32),
         pltpu.VMEM((256, 256), F32), pltpu.VMEM((16, 256), F32), dma((2,))],
        "unpack", 3, info, final, send(final, flip),
    )
    grads = [g[0] if g.shape[0] == 1 else g for g in grads]
    return (output[None], dx[None]) + tuple(grads)


def solution(mesh):
    fine = Mesh(mesh.devices.reshape(SIZES), AXES)
    flat, row, mid = P(WT), P(WT, None), P(None, WT, None)
    col = P(None, WT)
    tokens = P(WT, CTX, None)
    weights = (
        flat, row, row, flat, row, mid, flat, col, row, flat, row, row, row, row, flat, row, row,
    )
    return jax.shard_map(
        shards, mesh=fine, in_specs=(tokens, flat, tokens) + weights,
        out_specs=(tokens, tokens) + weights, check_vma=False,
    )
```

```python
import functools

import jax
import jax.numpy as jnp
import numpy as np
from jax import lax
from jax.experimental import pallas as pl
from jax.experimental.pallas import tpu as pltpu
from jax.sharding import Mesh
from jax.sharding import PartitionSpec as P

HEADS = 8
HEAD = 64
EPSILON = 1e-06
AXES = ("y", "xh", "core", "xl", "z")
SIZES = (4, 2, 2, 2, 4)
CTX = ("y", "xh", "core")
CHIPS = ("y", "xh")
WT = ("xl", "z")
BLOCK = 1024
LOG2E = 1.4426950408889634
BF = jnp.bfloat16
F32 = jnp.float32


def moves(target):
    pairs = []
    for source in range(int(np.prod(SIZES))):
        place = [int(v) for v in np.unravel_index(source, SIZES)]
        goal = target(*place)
        if goal is not None:
            pairs.append((source, int(np.ravel_multi_index(tuple(goal), SIZES))))
    return pairs


def shift(dy=0, dxh=0, dc=0, dxl=0, dz=0):
    return moves(
        lambda y, xh, c, xl, z: (
            (y + dy) % 4, (xh + dxh) % 2, (c + dc) % 2, (xl + dxl) % 2, (z + dz) % 4,
        )
    )


def along(step):
    def target(y, xh, c, xl, z):
        place = y * 4 + xh * 2 + c + step
        if place < 0 or place > 15:
            return None
        return (place // 4, place // 2 % 2, place % 2, xl, z)
    return moves(target)


def send(value, pairs):
    return lax.ppermute(value, AXES, pairs)


def matmul(left, right):
    return jnp.dot(left, right, preferred_element_type=F32)


def contract(left, right, ldim, rdim):
    return lax.dot_general(
        left, right, (((ldim,), (rdim,)), ((), ())), preferred_element_type=F32
    )


def smooth_unit(value):
    return value * jax.nn.sigmoid(value)


def smooth_slope(value):
    sigma = jax.nn.sigmoid(value)
    return sigma * (1.0 + value * (1.0 - sigma))


VMEM = pl.BlockSpec(memory_space=pltpu.VMEM)
SMEM = pl.BlockSpec(memory_space=pltpu.SMEM)
HBM = pl.BlockSpec(memory_space=pltpu.HBM)
ANY = pl.BlockSpec(memory_space=pl.ANY)
FREE = "free"


def attend_kernel(chips, rows, length_ref, core_ref, near_ref, far_ref, o_ref, e_ref, l_ref,
                  near_out, far_out, keys_ref, values_ref, sem):
    step = pl.program_id(0)
    span = chips * rows
    aug = 2 * HEAD
    pairs = [(near_ref, near_out), (far_ref, far_out)]

    @pl.when(step == chips - 1)
    def _():
        for i, (source, target) in enumerate(pairs):
            pltpu.make_async_copy(source, target, sem.at[i]).wait()

    @pl.when(step == 0)
    def _():
        launch(pairs, sem)
        length = length_ref[0]
        core = core_ref[0]
        ones = jnp.ones((16, rows), F32)
        for side in range(2):
            source = near_ref if side == 0 else far_ref
            base = HEAD if side == 0 else 0
            owner = core if side == 0 else 1 - core
            for chip in range(chips):
                cols = slice(side * span + chip * rows, side * span + (chip + 1) * rows)
                key = source[chip, base:base + HEAD, :]
                keys_ref[0:HEAD, cols] = key
                keys_ref[HEAD:aug, cols] = key
                place = (chip * 2 + owner) * rows + lax.broadcasted_iota(jnp.int32, (16, rows), 1)
                row = lax.broadcasted_iota(jnp.int32, (16, rows), 0)
                bias = jnp.where((place < length) | (row > 0), 0.0, -1e30)
                keys_ref[aug:aug + 16, cols] = bias.astype(BF)
                value = source[chip, base + HEAD:base + 2 * HEAD, :].astype(F32)
                stacked = jnp.concatenate([value, ones, jnp.zeros((48, rows), F32)], 0)
                values_ref[cols, :] = stacked.T.astype(BF)

    query = near_ref[step, 0:HEAD, :].astype(F32) * (LOG2E * HEAD ** -0.5)
    high = query.astype(BF)
    low = (query - high.astype(F32)).astype(BF)
    query = jnp.concatenate([high, low, jnp.ones((16, rows), BF)], 0)
    scores = contract(query, keys_ref[...], 0, 0)
    top = jnp.max(scores, 1, keepdims=True)
    expo = jnp.exp2(scores - top).astype(BF)
    e_ref[...] = expo
    out = matmul(expo, values_ref[...]).T
    inverse = 1.0 / out[HEAD:HEAD + 8]
    o_ref[0] = (out[0:HEAD] * inverse[0:1]).astype(BF)
    l_ref[0] = inverse


def attend(near, far, length, core):
    chips, _, rows = near.shape
    tokens = 2 * chips * rows
    return pl.pallas_call(
        functools.partial(attend_kernel, chips, rows),
        grid=(chips,),
        in_specs=[
            pl.BlockSpec(memory_space=pltpu.SMEM),
            pl.BlockSpec(memory_space=pltpu.SMEM),
            pl.BlockSpec(near.shape, lambda i: (0, 0, 0)),
            pl.BlockSpec(far.shape, lambda i: (0, 0, 0)),
        ],
        out_specs=[
            pl.BlockSpec((1, HEAD, rows), lambda i: (i, 0, 0)),
            pl.BlockSpec((rows, tokens), lambda i: (i, 0)),
            pl.BlockSpec((1, 8, rows), lambda i: (i, 0, 0)),
            HBM,
            HBM,
        ],
        out_shape=[
            pltpu.HBM((chips, HEAD, rows), BF),
            pltpu.HBM((chips * rows, tokens), BF),
            pltpu.HBM((chips, 8, rows), F32),
            pltpu.HBM(near.shape, BF),
            pltpu.HBM(far.shape, BF),
        ],
        scratch_shapes=[
            pltpu.VMEM((2 * HEAD + 16, tokens), BF),
            pltpu.VMEM((tokens, 2 * HEAD), BF),
            pltpu.SemaphoreType.DMA((2,)),
        ],
        compiler_params=pltpu.CompilerParams(vmem_limit_bytes=32 * 2**20),
        cost_estimate=cost(14),
        name="attend",
    )(length, core, near, far)


def attend_back_kernel(chips, rows, near_ref, far_ref, e_ref, o_ref, l_ref, do_ref,
                       keep_ref, give_ref, keys_ref, values_ref, dk_acc, dv_acc):
    step = pl.program_id(0)
    span = chips * rows

    @pl.when(step == 0)
    def _():
        row = lax.broadcasted_iota(jnp.int32, (16, rows), 0)
        ones = jnp.where(row < 3, 1.0, 0.0).astype(BF)
        for side in range(2):
            source = near_ref if side == 0 else far_ref
            base = HEAD if side == 0 else 0
            for chip in range(chips):
                cols = slice(side * span + chip * rows, side * span + (chip + 1) * rows)
                key = source[chip, base:base + HEAD, :].astype(F32)
                stacked = jnp.concatenate([key, jnp.zeros((HEAD, rows), F32)], 0)
                keys_ref[cols, :] = stacked.T.astype(BF)
                values_ref[0:HEAD, cols] = source[chip, base + HEAD:base + 2 * HEAD, :]
                values_ref[HEAD:HEAD + 16, cols] = ones
        dk_acc[...] = jnp.zeros_like(dk_acc)
        dv_acc[...] = jnp.zeros_like(dv_acc)

    inverse = l_ref[0, 0:1, :]
    grad = do_ref[0].astype(F32) * inverse
    total = -jnp.sum(grad * o_ref[0].astype(F32), 0, keepdims=True)
    high = total.astype(BF).astype(F32)
    mid = (total - high).astype(BF).astype(F32)
    low = total - high - mid
    grad_low = grad.astype(BF)
    row = lax.broadcasted_iota(jnp.int32, (16, rows), 0)
    extra = jnp.where(row == 0, high, jnp.where(row == 1, mid, jnp.where(row == 2, low, 0.0)))
    grads = jnp.concatenate([grad_low, extra.astype(BF)], 0)
    query = near_ref[step, 0:HEAD, :]
    grads = grads.T
    block = BLOCK
    dq = jnp.zeros((rows, 2 * HEAD), F32)
    for start in range(0, 2 * span, block):
        cols = slice(start, start + block)
        expo = e_ref[:, cols]
        d_scores = (expo.astype(F32) * matmul(grads, values_ref[:, cols])).astype(BF)
        dq = dq + matmul(d_scores, keys_ref[cols, :])
        dk_acc[:, cols] += matmul(query, d_scores)
        dv_acc[:, cols] += matmul(grad_low, expo)
    keep_ref[step, 0:HEAD, :] = (dq.T[0:HEAD] * HEAD ** -0.5).astype(BF)

    @pl.when(step == chips - 1)
    def _():
        for side in range(2):
            for chip in range(chips):
                cols = slice(side * span + chip * rows, side * span + (chip + 1) * rows)
                out_ref, base = (keep_ref, HEAD) if side == 0 else (give_ref, 0)
                out_ref[chip, base:base + HEAD, :] = (dk_acc[:, cols] * HEAD ** -0.5).astype(BF)
                out_ref[chip, base + HEAD:base + 2 * HEAD, :] = dv_acc[:, cols].astype(BF)


def attend_back(near, far, expo, out, inverse, d_out):
    chips, _, rows = near.shape
    tokens = 2 * chips * rows
    whole = lambda i: (0, 0, 0)
    one = lambda i: (i, 0, 0)
    return pl.pallas_call(
        functools.partial(attend_back_kernel, chips, rows),
        grid=(chips,),
        in_specs=[
            pl.BlockSpec(near.shape, whole),
            pl.BlockSpec(far.shape, whole),
            pl.BlockSpec((rows, tokens), lambda i: (i, 0)),
            pl.BlockSpec((1, HEAD, rows), one),
            pl.BlockSpec((1, 8, rows), one),
            pl.BlockSpec((1, HEAD, rows), one),
        ],
        out_specs=[pl.BlockSpec((chips, 3 * HEAD, rows), whole), pl.BlockSpec((chips, 2 * HEAD, rows), whole)],
        out_shape=[
            jax.ShapeDtypeStruct((chips, 3 * HEAD, rows), BF),
            jax.ShapeDtypeStruct((chips, 2 * HEAD, rows), BF),
        ],
        scratch_shapes=[
            pltpu.VMEM((tokens, 2 * HEAD), BF),
            pltpu.VMEM((HEAD + 16, tokens), BF),
            pltpu.VMEM((HEAD, tokens), F32),
            pltpu.VMEM((HEAD, tokens), F32),
        ],
        compiler_params=pltpu.CompilerParams(vmem_limit_bytes=32 * 2**20),
        cost_estimate=cost(3),
        name="attend_back",
    )(in_hbm(near), in_hbm(far), in_hbm(expo), in_hbm(out), in_hbm(inverse), d_out)


RIM = 8
FOLD = 0.3
ACT_N4 = slice(4096, 4608)
ACT_GY = slice(4608, 5120)
ACT_GA = slice(5120, 5632)
EARLY = 144
SMALL = 320
MIDDLE = 80
LATE = 128


def call(kernel, outs, specs, scratch, name, micros, *args):
    args = [arg if spec in (SMEM, FREE, ANY) else in_hbm(arg) for arg, spec in zip(args, specs)]
    kinds = [out[2] if len(out) > 2 else VMEM for out in outs]
    return pl.pallas_call(
        kernel,
        in_specs=[VMEM if spec is FREE else spec for spec in specs],
        out_specs=[VMEM if kind is FREE else kind for kind in kinds],
        out_shape=[
            (jax.ShapeDtypeStruct if kind is FREE else pltpu.HBM)(out[0], out[1])
            for kind, out in zip(kinds, outs)
        ],
        scratch_shapes=scratch,
        compiler_params=pltpu.CompilerParams(vmem_limit_bytes=32 * 2**20),
        cost_estimate=cost(micros),
        name=name,
    )(*args)


def in_hbm(value):
    return pltpu.with_memory_space_constraint(value, pltpu.HBM)


def cost(micros):
    return pl.CostEstimate(
        flops=int(micros * 1.0e9), bytes_accessed=int(micros * 3.0e6), transcendentals=0
    )


def launch(pairs, sems):
    copies = [
        pltpu.make_async_copy(source, target, sems.at[i]) for i, (source, target) in enumerate(pairs)
    ]
    for copy in copies:
        copy.start()
    return copies


def fetch(core, near_ref, far_ref, both_ref, sems):
    return launch([(near_ref, both_ref.at[core]), (far_ref, both_ref.at[1 - core])], sems)


def settle(copies):
    for copy in copies:
        copy.wait()


def gains_of(small_ref):
    total = small_ref[0, 0:16, :].astype(F32)
    for w in range(1, 8):
        total = total + small_ref[w, 0:16, :].astype(F32)
    return jnp.concatenate([total[0:8], total[8:16]], 1)


def taps_of(small_ref, index):
    small = small_ref[index, 16:32, :].astype(F32)
    return small[0:9], small[9:10]


def normal_of(value):
    average = jnp.mean(value, -1, keepdims=True)
    centred = value - average
    scale = lax.rsqrt(jnp.mean(centred * centred, -1, keepdims=True) + EPSILON)
    return centred * scale, scale


def back_of(incoming, normal, scale, gain):
    scaled = incoming * gain
    return scale * (
        scaled
        - jnp.mean(scaled, -1, keepdims=True)
        - normal * jnp.mean(scaled * normal, -1, keepdims=True)
    )


def column_sum(value):
    return jnp.sum(value, 0, keepdims=True)


def mask_of(info_ref, count, before):
    place = info_ref[1] - before + lax.broadcasted_iota(jnp.int32, (count, 1), 0)
    return jnp.where((place >= 0) & (place < info_ref[2]), 1.0, 0.0)


def block_cols(index, size=256):
    return pl.ds(pl.multiple_of(index * size, size), size)


def upper_block(both_ref, index):
    rows = pl.ds(pl.multiple_of(lax.rem(index, 4) * 64, 64), 64)
    if len(both_ref.shape) == 5:
        return both_ref[lax.div(index, 4), :, :, rows, :].reshape(512, 256)
    return both_ref[lax.div(index, 4), :, rows, :].reshape(512, 256)


def narrow_block(both_ref, tap):
    return both_ref[0, :, :, 256 + 64 * tap:320 + 64 * tap, :].reshape(512, 256)


def point_block(both_ref, index):
    return both_ref[1, lax.div(index, 4), lax.rem(index, 4), 256:512, :]


def collect(info_ref, near_refs, far_refs, both_ref, sems, rows=slice(0, 512)):
    core, x, z = info_ref[0], info_ref[5], info_ref[4]
    copies = []
    for side, refs in ((core, near_refs), (1 - core, far_refs)):
        for i, ref in enumerate(refs):
            place = x if i < 4 else 1 - x
            target = both_ref.at[side, place, lax.rem(z + i % 4, 4), rows]
            copies.append((ref.at[rows], target))
    return launch(copies, sems)


def glu_of(both_ref, side):
    return jnp.concatenate(
        [both_ref[side, :, 64 * i:64 * i + 64, :].reshape(512, 256) for i in range(2)], 1
    )


def queries_of(both_ref, side, part):
    return both_ref[side, :, 64 * part:64 * part + 64, :].reshape(512, 256)


def small_pair(one_ref, small_ref):
    return (one_ref.at[0, :, SMALL:SMALL + 32, :], small_ref)


def glu_kernel(info_ref, low_ref, x_ref, high_ref, near_ref, far_ref, n1_ref, a_ref, sg_ref, h1_ref,
               main_ref, w_ref, small_ref, sem):
    rows = x_ref.shape[0]
    main = slice(RIM, RIM + rows)
    core = info_ref[0]
    copies = launch(
        [(near_ref.at[:, SMALL:SMALL + 32, :], small_ref), (near_ref.at[:, 0:128, :], w_ref.at[core]),
         (far_ref.at[:, 0:128, :], w_ref.at[1 - core])], sem
    )
    x = jnp.concatenate(
        [low_ref[...].astype(F32), x_ref[...].astype(F32), high_ref[...].astype(F32)], 0
    )
    normal, _ = normal_of(x)
    settle(copies)
    normed = normal * gains_of(small_ref)[0:1]
    n1 = normed.astype(BF)
    n1_ref[...] = normed[main].astype(BF)
    a = matmul(n1, glu_of(w_ref, 0))
    sg = jax.nn.sigmoid(matmul(n1, glu_of(w_ref, 1)))
    a_ref[...] = a[main].astype(BF)
    sg_ref[...] = sg[main].astype(BF)
    h1 = x + a * sg
    h1_ref[...] = h1
    main_ref[...] = h1[main]


def conv_kernel(info_ref, h1_ref, *refs):
    near2, far2, rest = refs[0:8], refs[8:16], refs[16:]
    conv_body(info_ref, h1_ref, near2, far2, *rest)


def conv_body(info_ref, h1_ref, near2, far2, near1_ref, far1_ref,
              n2_ref, wp_out, np_ref, nm_out, mean_ref, scale_ref, sp_out, h2_ref, n3_ref,
              qkv_ref, two_ref, one_ref, w2_ref, w1_ref, mix_ref, wp_ref, nm_ref, sp_ref, slab_ref,
              sem2, semq, sems):
    core = info_ref[0]
    rim_rows = h1_ref.shape[0]
    rows = rim_rows - 2 * RIM
    copiesq = fetch(core, near1_ref, far1_ref, w1_ref, semq)
    copies2 = collect(info_ref, near2, far2, w2_ref, sem2)
    small_ref = w1_ref.at[0, :, SMALL:SMALL + 32, :]
    settle(copiesq)
    copiesq = launch([(w1_ref, one_ref)], semq)

    def leaving(which, index):
        source, target = ((wp_ref, wp_out), (nm_ref, nm_out), (sp_ref, sp_out))[which]
        cols = block_cols(index)
        return pltpu.make_async_copy(source.at[:, cols], target.at[:, cols], sems.at[which, index])

    gains = gains_of(small_ref)
    valid = mask_of(info_ref, rim_rows, RIM)
    normal, _ = normal_of(h1_ref[...])
    n2f = normal * gains[1:2] * valid
    n2 = n2f.astype(BF)
    n2_ref[...] = n2
    n2f = n2.astype(F32)
    settle(copies2)
    copies2 = launch([(w2_ref, two_ref)], sem2)
    narrow = jnp.zeros((rim_rows, 256), F32)
    for tap in range(3):
        if tap == 1:
            moved = n2
        else:
            moved = pltpu.roll(n2f, 1 if tap == 0 else rim_rows - 1, 0).astype(BF)
        narrow = narrow + matmul(moved, narrow_block(w2_ref, tap))
    np_ref[...] = narrow
    narrow = smooth_unit(narrow)

    def first_pass(index, total):
        weights = jnp.concatenate([upper_block(w2_ref, 2 * index + i) for i in range(2)], 1)
        wide = matmul(n2_ref[...], weights)
        wp_ref[:, block_cols(index, 512)] = wide
        for i in range(2):
            leaving(0, 2 * index + i).start()
        mixed = smooth_unit(wide)
        head = mixed[:, 0:256] + narrow * jnp.where(index == 0, 1.0, 0.0)
        mixed = jnp.concatenate([head, mixed[:, 256:512]], 1)
        mix_ref[:, block_cols(index, 512)] = mixed
        return total + jnp.sum(mixed, -1, keepdims=True)

    total = lax.fori_loop(0, 4, first_pass, jnp.zeros((rim_rows, 1), F32))
    mean = total * (1.0 / 2048)

    total = jnp.zeros((rim_rows, 1), F32)
    for index in range(8):
        centred = mix_ref[:, 256 * index:256 * index + 256] - mean
        total = total + jnp.sum(centred * centred, -1, keepdims=True)
    scale = lax.rsqrt(total * (1.0 / 2048) + EPSILON)
    mean_ref[...] = jnp.broadcast_to(mean, mean_ref.shape)
    scale_ref[...] = jnp.broadcast_to(scale, scale_ref.shape)
    h2_ref[...] = h1_ref[RIM:RIM + rows, :]

    def third_pass(index, carry):
        cols = block_cols(index)
        taps, gain = taps_of(small_ref, index)
        nm = ((mix_ref[:, cols] - mean) * scale * gain * valid).astype(BF)
        nm_ref[:, cols] = nm
        leaving(1, index).start()
        nm = nm.astype(F32)
        halves = []
        for half in range(2):
            lanes = slice(128 * half, 128 * half + 128)
            slab_ref[half] = nm[:, lanes]
            spread = jnp.zeros((rows, 128), F32)
            for tap in range(9):
                spread = spread + slab_ref[half, 4 + tap:4 + tap + rows, :] * taps[tap:tap + 1, lanes]
            halves.append(spread)
        spread = jnp.concatenate(halves, 1).astype(BF)
        sp_ref[:, cols] = spread
        leaving(2, index).start()
        h2_ref[:, 0:256] += matmul(spread, point_block(w2_ref, index))
        return carry

    lax.fori_loop(0, 8, third_pass, 0, unroll=2)
    normal, _ = normal_of(h2_ref[...])
    n3 = (normal * gains[2:3]).astype(BF)
    n3_ref[...] = n3
    for part in range(3):
        for side in range(2):
            block = matmul(n3, w1_ref[side, :, 128 + 64 * part:192 + 64 * part, :].reshape(512, 256))
            qkv_ref[4 * side:4 * side + 4, 64 * part:64 * part + 64, :] = (
                block.T.astype(BF).reshape(4, 64, rows)
            )
    settle(copies2 + copiesq)
    for which in range(3):
        for index in range(8):
            leaving(which, index).wait()


def ffn_kernel(info_ref, h2_ref, o_ref, cot_ref, one_ref, near_ref, far_ref,
               out_ref, acts_ref, g3_ref, dob_ref, gain_ref, heads_ref,
               w_ref, small_ref, y_ref, dn_ref, sem):
    rows = h2_ref.shape[0]
    core = info_ref[0]
    x = info_ref[5]
    pairs = [small_pair(one_ref, small_ref)]
    for side, ref in ((core, near_ref), (1 - core, far_ref)):
        pairs += [(ref.at[:, 0], w_ref.at[side, x]), (ref.at[:, 1], w_ref.at[side, 1 - x])]
    copies = launch(pairs, sem)
    valid = mask_of(info_ref, rows, 0)
    heads_ref[...] = o_ref[...]
    heads = o_ref[...].reshape(512, rows)
    gy = (cot_ref[...].astype(F32) * valid).astype(BF)
    acts_ref[:, ACT_GY] = gy
    settle(copies)
    gains = gains_of(small_ref)
    outs = [w_ref[side, :, :, 512:576, :].reshape(512, 256) for side in range(2)]
    h3 = h2_ref[...] + jnp.concatenate([contract(heads, outs[side], 0, 0) for side in range(2)], 1)
    normal, scale = normal_of(h3)
    acts_ref[:, ACT_N4] = (normal * gains[3:4]).astype(BF)
    y_ref[...] = h3
    dn_ref[...] = jnp.zeros_like(dn_ref)

    gy0, gy1 = acts_ref[:, 4608:4864], acts_ref[:, 4864:5120]

    def step(index, carry):
        upper = jnp.concatenate([upper_block(w_ref, 2 * index + i) for i in range(2)], 1)
        lower = []
        for side in range(2):
            blocks = [2 * index + i for i in range(2)]
            blocks = [w_ref[side, lax.div(k, 4), lax.rem(k, 4), 256:512, :] for k in blocks]
            lower.append(jnp.concatenate(blocks, 0))
        u = matmul(acts_ref[:, ACT_N4], upper)
        sigma = jax.nn.sigmoid(u)
        r = (u * sigma).astype(BF)
        acts_ref[:, block_cols(index, 512)] = r
        dr = contract(gy0, lower[0], 1, 1) + contract(gy1, lower[1], 1, 1)
        du = (dr * (sigma * (1.0 + u * (1.0 - sigma)))).astype(BF)
        acts_ref[:, block_cols(index + 4, 512)] = du
        y_ref[:, 0:256] += matmul(r, lower[0])
        y_ref[:, 256:512] += matmul(r, lower[1])
        dn_ref[...] += contract(du, upper, 1, 1)
        return carry

    lax.fori_loop(0, 4, step, 0)
    out_ref[...] = (y_ref[...] * valid).astype(BF)
    dn = dn_ref[...]
    gain_ref[...] = column_sum(dn * normal)
    g3 = gy.astype(F32) + back_of(dn, normal, scale, gains[3:4])
    g3_ref[...] = g3
    ga = g3.astype(BF)
    acts_ref[:, ACT_GA] = ga
    dob = contract(outs[0], ga[:, 0:256], 1, 1) + contract(outs[1], ga[:, 256:512], 1, 1)
    dob_ref[...] = dob.astype(BF).reshape(HEADS, HEAD, rows)


def pair_rows(value):
    split = value.reshape(8, 8, 8, 256)
    return jnp.concatenate([split[..., 0:128], split[..., 128:256]], 2)


FULL = slice(None)


def by_chip(out_ref, c, rows, value):
    out_ref[c % 2, :, :, c // 2, rows, :] = value.astype(BF).reshape((2, 4) + value.shape[1:])


def by_shard(out_ref, w, rows, value):
    value = value.astype(BF).reshape((4, 2) + value.shape[1:])
    for xh in range(2):
        out_ref[xh, w // 4, w % 4, :, rows, :] = value[:, xh]


def stack_rows(*pieces):
    return jnp.concatenate(pieces, 0)


def early_kernel(info_ref, acts_ref, heads_ref, acts2_ref, heads2_ref, out_ref):
    rows = acts_ref.shape[0]
    side = info_ref[0]

    def tokens(cols):
        return stack_rows(acts_ref[:, cols], acts2_ref[:, cols])

    n4 = tokens(ACT_N4).T
    for j in range(4):
        res = matmul(n4, tokens(block_cols(side * 4 + j + 8)))
        for i in range(2):
            by_chip(out_ref, 2 * j + i, slice(0, 64), res[:, 128 * i:128 * i + 128].reshape(8, 64, 128))
    gy = tokens(block_cols(side + 18)).T
    for w in range(8):
        res = matmul(gy, tokens(slice(256 * w, 256 * w + 256))).reshape(8, 32, 256)
        for i in range(2):
            by_shard(out_ref, w, slice(64 + 32 * i, 96 + 32 * i), res[:, :, 128 * i:128 * i + 128])
    heads = jnp.concatenate([heads_ref[...].reshape(512, rows), heads2_ref[...].reshape(512, rows)], 1)
    packed = pair_rows(matmul(heads, tokens(block_cols(side + 20))))
    for c in range(8):
        by_chip(out_ref, c, slice(128, 144), packed[:, c])


def attn_in_kernel(info_ref, d_ref, h2_in, g3_in, one_ref,
                   g2_ref, gs_ref, lo_ref, hi_ref, gain_ref, w_ref, small_ref, h2_ref, g3_ref, sem):
    rows = h2_ref.shape[0]
    copies = launch(
        [(h2_in, h2_ref), small_pair(one_ref, small_ref), (one_ref.at[:, :, 128:SMALL, :], w_ref),
         (g3_in, g3_ref)], sem
    )
    settle(copies[:1])
    normal, scale = normal_of(h2_ref[...])
    settle(copies[1:])
    gains = gains_of(small_ref)
    parts = [(part, side) for part in range(3) for side in range(2)]
    blocks = [
        d_ref[4 * side:4 * side + 4, 64 * part:64 * part + 64, :].reshape(256, rows) for part, side in parts
    ]
    weights = [queries_of(w_ref, side, part) for part, side in parts]
    dn = contract(stack_rows(*blocks).T, jnp.concatenate(weights, 1), 1, 1)
    gain_ref[...] = column_sum(dn * normal)
    g2 = g3_ref[...] + back_of(dn, normal, scale, gains[2:3])
    g2_ref[...] = g2
    gs = g2[:, 0:256]
    gs_ref[...] = gs.astype(BF)
    lo_ref[...] = gs[0:RIM].astype(BF)
    hi_ref[...] = gs[rows - RIM:rows].astype(BF)


def conv_back_kernel(info_ref, lo_ref, gs_ref, hi_ref, np_ref, mean_ref, scale_ref, nm_in, wp_in,
                     two_ref, one_ref, dw_ref, dnar_ref, table_ref, pt_ref, small_ref, nmf_ref,
                     dsp_ref, sc_ref, hat_ref, nm_ref, wp_ref, sem, sems):
    rim_rows = wp_ref.shape[0]
    rows = rim_rows - 2 * RIM
    main = slice(RIM, RIM + rows)
    copies = launch(
        [small_pair(one_ref, small_ref), (two_ref.at[1, :, :, 256:512, :], pt_ref)], sem
    )

    def arriving(which, index):
        source, target = ((nm_in, nm_ref), (wp_in, wp_ref))[which]
        cols = block_cols(index)
        return pltpu.make_async_copy(source.at[:, cols], target.at[:, cols], sems.at[which, index])

    for index in range(8):
        for which in range(2):
            arriving(which, index).start()
    valid = mask_of(info_ref, rim_rows, RIM)
    gs = jnp.concatenate(
        [lo_ref[...].astype(F32), gs_ref[...].astype(F32), hi_ref[...].astype(F32)], 0
    ).astype(BF)
    mean = mean_ref[:, 0:1]
    scale = scale_ref[:, 0:1]
    table_ref[...] = jnp.zeros_like(table_ref)
    dsp_ref[:, 0:RIM, :] = jnp.zeros((2, RIM, 128), F32)
    dsp_ref[:, RIM + rim_rows:, :] = jnp.zeros((2, RIM, 128), F32)
    settle(copies)

    def first_pass(index, carry):
        one, two = carry
        cols = block_cols(index)
        taps, gain = taps_of(small_ref, index)
        arriving(0, index).wait()
        arriving(1, index).wait()
        dsp = contract(gs, pt_ref[lax.div(index, 4), lax.rem(index, 4)], 1, 1).astype(BF).astype(F32)
        nm = nm_ref[:, cols].astype(F32)
        halves = []
        sums = []
        for half in range(2):
            lanes = slice(128 * half, 128 * half + 128)
            dsp_ref[half, RIM:RIM + rim_rows, :] = dsp[:, lanes]
            nmf_ref[half] = nm[:, lanes]
            inner = dsp[main, lanes]
            dn = jnp.zeros((rim_rows, 128), F32)
            parts = []
            for tap in range(9):
                dn = dn + dsp_ref[half, 12 - tap:12 - tap + rim_rows, :] * taps[tap:tap + 1, lanes]
                parts.append(column_sum(nmf_ref[half, 4 + tap:4 + tap + rows, :] * inner))
            halves.append(dn)
            sums.append(jnp.concatenate(parts, 0))
        table_ref[0:9, cols] = jnp.concatenate(sums, 1)
        dn = jnp.concatenate(halves, 1) * valid
        mixed = smooth_unit(wp_ref[:, cols]) + smooth_unit(np_ref[...]) * jnp.where(index == 0, 1.0, 0.0)
        hat = (mixed - mean) * scale
        hat_ref[:, cols] = hat
        table_ref[9:10, cols] = column_sum((dn * hat)[main])
        scaled = dn * gain
        sc_ref[:, cols] = scaled
        return (one + jnp.sum(scaled, -1, keepdims=True),
                two + jnp.sum(scaled * hat, -1, keepdims=True))

    zero = jnp.zeros((rim_rows, 1), F32)
    one, two = lax.fori_loop(0, 8, first_pass, (zero, zero))
    one = one * (1.0 / 2048)
    two = two * (1.0 / 2048)
    back = scale * (sc_ref[:, 0:256] - one - hat_ref[:, 0:256] * two)
    dnar_ref[...] = (back * smooth_slope(np_ref[...])).astype(BF)

    def second_pass(index, carry):
        cols = block_cols(index)
        back = scale[main] * (
            sc_ref[main, cols] - one[main] - hat_ref[main, cols] * two[main]
        )
        dw_ref[:, cols] = (back * smooth_slope(wp_ref[main, cols])).astype(BF)
        return carry

    lax.fori_loop(0, 8, second_pass, 0)


def glu_back_kernel(info_ref, dw_ref, dnar_ref, h1_in, two_ref, one_ref, g2_ref,
                    a_in, sg_in, x_in, table_ref, gattn_ref, gffn_ref, dx_ref, dab_ref, sums_ref,
                    w2_ref, w1_ref, small_ref, nar_ref, h1_ref, a_ref, sg_ref, x_ref, sem):
    rows = g2_ref.shape[0]
    first = launch([(h1_in, h1_ref)], sem)
    copies = launch(
        [(two_ref.at[0, :, :, 0:448, :], w2_ref.at[0]),
         (two_ref.at[1, :, :, 0:256, :], w2_ref.at[1, :, :, 0:256, :])], sem.at[1:3]
    )
    copies1 = launch(
        [small_pair(one_ref, small_ref), (one_ref.at[:, :, 0:128, :], w1_ref), (a_in, a_ref),
         (sg_in, sg_ref), (x_in, x_ref)], sem.at[3:8]
    )
    valid = mask_of(info_ref, rows, 0)
    nar_ref[...] = dnar_ref[...].astype(F32)
    settle(first)
    normal, scale1 = normal_of(h1_ref[...])
    moved = jnp.concatenate([nar_ref[9 - tap:9 - tap + rows, :].astype(BF) for tap in range(3)], 1)
    dn = jnp.zeros((rows, 512), F32)
    for side in range(2):
        copies[side].wait()
        weights = [w2_ref[side, :, :, 64 * j:64 * j + 64, :].reshape(512, 256) for j in range(4)]
        dn = dn + contract(dw_ref[:, 1024 * side:1024 * side + 1024], jnp.concatenate(weights, 1), 1, 1)
        if side == 0:
            weights = jnp.concatenate([narrow_block(w2_ref, tap) for tap in range(3)], 1)
            dn = dn + contract(moved, weights, 1, 1)
    settle(copies1)
    gains = gains_of(small_ref)
    dn = dn * valid
    gconv = column_sum(dn * normal)
    g1 = g2_ref[...] + back_of(dn, normal, scale1, gains[1:2])
    sg = sg_ref[...].astype(F32)
    da = (g1 * sg).astype(BF)
    db = (g1 * a_ref[...].astype(F32) * sg * (1.0 - sg)).astype(BF)
    dab_ref[:, 0:512] = da
    dab_ref[:, 512:1024] = db
    sums_ref[0:16, :] = table_ref[...]
    sums_ref[16:24, :] = jnp.zeros((8, 2048), F32)
    sums_ref[17:18, 0:512] = gconv
    sums_ref[18:19, 0:512] = gattn_ref[...]
    sums_ref[19:20, 0:512] = gffn_ref[...]
    dn = contract(da, glu_of(w1_ref, 0), 1, 1) + contract(db, glu_of(w1_ref, 1), 1, 1)
    normal, scale0 = normal_of(x_ref[...].astype(F32))
    sums_ref[16:17, 0:512] = column_sum(dn * normal)
    dx_ref[...] = g1 + back_of(dn, normal, scale0, gains[0:1])


def middle_kernel(info_ref, sp_ref, gs_ref, n3_ref, d_ref, sp2_ref, gs2_ref, n32_ref, d2_ref, out_ref):
    rows = gs_ref.shape[0]
    side = info_ref[0]
    gs = stack_rows(gs_ref[:, block_cols(side, 128)], gs2_ref[:, block_cols(side, 128)]).T
    for w in range(8):
        cols = slice(256 * w, 256 * w + 256)
        res = matmul(gs, stack_rows(sp_ref[:, cols], sp2_ref[:, cols])).reshape(8, 16, 256)
        for i in range(2):
            out_ref[:, w, 16 * i:16 * i + 16, :] = res[:, :, 128 * i:128 * i + 128].astype(BF)
    n3 = stack_rows(n3_ref[...], n32_ref[...]).T
    for part in range(3):
        d = [ref[pl.ds(side * 4, 4), 64 * part:64 * part + 64, :].reshape(256, rows) for ref in (d_ref, d2_ref)]
        packed = pair_rows(contract(n3, jnp.concatenate(d, 1), 1, 1)).astype(BF)
        for w in range(8):
            out_ref[:, w, 32 + 16 * part:48 + 16 * part, :] = packed[w]


def late_kernel(info_ref, n2_ref, dw_ref, dnar_ref, n1_ref, dab_ref, small_ref, n22_ref, dw2_ref,
                dnar2_ref, n12_ref, dab2_ref, small2_ref, out_ref, n2f_ref, narf_ref):
    rows = dw_ref.shape[0]
    side = info_ref[0]
    shifted = []
    dnar = []
    for n_ref, d_ref in ((n2_ref, dnar_ref), (n22_ref, dnar2_ref)):
        n2f_ref[...] = n_ref[...].astype(F32)
        narf_ref[...] = d_ref[...].astype(F32)
        shifted.append([n2f_ref[7 + tap:7 + tap + rows, :].astype(BF) for tap in range(3)])
        dnar.append(narf_ref[RIM:RIM + rows, block_cols(side, 128)].astype(BF))
    shifted = [stack_rows(*pair).T for pair in zip(*shifted)]
    dnar = stack_rows(*dnar)
    for j in range(4):
        cols = block_cols(side * 4 + j)
        res = matmul(shifted[1], stack_rows(dw_ref[:, cols], dw2_ref[:, cols]))
        for i in range(2):
            part = res[:, 128 * i:128 * i + 128].reshape(8, 64, 128)
            out_ref[2 * j + i, :, 0:64, :] = part.astype(BF)
    narrow = [matmul(piece, dnar) for piece in shifted]
    for w in range(8):
        lanes = pl.ds(pl.multiple_of(w * 256 + side * 128, 128), 128)
        pair = slice(128 * (w // 2), 128 * (w // 2) + 128)
        table = small_ref[0:16, lanes] + small2_ref[0:16, lanes]
        gains = small_ref[16:20, pair] + small2_ref[16:20, pair]
        table = jnp.concatenate([table[0:10], gains, table[14:16]], 0)
        for c in range(8):
            pieces = [n[64 * w + 8 * c:64 * w + 8 * c + 8] for n in narrow]
            pieces += [table[2 * c:2 * c + 2], jnp.zeros((6, 128), F32)]
            out_ref[c, w, 64:96, :] = jnp.concatenate(pieces, 0).astype(BF)
    n1 = stack_rows(n1_ref[...], n12_ref[...]).T
    for place in range(2):
        cols = block_cols(side + 2 * place)
        packed = pair_rows(matmul(n1, stack_rows(dab_ref[:, cols], dab2_ref[:, cols]))).astype(BF)
        for w in range(8):
            out_ref[:, w, 96 + 16 * place:112 + 16 * place, :] = packed[w]


def unpack_kernel(info_ref, near_ref, far_ref, gglu_ref, val_ref, gat_ref, gconv_ref, wid_ref, nar_ref,
                  gmid_ref, dep_ref, pnt_ref, gatt_ref, qry_ref, key_ref, vls_ref, outp_ref,
                  gffn_ref, upper_ref, lower_ref, fin_ref, low_ref, pt_ref, table_ref, sem):
    settle(fetch(info_ref[0], near_ref, far_ref, fin_ref, sem))
    for c in range(8):
        for k in range(2):
            fin = fin_ref[k, c].astype(F32)
            lanes = slice(k * 1024 + c * 128, k * 1024 + c * 128 + 128)
            upper_ref[:, lanes] = fin[0:64]
            wid_ref[:, lanes] = fin[EARLY + MIDDLE:EARLY + MIDDLE + 64]
            middle = EARLY
            late = EARLY + MIDDLE
            for i in range(2):
                low_ref[k * 256 + c * 32:k * 256 + c * 32 + 32, 128 * i:128 * i + 128] = (
                    fin[64 + 32 * i:96 + 32 * i]
                )
                pt_ref[k * 128 + c * 16:k * 128 + c * 16 + 16, 128 * i:128 * i + 128] = (
                    fin[middle + 16 * i:middle + 16 * i + 16]
                )
            for tap in range(3):
                nar_ref[tap, 8 * c:8 * c + 8, 128 * k:128 * k + 128] = (
                    fin[late + 64 + 8 * tap:late + 72 + 8 * tap]
                )
            table_ref[2 * c:2 * c + 2, 128 * k:128 * k + 128] = fin[late + 88:late + 90]
            bases = [128] + [middle + 32 + 16 * i for i in range(3)] + [late + 96, late + 112]
            targets = [outp_ref, qry_ref, key_ref, vls_ref, val_ref, gat_ref]
            for base, target in zip(bases, targets):
                for i in range(2):
                    target[8 * c:8 * c + 8, k * 256 + 128 * i:k * 256 + 128 * i + 128] = (
                        fin[base + 8 * i:base + 8 * i + 8]
                    )
    lower_ref[...] = low_ref[...].T
    pnt_ref[...] = pt_ref[...].T
    dep_ref[...] = table_ref[0:9, :]
    gmid_ref[...] = table_ref[9:10, :]
    even = info_ref[3] == 0
    gains = jnp.where(even, table_ref[10:14, 0:64], table_ref[10:14, 64:128])
    gglu_ref[...] = gains[0:1]
    gconv_ref[...] = gains[1:2]
    gatt_ref[...] = gains[2:3]
    gffn_ref[...] = gains[3:4]


def pack_ring_kernel(info_ref, wide_ref, narrow_ref, point_ref, out_ref, sem):
    core = info_ref[0]
    pairs = [
        (wide_ref.at[:, block_cols(core * 4 + j)], out_ref.at[64 * j:64 * j + 64, :]) for j in range(4)
    ]
    copies = launch(pairs, sem)

    @pl.when(core == 0)
    def _():
        settle(launch([(narrow_ref, out_ref.at[256:448, :]),
                       (narrow_ref.at[0:64, :], out_ref.at[448:512, :])], sem.at[4:6]))

    @pl.when(core == 1)
    def _():
        settle(launch([(point_ref, out_ref.at[256:512, :])], sem.at[4:5]))

    settle(copies)


def pack_rest_kernel(info_ref, value_ref, gate_ref, query_ref, key_ref, values_ref, g0_ref, g1_ref,
                     g2_ref, g3_ref, depth_ref, mid_ref, in_ref, out_ref, outw_ref, one_ref,
                     three_ref, pack_ref, g0, g1, g2, g3, depth, mid, sem):
    core = info_ref[0]
    own = block_cols(core)
    small = [(g0_ref, g0), (g1_ref, g1), (g2_ref, g2), (g3_ref, g3), (depth_ref, depth), (mid_ref, mid)]
    small = launch(small, sem)
    weights = launch(
        [(ref.at[:, own], pack_ref.at[128 + 64 * i:192 + 64 * i, :])
         for i, ref in enumerate((query_ref, key_ref, values_ref))], sem.at[6:9],
    )
    later = [(in_ref.at[:, block_cols(core * 4 + j)], three_ref.at[64 * j:64 * j + 64, :]) for j in range(4)]
    later += [(out_ref.at[:, own], three_ref.at[256:512, :]), (outw_ref.at[:, own], three_ref.at[512:576, :])]
    later = launch(later, sem.at[9:15])
    for index, ref in ((0, value_ref), (1, gate_ref)):
        @pl.when(core == index)
        def _():
            settle(launch([(ref.at[:, 256 * i:256 * i + 256], pack_ref.at[64 * i:64 * i + 64, :])
                           for i in range(2)], sem.at[15:17]))
    settle(small)
    gains = jnp.concatenate(
        [ref[...].astype(F32) for ref in (g0, g1, g2, g3)] + [jnp.zeros((4, 64), F32)], 0
    )
    gains = jnp.concatenate([gains] * 8, 1)
    place = lax.broadcasted_iota(jnp.int32, (8, 512), 1)
    start = (info_ref[5] * 4 + info_ref[4]) * 64
    gains = jnp.where((place >= start) & (place < start + 64), gains, 0.0)
    gains = jnp.concatenate([gains[:, 0:256], gains[:, 256:512]], 0)
    pack_ref[SMALL:SMALL + 16, :] = gains.astype(BF)
    taps = jnp.concatenate([depth[...].astype(F32), mid[...].astype(F32), jnp.zeros((6, 256), F32)], 0)
    pack_ref[SMALL + 16:SMALL + 32, :] = taps.astype(BF)
    settle(weights)
    for w in range(8):
        one_ref[w] = pack_ref[...]
    settle(later)


def fold_kernel(*refs):
    total = refs[0][...].astype(F32)
    for ref in refs[1:4]:
        total = total + ref[...].astype(F32)
    refs[4][...] = total.astype(BF)


def over_x(value):
    value = value.reshape((4,) + value.shape[2:])
    return lax.psum_scatter(value, ("xh", "xl"), scatter_dimension=0, tiled=True)[0]


def over_z(value):
    return lax.psum_scatter(value, "z", scatter_dimension=0, tiled=True)[0]


def spread_out(own, axes, count):
    copies = jnp.broadcast_to(own[None], (count,) + own.shape)
    return lax.all_to_all(copies, axes, 0, 0, tiled=True)


def shards(
    inputs, lengths, cotangent, glu_gain, glu_value, glu_gate, conv_gain, wide_weight,
    narrow_weight, mid_gain, depth_weight, point_weight, attn_gain, query_weight, key_weight,
    value_weight, output_weight, ffn_gain, ffn_in, ffn_out,
):
    rows, width = inputs.shape[1], inputs.shape[2]
    units = wide_weight.shape[1]
    rim_rows = rows + 2 * RIM
    core = lax.axis_index("core")
    shard = lax.axis_index("xl") * 4 + lax.axis_index("z")
    first = (lax.axis_index("y") * 4 + lax.axis_index("xh") * 2 + core) * rows
    xl, z = lax.axis_index("xl"), lax.axis_index("z")
    info = jnp.stack([core, first, lengths[0], shard % 2, z, xl]).astype(jnp.int32)
    flip = shift(dc=1)
    dma = pltpu.SemaphoreType.DMA

    pack2 = call(
        pack_ring_kernel, [((512, 256), BF, FREE)], [SMEM] + [HBM] * 3, [dma((6,))], "pack_ring", 1,
        info, wide_weight, narrow_weight.reshape(192, 256), point_weight,
    )[0]
    steps = [shift(dz=-1), shift(dz=2), shift(dz=1)]
    other = send(pack2, shift(dxl=1))
    own_pieces = [send(pack2, step) for step in steps]
    other_pieces = [send(other, step) for step in steps]

    line = lambda v: v.reshape(1, -1)
    pack1, pack3 = call(
        pack_rest_kernel, [((8, SMALL + 32, 256), BF, FREE), ((576, 256), BF, FREE)], [SMEM] + [HBM] * 14,
        [pltpu.VMEM((SMALL + 32, 256), BF)] + [pltpu.VMEM((1, 64), BF)] * 4
        + [pltpu.VMEM((9, 256), BF), pltpu.VMEM((1, 256), BF), dma((17,))],
        "pack_rest", 1, info, glu_value, glu_gate, query_weight, key_weight, value_weight,
        line(glu_gain), line(conv_gain), line(attn_gain), line(ffn_gain), depth_weight,
        line(mid_gain), ffn_in, ffn_out, output_weight,
    )

    pack1, *_ = lax.optimization_barrier((pack1, *own_pieces, other))
    near1 = lax.all_to_all(pack1, WT, 0, 0, tiled=True)
    x = inputs[0]
    low_x = send(x[rows - RIM:], along(1))
    high_x = send(x[:RIM], along(-1))
    other3 = send(pack3, shift(dxl=1))
    near1, pack3, other3, low_x, high_x, *ready = lax.optimization_barrier(
        (near1, pack3, other3, low_x, high_x, *own_pieces, *other_pieces)
    )
    near2 = [pack2] + ready[:3] + [other] + ready[3:]
    far2 = [send(piece, flip) for piece in near2]
    far1 = send(near1, flip)
    near3 = lax.all_gather(jnp.stack([pack3, other3]), "z", axis=0)

    tall, wide, narrow = (rows, width), (rows, units), (rows, 256)
    tiny = pltpu.VMEM((8, 32, 256), BF)
    ring = pltpu.VMEM((2, 2, 4) + pack2.shape, BF)
    n1, a, sg, h1, h1m = call(
        glu_kernel,
        [(tall, BF), (tall, BF), (tall, BF), ((rim_rows, width), F32, FREE), (tall, F32)],
        [SMEM] + [FREE] * 3 + [ANY] * 2, [pltpu.VMEM((2, 8, 128, 256), BF), tiny, dma((3,))], "glu", 3,
        info, low_x, x, high_x, near1, far1,
    )
    n2, wp, np_, nm, mean, scale, sp, h2, n3, qkv, two, one = call(
        conv_kernel,
        [((rim_rows, width), BF), ((rim_rows, units), F32, HBM), ((rim_rows, 256), F32),
         ((rim_rows, units), BF, HBM), ((rim_rows, 128), F32), ((rim_rows, 128), F32),
         (wide, BF, HBM), (tall, F32), (tall, BF), ((HEADS, 3 * HEAD, rows), BF, FREE),
         (ring.shape, BF, HBM), ((2,) + near1.shape, BF, HBM)],
        [SMEM, FREE] + [ANY] * 18,
        [ring, pltpu.VMEM((2,) + near1.shape, BF), pltpu.VMEM((rim_rows, units), F32),
         pltpu.VMEM((rim_rows, units), F32), pltpu.VMEM((rim_rows, units), BF), pltpu.VMEM(wide, BF),
         pltpu.VMEM((2, rim_rows, 128), F32), dma((16,)), dma((2,)), dma((3, 8))],
        "conv", 15, info, h1, *near2, *far2, near1, far1,
    )
    near = lax.all_to_all(qkv, CHIPS, 0, 0, tiled=True)
    far = send(near[:, HEAD:], flip)
    head_out, expo, inverse, near, far = attend(near, far, lengths, info[:1])
    near3, _ = lax.optimization_barrier((near3, head_out))
    far3 = send(near3, flip)
    heads_in = lax.all_to_all(head_out, CHIPS, 0, 0, tiled=True)
    output, acts, g3, dob, d_gffn, heads_in = call(
        ffn_kernel,
        [(tall, BF), ((rows, 5632), BF, FREE), (tall, F32), ((HEADS, HEAD, rows), BF),
         ((1, width), F32), ((HEADS, HEAD, rows), BF, FREE)],
        [SMEM, VMEM, FREE, VMEM, HBM, HBM, ANY],
        [pltpu.VMEM((2, 2, 4) + pack3.shape, BF), tiny, pltpu.VMEM(tall, F32), pltpu.VMEM(tall, F32),
         dma((5,))],
        "ffn", 11, info, h2, heads_in, cotangent[0], one, near3, far3,
    )

    d_near = lax.all_to_all(dob, CHIPS, 0, 0, tiled=True)
    early = call(
        early_kernel, [((2, 2, 4, 4, EARLY, 128), BF)], [SMEM] + [FREE] * 4, [], "early", 0.3,
        info, acts, heads_in, send(acts, flip), send(heads_in, flip),
    )[0]
    d_near, early = lax.optimization_barrier((d_near, early))
    early = over_x(early)
    keep, give = attend_back(near, far, expo, head_out, inverse, d_near)
    take = jnp.pad(send(give, flip), ((0, 0), (HEAD, 0), (0, 0)))
    d_qkv = (keep.astype(F32) + take.astype(F32)).astype(BF)
    d_qkv = lax.all_to_all(d_qkv, CHIPS, 0, 0, tiled=True)
    early = over_z(early)
    sp2, n32 = send(sp, flip), send(n3, flip)
    info_attn, _ = lax.optimization_barrier((info, sp2))
    g2, gs, lo, hi, d_gatt = call(
        attn_in_kernel,
        [(tall, F32), (narrow, BF, FREE), ((RIM, 256), BF), ((RIM, 256), BF), ((1, width), F32)],
        [SMEM, FREE] + [HBM] * 3,
        [pltpu.VMEM((2, 8, SMALL - 128, 256), BF), tiny, pltpu.VMEM(tall, F32), pltpu.VMEM(tall, F32),
         dma((4,))],
        "attn_in", 0.5, info_attn, d_qkv, h2, g3, one,
    )
    low_gs = send(hi, along(1))
    high_gs = send(lo, along(-1))
    info_mid, _, _ = lax.optimization_barrier((info, low_gs, high_gs))
    middle = call(
        middle_kernel, [((8, 8, MIDDLE, 128), BF)], [SMEM, VMEM, FREE, VMEM, FREE] + [FREE] * 4, [], "middle", 0.3,
        info_mid, sp, gs, n3, d_qkv, sp2, send(gs, flip), n32, send(d_qkv, flip),
    )[0]
    info_conv, middle = lax.optimization_barrier((info, middle))
    middle = lax.all_to_all(middle.reshape(64, MIDDLE, 128), CHIPS + WT, 0, 0, tiled=True)
    rim_narrow = ((rim_rows, 256), BF)
    dw, dnar, table = call(
        conv_back_kernel, [(wide, BF, FREE), ((rim_rows, 256), BF, FREE), ((16, units), F32, FREE)],
        [SMEM, FREE, FREE, FREE] + [VMEM] * 3 + [HBM] * 4,
        [pltpu.VMEM((2, 4, 256, 256), BF), tiny, pltpu.VMEM((2, rim_rows, 128), F32),
         pltpu.VMEM((2, rim_rows + 2 * RIM, 128), F32), pltpu.VMEM((rim_rows, units), F32),
         pltpu.VMEM((rim_rows, units), F32), pltpu.VMEM((rim_rows, units), BF),
         pltpu.VMEM((rim_rows, units), F32), dma((2,)), dma((2, 8))],
        "conv_back", 2, info_conv, low_gs, gs, high_gs, np_, mean, scale, nm, wp, two, one,
    )
    dw2, dnar2 = send(dw, flip), send(dnar, flip)
    info_glu, early = lax.optimization_barrier((info, early))
    dx, dab, sums = call(
        glu_back_kernel,
        [(tall, F32), ((rows, 2 * width), BF, FREE), ((24, units), F32, FREE)],
        [SMEM, FREE, FREE, HBM, HBM, HBM, VMEM, HBM, HBM, HBM, FREE, VMEM, VMEM],
        [pltpu.VMEM((2, 2, 4, 448, 256), BF), pltpu.VMEM((2, 8, 128, 256), BF), tiny,
         pltpu.VMEM((rim_rows, 256), F32), pltpu.VMEM(tall, F32), pltpu.VMEM(tall, BF),
         pltpu.VMEM(tall, BF), pltpu.VMEM(tall, BF), dma((8,))],
        "glu_back", 1, info_glu, dw, dnar, h1m, two, one, g2, a, sg, x, table, d_gatt, d_gffn,
    )
    dab2, sums2 = send(dab, flip), send(sums, flip)
    middle = jnp.sum(middle.astype(F32), 0).astype(BF)
    late = call(
        late_kernel, [((8, 8, LATE, 128), BF)], [SMEM, VMEM, FREE, FREE, VMEM, FREE, FREE] + [FREE] * 6,
        [pltpu.VMEM((rim_rows, width), F32), pltpu.VMEM((rim_rows, 256), F32)], "late", 0.5,
        info, n2, dw, dnar, n1, dab, sums, send(n2, flip), dw2, dnar2, send(n1, flip), dab2, sums2,
    )[0]
    _, early = lax.optimization_barrier((late, early))
    y = lax.axis_index("y")
    pick = lambda index: lax.dynamic_index_in_dim(early, index % 4, 0, keepdims=False)
    parts = [send(pick(y + d), shift(dy=d)) for d in (1, 2, 3)]
    early = call(
        fold_kernel, [((EARLY, 128), BF, FREE)], [FREE] * 4, [], "fold", FOLD, pick(y), *parts
    )[0]
    late = lax.all_to_all(late.reshape(64, LATE, 128), CHIPS + WT, 0, 0, tiled=True)
    late = jnp.sum(late.astype(F32), 0).astype(BF)
    final = spread_out(jnp.concatenate([early, middle, late], 0), CHIPS, 8)
    square, broad = ((64, 512), F32), ((64, 2048), F32)
    line = ((1, 64), F32)
    grads = call(
        unpack_kernel,
        [line, square, square, line, broad, ((3, 64, 256), F32), ((1, 256), F32),
         ((9, 256), F32), ((256, 256), F32), line, square, square, square, square, line, broad,
         ((256, 512), F32)],
        [SMEM, ANY, ANY],
        [pltpu.VMEM((2,) + final.shape, BF), pltpu.VMEM((512, 256), F32),
         pltpu.VMEM((256, 256), F32), pltpu.VMEM((16, 256), F32), dma((2,))],
        "unpack", 3, info, final, send(final, flip),
    )
    grads = [g[0] if g.shape[0] == 1 else g for g in grads]
    return (output[None], dx[None]) + tuple(grads)


def solution(mesh):
    fine = Mesh(mesh.devices.reshape(SIZES), AXES)
    flat, row, mid = P(WT), P(WT, None), P(None, WT, None)
    col = P(None, WT)
    tokens = P(WT, CTX, None)
    weights = (
        flat, row, row, flat, row, mid, flat, col, row, flat, row, row, row, row, flat, row, row,
    )
    return jax.shard_map(
        shards, mesh=fine, in_specs=(tokens, flat, tokens) + weights,
        out_specs=(tokens, tokens) + weights, check_vma=False,
    )
```

```python
import functools

import jax
import jax.numpy as jnp
import numpy as np
from jax import lax
from jax.experimental import pallas as pl
from jax.experimental.pallas import tpu as pltpu
from jax.sharding import Mesh
from jax.sharding import PartitionSpec as P

HEADS = 8
HEAD = 64
EPSILON = 1e-06
AXES = ("y", "xh", "core", "xl", "z")
SIZES = (4, 2, 2, 2, 4)
CTX = ("y", "xh", "core")
CHIPS = ("y", "xh")
WT = ("xl", "z")
BLOCK = 1024
LOG2E = 1.4426950408889634
BF = jnp.bfloat16
F32 = jnp.float32


def moves(target):
    pairs = []
    for source in range(int(np.prod(SIZES))):
        place = [int(v) for v in np.unravel_index(source, SIZES)]
        goal = target(*place)
        if goal is not None:
            pairs.append((source, int(np.ravel_multi_index(tuple(goal), SIZES))))
    return pairs


def shift(dy=0, dxh=0, dc=0, dxl=0, dz=0):
    return moves(
        lambda y, xh, c, xl, z: (
            (y + dy) % 4, (xh + dxh) % 2, (c + dc) % 2, (xl + dxl) % 2, (z + dz) % 4,
        )
    )


def along(step):
    def target(y, xh, c, xl, z):
        place = y * 4 + xh * 2 + c + step
        if place < 0 or place > 15:
            return None
        return (place // 4, place // 2 % 2, place % 2, xl, z)
    return moves(target)


def send(value, pairs):
    return lax.ppermute(value, AXES, pairs)


def matmul(left, right):
    return jnp.dot(left, right, preferred_element_type=F32)


def contract(left, right, ldim, rdim):
    return lax.dot_general(
        left, right, (((ldim,), (rdim,)), ((), ())), preferred_element_type=F32
    )


def smooth_unit(value):
    return value * jax.nn.sigmoid(value)


def smooth_slope(value):
    sigma = jax.nn.sigmoid(value)
    return sigma * (1.0 + value * (1.0 - sigma))


VMEM = pl.BlockSpec(memory_space=pltpu.VMEM)
SMEM = pl.BlockSpec(memory_space=pltpu.SMEM)
HBM = pl.BlockSpec(memory_space=pltpu.HBM)
ANY = pl.BlockSpec(memory_space=pl.ANY)
FREE = "free"


def attend_kernel(chips, rows, length_ref, core_ref, near_ref, far_ref, o_ref, e_ref, l_ref,
                  near_out, far_out, keys_ref, values_ref, sem):
    step = pl.program_id(0)
    span = chips * rows
    aug = 2 * HEAD
    pairs = [(near_ref, near_out), (far_ref, far_out)]

    @pl.when(step == chips - 1)
    def _():
        for i, (source, target) in enumerate(pairs):
            pltpu.make_async_copy(source, target, sem.at[i]).wait()

    @pl.when(step == 0)
    def _():
        launch(pairs, sem)
        length = length_ref[0]
        core = core_ref[0]
        ones = jnp.ones((16, rows), F32)
        for side in range(2):
            source = near_ref if side == 0 else far_ref
            base = HEAD if side == 0 else 0
            owner = core if side == 0 else 1 - core
            for chip in range(chips):
                cols = slice(side * span + chip * rows, side * span + (chip + 1) * rows)
                key = source[chip, base:base + HEAD, :]
                keys_ref[0:HEAD, cols] = key
                keys_ref[HEAD:aug, cols] = key
                place = (chip * 2 + owner) * rows + lax.broadcasted_iota(jnp.int32, (16, rows), 1)
                row = lax.broadcasted_iota(jnp.int32, (16, rows), 0)
                bias = jnp.where((place < length) | (row > 0), 0.0, -1e30)
                keys_ref[aug:aug + 16, cols] = bias.astype(BF)
                value = source[chip, base + HEAD:base + 2 * HEAD, :].astype(F32)
                stacked = jnp.concatenate([value, ones, jnp.zeros((48, rows), F32)], 0)
                values_ref[cols, :] = stacked.T.astype(BF)

    query = near_ref[step, 0:HEAD, :].astype(F32) * (LOG2E * HEAD ** -0.5)
    high = query.astype(BF)
    low = (query - high.astype(F32)).astype(BF)
    query = jnp.concatenate([high, low, jnp.ones((16, rows), BF)], 0)
    scores = contract(query, keys_ref[...], 0, 0)
    top = jnp.max(scores, 1, keepdims=True)
    expo = jnp.exp2(scores - top).astype(BF)
    e_ref[...] = expo
    out = matmul(expo, values_ref[...]).T
    inverse = 1.0 / out[HEAD:HEAD + 8]
    o_ref[0] = (out[0:HEAD] * inverse[0:1]).astype(BF)
    l_ref[0] = inverse


def attend(near, far, length, core):
    chips, _, rows = near.shape
    tokens = 2 * chips * rows
    return pl.pallas_call(
        functools.partial(attend_kernel, chips, rows),
        grid=(chips,),
        in_specs=[
            pl.BlockSpec(memory_space=pltpu.SMEM),
            pl.BlockSpec(memory_space=pltpu.SMEM),
            pl.BlockSpec(near.shape, lambda i: (0, 0, 0)),
            pl.BlockSpec(far.shape, lambda i: (0, 0, 0)),
        ],
        out_specs=[
            pl.BlockSpec((1, HEAD, rows), lambda i: (i, 0, 0)),
            pl.BlockSpec((rows, tokens), lambda i: (i, 0)),
            pl.BlockSpec((1, 8, rows), lambda i: (i, 0, 0)),
            HBM,
            HBM,
        ],
        out_shape=[
            pltpu.HBM((chips, HEAD, rows), BF),
            pltpu.HBM((chips * rows, tokens), BF),
            pltpu.HBM((chips, 8, rows), F32),
            pltpu.HBM(near.shape, BF),
            pltpu.HBM(far.shape, BF),
        ],
        scratch_shapes=[
            pltpu.VMEM((2 * HEAD + 16, tokens), BF),
            pltpu.VMEM((tokens, 2 * HEAD), BF),
            pltpu.SemaphoreType.DMA((2,)),
        ],
        compiler_params=pltpu.CompilerParams(vmem_limit_bytes=32 * 2**20),
        cost_estimate=cost(14),
        name="attend",
    )(length, core, near, far)


def attend_back_kernel(chips, rows, near_ref, far_ref, e_ref, o_ref, l_ref, do_ref,
                       keep_ref, give_ref, keys_ref, values_ref, dk_acc, dv_acc):
    step = pl.program_id(0)
    span = chips * rows

    @pl.when(step == 0)
    def _():
        row = lax.broadcasted_iota(jnp.int32, (16, rows), 0)
        ones = jnp.where(row < 3, 1.0, 0.0).astype(BF)
        for side in range(2):
            source = near_ref if side == 0 else far_ref
            base = HEAD if side == 0 else 0
            for chip in range(chips):
                cols = slice(side * span + chip * rows, side * span + (chip + 1) * rows)
                key = source[chip, base:base + HEAD, :].astype(F32)
                stacked = jnp.concatenate([key, jnp.zeros((HEAD, rows), F32)], 0)
                keys_ref[cols, :] = stacked.T.astype(BF)
                values_ref[0:HEAD, cols] = source[chip, base + HEAD:base + 2 * HEAD, :]
                values_ref[HEAD:HEAD + 16, cols] = ones
        dk_acc[...] = jnp.zeros_like(dk_acc)
        dv_acc[...] = jnp.zeros_like(dv_acc)

    inverse = l_ref[0, 0:1, :]
    grad = do_ref[0].astype(F32) * inverse
    total = -jnp.sum(grad * o_ref[0].astype(F32), 0, keepdims=True)
    high = total.astype(BF).astype(F32)
    mid = (total - high).astype(BF).astype(F32)
    low = total - high - mid
    grad_low = grad.astype(BF)
    row = lax.broadcasted_iota(jnp.int32, (16, rows), 0)
    extra = jnp.where(row == 0, high, jnp.where(row == 1, mid, jnp.where(row == 2, low, 0.0)))
    grads = jnp.concatenate([grad_low, extra.astype(BF)], 0)
    query = near_ref[step, 0:HEAD, :]
    grads = grads.T
    block = BLOCK
    dq = jnp.zeros((rows, 2 * HEAD), F32)
    for start in range(0, 2 * span, block):
        cols = slice(start, start + block)
        expo = e_ref[:, cols]
        d_scores = (expo.astype(F32) * matmul(grads, values_ref[:, cols])).astype(BF)
        dq = dq + matmul(d_scores, keys_ref[cols, :])
        dk_acc[:, cols] += matmul(query, d_scores)
        dv_acc[:, cols] += matmul(grad_low, expo)
    keep_ref[step, 0:HEAD, :] = (dq.T[0:HEAD] * HEAD ** -0.5).astype(BF)

    @pl.when(step == chips - 1)
    def _():
        for side in range(2):
            for chip in range(chips):
                cols = slice(side * span + chip * rows, side * span + (chip + 1) * rows)
                out_ref, base = (keep_ref, HEAD) if side == 0 else (give_ref, 0)
                out_ref[chip, base:base + HEAD, :] = (dk_acc[:, cols] * HEAD ** -0.5).astype(BF)
                out_ref[chip, base + HEAD:base + 2 * HEAD, :] = dv_acc[:, cols].astype(BF)


def attend_back(near, far, expo, out, inverse, d_out):
    chips, _, rows = near.shape
    tokens = 2 * chips * rows
    whole = lambda i: (0, 0, 0)
    one = lambda i: (i, 0, 0)
    return pl.pallas_call(
        functools.partial(attend_back_kernel, chips, rows),
        grid=(chips,),
        in_specs=[
            pl.BlockSpec(near.shape, whole),
            pl.BlockSpec(far.shape, whole),
            pl.BlockSpec((rows, tokens), lambda i: (i, 0)),
            pl.BlockSpec((1, HEAD, rows), one),
            pl.BlockSpec((1, 8, rows), one),
            pl.BlockSpec((1, HEAD, rows), one),
        ],
        out_specs=[pl.BlockSpec((chips, 3 * HEAD, rows), whole), pl.BlockSpec((chips, 2 * HEAD, rows), whole)],
        out_shape=[
            jax.ShapeDtypeStruct((chips, 3 * HEAD, rows), BF),
            jax.ShapeDtypeStruct((chips, 2 * HEAD, rows), BF),
        ],
        scratch_shapes=[
            pltpu.VMEM((tokens, 2 * HEAD), BF),
            pltpu.VMEM((HEAD + 16, tokens), BF),
            pltpu.VMEM((HEAD, tokens), F32),
            pltpu.VMEM((HEAD, tokens), F32),
        ],
        compiler_params=pltpu.CompilerParams(vmem_limit_bytes=32 * 2**20),
        cost_estimate=cost(3),
        name="attend_back",
    )(in_hbm(near), in_hbm(far), in_hbm(expo), in_hbm(out), in_hbm(inverse), d_out)


RIM = 8
FOLD = 0.3
ACT_N4 = slice(4096, 4608)
ACT_GY = slice(4608, 5120)
ACT_GA = slice(5120, 5632)
EARLY = 144
SMALL = 128
MIDDLE = 80
LATE = 128


def call(kernel, outs, specs, scratch, name, micros, *args):
    args = [arg if spec in (SMEM, FREE, ANY) else in_hbm(arg) for arg, spec in zip(args, specs)]
    kinds = [out[2] if len(out) > 2 else VMEM for out in outs]
    return pl.pallas_call(
        kernel,
        in_specs=[VMEM if spec is FREE else spec for spec in specs],
        out_specs=[VMEM if kind is FREE else kind for kind in kinds],
        out_shape=[
            (jax.ShapeDtypeStruct if kind is FREE else pltpu.HBM)(out[0], out[1])
            for kind, out in zip(kinds, outs)
        ],
        scratch_shapes=scratch,
        compiler_params=pltpu.CompilerParams(vmem_limit_bytes=32 * 2**20),
        cost_estimate=cost(micros),
        name=name,
    )(*args)


def in_hbm(value):
    return pltpu.with_memory_space_constraint(value, pltpu.HBM)


def cost(micros):
    return pl.CostEstimate(
        flops=int(micros * 1.0e9), bytes_accessed=int(micros * 3.0e6), transcendentals=0
    )


def launch(pairs, sems):
    copies = [
        pltpu.make_async_copy(source, target, sems.at[i]) for i, (source, target) in enumerate(pairs)
    ]
    for copy in copies:
        copy.start()
    return copies


def fetch(core, near_ref, far_ref, both_ref, sems):
    return launch([(near_ref, both_ref.at[core]), (far_ref, both_ref.at[1 - core])], sems)


def settle(copies):
    for copy in copies:
        copy.wait()


def gains_of(small_ref):
    total = small_ref[0, 0:16, :].astype(F32)
    for w in range(1, 8):
        total = total + small_ref[w, 0:16, :].astype(F32)
    return jnp.concatenate([total[0:8], total[8:16]], 1)


def taps_of(small_ref, index):
    small = small_ref[index, 16:32, :].astype(F32)
    return small[0:9], small[9:10]


def normal_of(value):
    average = jnp.mean(value, -1, keepdims=True)
    centred = value - average
    scale = lax.rsqrt(jnp.mean(centred * centred, -1, keepdims=True) + EPSILON)
    return centred * scale, scale


def back_of(incoming, normal, scale, gain):
    scaled = incoming * gain
    return scale * (
        scaled
        - jnp.mean(scaled, -1, keepdims=True)
        - normal * jnp.mean(scaled * normal, -1, keepdims=True)
    )


def column_sum(value):
    return jnp.sum(value, 0, keepdims=True)


def mask_of(info_ref, count, before):
    place = info_ref[1] - before + lax.broadcasted_iota(jnp.int32, (count, 1), 0)
    return jnp.where((place >= 0) & (place < info_ref[2]), 1.0, 0.0)


def block_cols(index, size=256):
    return pl.ds(pl.multiple_of(index * size, size), size)


def upper_block(both_ref, index):
    rows = pl.ds(pl.multiple_of(lax.rem(index, 4) * 64, 64), 64)
    if len(both_ref.shape) == 5:
        return both_ref[lax.div(index, 4), :, :, rows, :].reshape(512, 256)
    return both_ref[lax.div(index, 4), :, rows, :].reshape(512, 256)


def narrow_block(both_ref, tap):
    return both_ref[0, :, :, 256 + 64 * tap:320 + 64 * tap, :].reshape(512, 256)


def point_block(both_ref, index):
    return both_ref[1, lax.div(index, 4), lax.rem(index, 4), 256:512, :]


def collect(info_ref, near_refs, far_refs, both_ref, sems, rows=slice(0, 512)):
    core, x, z = info_ref[0], info_ref[5], info_ref[4]
    copies = []
    for side, refs in ((core, near_refs), (1 - core, far_refs)):
        for i, ref in enumerate(refs):
            place = x if i < 4 else 1 - x
            target = both_ref.at[side, place, lax.rem(z + i % 4, 4), rows]
            copies.append((ref.at[rows], target))
    return launch(copies, sems)


def glu_of(both_ref, side):
    return jnp.concatenate(
        [both_ref[side, :, 64 * i:64 * i + 64, :].reshape(512, 256) for i in range(2)], 1
    )


def queries_of(both_ref, side, part):
    return both_ref[side, :, 64 * part:64 * part + 64, :].reshape(512, 256)


def small_pair(one_ref, small_ref):
    return (one_ref.at[0, :, SMALL:SMALL + 32, :], small_ref)


def glu_kernel(info_ref, low_ref, x_ref, high_ref, near_ref, far_ref, n1_ref, a_ref, sg_ref, h1_ref,
               main_ref, w_ref, small_ref, sem):
    rows = x_ref.shape[0]
    main = slice(RIM, RIM + rows)
    core = info_ref[0]
    copies = launch(
        [(near_ref.at[:, SMALL:SMALL + 32, :], small_ref), (near_ref.at[:, 0:128, :], w_ref.at[core]),
         (far_ref.at[:, 0:128, :], w_ref.at[1 - core])], sem
    )
    x = jnp.concatenate(
        [low_ref[...].astype(F32), x_ref[...].astype(F32), high_ref[...].astype(F32)], 0
    )
    normal, _ = normal_of(x)
    settle(copies)
    normed = normal * gains_of(small_ref)[0:1]
    n1 = normed.astype(BF)
    n1_ref[...] = normed[main].astype(BF)
    a = matmul(n1, glu_of(w_ref, 0))
    sg = jax.nn.sigmoid(matmul(n1, glu_of(w_ref, 1)))
    a_ref[...] = a[main].astype(BF)
    sg_ref[...] = sg[main].astype(BF)
    h1 = x + a * sg
    h1_ref[...] = h1
    main_ref[...] = h1[main]


def conv_kernel(info_ref, h1_ref, *refs):
    near2, far2, rest = refs[0:8], refs[8:16], refs[16:]
    conv_body(info_ref, h1_ref, near2, far2, *rest)


def conv_body(info_ref, h1_ref, near2, far2, near1_ref, far1_ref,
              n2_ref, wp_out, np_ref, nm_out, mean_ref, scale_ref, sp_out, h2_ref, n3_ref,
              two_ref, one_ref, w2_ref, w1_ref, mix_ref, wp_ref, nm_ref, sp_ref, slab_ref,
              sem2, semq, sems):
    core = info_ref[0]
    rim_rows = h1_ref.shape[0]
    rows = rim_rows - 2 * RIM
    copiesq = fetch(core, near1_ref, far1_ref, w1_ref, semq)
    copies2 = collect(info_ref, near2, far2, w2_ref, sem2)
    small_ref = w1_ref.at[0, :, SMALL:SMALL + 32, :]
    settle(copiesq)
    copiesq = launch([(w1_ref, one_ref)], semq)

    def leaving(which, index):
        source, target = ((wp_ref, wp_out), (nm_ref, nm_out), (sp_ref, sp_out))[which]
        cols = block_cols(index)
        return pltpu.make_async_copy(source.at[:, cols], target.at[:, cols], sems.at[which, index])

    gains = gains_of(small_ref)
    valid = mask_of(info_ref, rim_rows, RIM)
    normal, _ = normal_of(h1_ref[...])
    n2f = normal * gains[1:2] * valid
    n2 = n2f.astype(BF)
    n2_ref[...] = n2
    n2f = n2.astype(F32)
    settle(copies2)
    copies2 = launch([(w2_ref, two_ref)], sem2)
    narrow = jnp.zeros((rim_rows, 256), F32)
    for tap in range(3):
        if tap == 1:
            moved = n2
        else:
            moved = pltpu.roll(n2f, 1 if tap == 0 else rim_rows - 1, 0).astype(BF)
        narrow = narrow + matmul(moved, narrow_block(w2_ref, tap))
    np_ref[...] = narrow
    narrow = smooth_unit(narrow)

    def first_pass(index, total):
        weights = jnp.concatenate([upper_block(w2_ref, 2 * index + i) for i in range(2)], 1)
        wide = matmul(n2_ref[...], weights)
        wp_ref[:, block_cols(index, 512)] = wide
        for i in range(2):
            leaving(0, 2 * index + i).start()
        mixed = smooth_unit(wide)
        head = mixed[:, 0:256] + narrow * jnp.where(index == 0, 1.0, 0.0)
        mixed = jnp.concatenate([head, mixed[:, 256:512]], 1)
        mix_ref[:, block_cols(index, 512)] = mixed
        return total + jnp.sum(mixed, -1, keepdims=True)

    total = lax.fori_loop(0, 4, first_pass, jnp.zeros((rim_rows, 1), F32))
    mean = total * (1.0 / 2048)

    total = jnp.zeros((rim_rows, 1), F32)
    for index in range(8):
        centred = mix_ref[:, 256 * index:256 * index + 256] - mean
        total = total + jnp.sum(centred * centred, -1, keepdims=True)
    scale = lax.rsqrt(total * (1.0 / 2048) + EPSILON)
    mean_ref[...] = jnp.broadcast_to(mean, mean_ref.shape)
    scale_ref[...] = jnp.broadcast_to(scale, scale_ref.shape)
    h2_ref[...] = h1_ref[RIM:RIM + rows, :]

    def third_pass(index, carry):
        cols = block_cols(index)
        taps, gain = taps_of(small_ref, index)
        nm = ((mix_ref[:, cols] - mean) * scale * gain * valid).astype(BF)
        nm_ref[:, cols] = nm
        leaving(1, index).start()
        nm = nm.astype(F32)
        halves = []
        for half in range(2):
            lanes = slice(128 * half, 128 * half + 128)
            slab_ref[half] = nm[:, lanes]
            spread = jnp.zeros((rows, 128), F32)
            for tap in range(9):
                spread = spread + slab_ref[half, 4 + tap:4 + tap + rows, :] * taps[tap:tap + 1, lanes]
            halves.append(spread)
        spread = jnp.concatenate(halves, 1).astype(BF)
        sp_ref[:, cols] = spread
        leaving(2, index).start()
        h2_ref[:, 0:256] += matmul(spread, point_block(w2_ref, index))
        return carry

    lax.fori_loop(0, 8, third_pass, 0, unroll=2)
    normal, _ = normal_of(h2_ref[...])
    n3 = (normal * gains[2:3]).astype(BF)
    n3_ref[...] = n3
    settle(copies2 + copiesq)
    for which in range(3):
        for index in range(8):
            leaving(which, index).wait()


def queries_kernel(info_ref, n3_ref, near_ref, far_ref, qkv_ref, wq_out, w_ref, sem):
    rows = n3_ref.shape[0]
    settle(fetch(info_ref[0], near_ref, far_ref, w_ref, sem))
    copies = launch([(w_ref, wq_out)], sem)
    for part in range(3):
        for side in range(2):
            block = matmul(n3_ref[...], queries_of(w_ref, side, part))
            qkv_ref[4 * side:4 * side + 4, 64 * part:64 * part + 64, :] = (
                block.T.astype(BF).reshape(4, 64, rows)
            )
    settle(copies)


def ffn_kernel(info_ref, h2_ref, o_ref, cot_ref, one_ref, near_ref, far_ref,
               out_ref, acts_ref, g3_ref, dob_ref, gain_ref, heads_ref,
               w_ref, small_ref, y_ref, dn_ref, sem, sem_later):
    rows = h2_ref.shape[0]
    core = info_ref[0]
    x = info_ref[5]
    pairs, later = [small_pair(one_ref, small_ref)], []
    for side, ref in ((core, near_ref), (1 - core, far_ref)):
        for rel, place in ((0, x), (1, 1 - x)):
            pairs.append((ref.at[:, rel, 512:576, :], w_ref.at[side, place, :, 512:576, :]))
            later.append((ref.at[:, rel, 0:512, :], w_ref.at[side, place, :, 0:512, :]))
    copies = launch(pairs, sem)
    later = launch(later, sem_later)
    valid = mask_of(info_ref, rows, 0)
    heads_ref[...] = o_ref[...]
    heads = o_ref[...].reshape(512, rows)
    gy = (cot_ref[...].astype(F32) * valid).astype(BF)
    acts_ref[:, ACT_GY] = gy
    settle(copies)
    gains = gains_of(small_ref)
    outs = [w_ref[side, :, :, 512:576, :].reshape(512, 256) for side in range(2)]
    h3 = h2_ref[...] + jnp.concatenate([contract(heads, outs[side], 0, 0) for side in range(2)], 1)
    normal, scale = normal_of(h3)
    acts_ref[:, ACT_N4] = (normal * gains[3:4]).astype(BF)
    y_ref[...] = h3
    dn_ref[...] = jnp.zeros_like(dn_ref)

    settle(later)
    gy0, gy1 = acts_ref[:, 4608:4864], acts_ref[:, 4864:5120]

    def step(index, carry):
        upper = jnp.concatenate([upper_block(w_ref, 2 * index + i) for i in range(2)], 1)
        lower = []
        for side in range(2):
            blocks = [2 * index + i for i in range(2)]
            blocks = [w_ref[side, lax.div(k, 4), lax.rem(k, 4), 256:512, :] for k in blocks]
            lower.append(jnp.concatenate(blocks, 0))
        u = matmul(acts_ref[:, ACT_N4], upper)
        sigma = jax.nn.sigmoid(u)
        r = (u * sigma).astype(BF)
        acts_ref[:, block_cols(index, 512)] = r
        dr = contract(gy0, lower[0], 1, 1) + contract(gy1, lower[1], 1, 1)
        du = (dr * (sigma * (1.0 + u * (1.0 - sigma)))).astype(BF)
        acts_ref[:, block_cols(index + 4, 512)] = du
        y_ref[:, 0:256] += matmul(r, lower[0])
        y_ref[:, 256:512] += matmul(r, lower[1])
        dn_ref[...] += contract(du, upper, 1, 1)
        return carry

    lax.fori_loop(0, 4, step, 0)
    out_ref[...] = (y_ref[...] * valid).astype(BF)
    dn = dn_ref[...]
    gain_ref[...] = column_sum(dn * normal)
    g3 = gy.astype(F32) + back_of(dn, normal, scale, gains[3:4])
    g3_ref[...] = g3
    ga = g3.astype(BF)
    acts_ref[:, ACT_GA] = ga
    dob = contract(outs[0], ga[:, 0:256], 1, 1) + contract(outs[1], ga[:, 256:512], 1, 1)
    dob_ref[...] = dob.astype(BF).reshape(HEADS, HEAD, rows)


def pair_rows(value):
    split = value.reshape(8, 8, 8, 256)
    return jnp.concatenate([split[..., 0:128], split[..., 128:256]], 2)


FULL = slice(None)


def by_chip(out_ref, c, rows, value):
    out_ref[c % 2, :, :, c // 2, rows, :] = value.astype(BF).reshape((2, 4) + value.shape[1:])


def by_shard(out_ref, w, rows, value):
    value = value.astype(BF).reshape((4, 2) + value.shape[1:])
    for xh in range(2):
        out_ref[xh, w // 4, w % 4, :, rows, :] = value[:, xh]


def stack_rows(*pieces):
    return jnp.concatenate(pieces, 0)


def early_kernel(info_ref, acts_ref, heads_ref, acts2_ref, heads2_ref, out_ref):
    rows = acts_ref.shape[0]
    side = info_ref[0]

    def tokens(cols):
        return stack_rows(acts_ref[:, cols], acts2_ref[:, cols])

    n4 = tokens(ACT_N4).T
    for j in range(4):
        res = matmul(n4, tokens(block_cols(side * 4 + j + 8)))
        for i in range(2):
            by_chip(out_ref, 2 * j + i, slice(0, 64), res[:, 128 * i:128 * i + 128].reshape(8, 64, 128))
    gy = tokens(block_cols(side + 18)).T
    for w in range(8):
        res = matmul(gy, tokens(slice(256 * w, 256 * w + 256))).reshape(8, 32, 256)
        for i in range(2):
            by_shard(out_ref, w, slice(64 + 32 * i, 96 + 32 * i), res[:, :, 128 * i:128 * i + 128])
    heads = jnp.concatenate([heads_ref[...].reshape(512, rows), heads2_ref[...].reshape(512, rows)], 1)
    packed = pair_rows(matmul(heads, tokens(block_cols(side + 20))))
    for c in range(8):
        by_chip(out_ref, c, slice(128, 144), packed[:, c])


def attn_in_kernel(info_ref, d_ref, h2_in, g3_in, one_ref, wq_ref,
                   g2_ref, gs_ref, lo_ref, hi_ref, gain_ref, w_ref, small_ref, h2_ref, g3_ref, sem):
    rows = h2_ref.shape[0]
    copies = launch(
        [(h2_in, h2_ref), small_pair(one_ref, small_ref), (wq_ref, w_ref),
         (g3_in, g3_ref)], sem
    )
    settle(copies[:1])
    normal, scale = normal_of(h2_ref[...])
    settle(copies[1:])
    gains = gains_of(small_ref)
    parts = [(part, side) for part in range(3) for side in range(2)]
    blocks = [
        d_ref[4 * side:4 * side + 4, 64 * part:64 * part + 64, :].reshape(256, rows) for part, side in parts
    ]
    weights = [queries_of(w_ref, side, part) for part, side in parts]
    dn = contract(stack_rows(*blocks).T, jnp.concatenate(weights, 1), 1, 1)
    gain_ref[...] = column_sum(dn * normal)
    g2 = g3_ref[...] + back_of(dn, normal, scale, gains[2:3])
    g2_ref[...] = g2
    gs = g2[:, 0:256]
    gs_ref[...] = gs.astype(BF)
    lo_ref[...] = gs[0:RIM].astype(BF)
    hi_ref[...] = gs[rows - RIM:rows].astype(BF)


def conv_back_kernel(info_ref, lo_ref, gs_ref, hi_ref, np_ref, mean_ref, scale_ref, nm_in, wp_in,
                     two_ref, one_ref, dw_ref, dnar_ref, table_ref, pt_ref, small_ref, nmf_ref,
                     dsp_ref, sc_ref, hat_ref, nm_ref, wp_ref, sem, sems):
    rim_rows = wp_ref.shape[0]
    rows = rim_rows - 2 * RIM
    main = slice(RIM, RIM + rows)
    copies = launch(
        [small_pair(one_ref, small_ref), (two_ref.at[1, :, :, 256:512, :], pt_ref)], sem
    )

    def arriving(which, index):
        source, target = ((nm_in, nm_ref), (wp_in, wp_ref))[which]
        cols = block_cols(index)
        return pltpu.make_async_copy(source.at[:, cols], target.at[:, cols], sems.at[which, index])

    for index in range(8):
        for which in range(2):
            arriving(which, index).start()
    valid = mask_of(info_ref, rim_rows, RIM)
    gs = jnp.concatenate(
        [lo_ref[...].astype(F32), gs_ref[...].astype(F32), hi_ref[...].astype(F32)], 0
    ).astype(BF)
    mean = mean_ref[:, 0:1]
    scale = scale_ref[:, 0:1]
    table_ref[...] = jnp.zeros_like(table_ref)
    dsp_ref[:, 0:RIM, :] = jnp.zeros((2, RIM, 128), F32)
    dsp_ref[:, RIM + rim_rows:, :] = jnp.zeros((2, RIM, 128), F32)
    settle(copies)

    def first_pass(index, carry):
        one, two = carry
        cols = block_cols(index)
        taps, gain = taps_of(small_ref, index)
        arriving(0, index).wait()
        arriving(1, index).wait()
        dsp = contract(gs, pt_ref[lax.div(index, 4), lax.rem(index, 4)], 1, 1).astype(BF).astype(F32)
        nm = nm_ref[:, cols].astype(F32)
        halves = []
        sums = []
        for half in range(2):
            lanes = slice(128 * half, 128 * half + 128)
            dsp_ref[half, RIM:RIM + rim_rows, :] = dsp[:, lanes]
            nmf_ref[half] = nm[:, lanes]
            inner = dsp[main, lanes]
            dn = jnp.zeros((rim_rows, 128), F32)
            parts = []
            for tap in range(9):
                dn = dn + dsp_ref[half, 12 - tap:12 - tap + rim_rows, :] * taps[tap:tap + 1, lanes]
                parts.append(column_sum(nmf_ref[half, 4 + tap:4 + tap + rows, :] * inner))
            halves.append(dn)
            sums.append(jnp.concatenate(parts, 0))
        table_ref[0:9, cols] = jnp.concatenate(sums, 1)
        dn = jnp.concatenate(halves, 1) * valid
        mixed = smooth_unit(wp_ref[:, cols]) + smooth_unit(np_ref[...]) * jnp.where(index == 0, 1.0, 0.0)
        hat = (mixed - mean) * scale
        hat_ref[:, cols] = hat
        table_ref[9:10, cols] = column_sum((dn * hat)[main])
        scaled = dn * gain
        sc_ref[:, cols] = scaled
        return (one + jnp.sum(scaled, -1, keepdims=True),
                two + jnp.sum(scaled * hat, -1, keepdims=True))

    zero = jnp.zeros((rim_rows, 1), F32)
    one, two = lax.fori_loop(0, 8, first_pass, (zero, zero))
    one = one * (1.0 / 2048)
    two = two * (1.0 / 2048)
    back = scale * (sc_ref[:, 0:256] - one - hat_ref[:, 0:256] * two)
    dnar_ref[...] = (back * smooth_slope(np_ref[...])).astype(BF)

    def second_pass(index, carry):
        cols = block_cols(index)
        back = scale[main] * (
            sc_ref[main, cols] - one[main] - hat_ref[main, cols] * two[main]
        )
        dw_ref[:, cols] = (back * smooth_slope(wp_ref[main, cols])).astype(BF)
        return carry

    lax.fori_loop(0, 8, second_pass, 0)


def glu_back_kernel(info_ref, dw_ref, dnar_ref, h1_in, two_ref, one_ref, g2_ref,
                    a_in, sg_in, x_in, table_ref, gattn_ref, gffn_ref, dx_ref, dab_ref, sums_ref,
                    w2_ref, w1_ref, small_ref, nar_ref, h1_ref, a_ref, sg_ref, x_ref, sem):
    rows = g2_ref.shape[0]
    first = launch([(h1_in, h1_ref)], sem)
    copies = launch(
        [(two_ref.at[0, :, :, 0:448, :], w2_ref.at[0]),
         (two_ref.at[1, :, :, 0:256, :], w2_ref.at[1, :, :, 0:256, :])], sem.at[1:3]
    )
    copies1 = launch(
        [small_pair(one_ref, small_ref), (one_ref.at[:, :, 0:128, :], w1_ref), (a_in, a_ref),
         (sg_in, sg_ref), (x_in, x_ref)], sem.at[3:8]
    )
    valid = mask_of(info_ref, rows, 0)
    nar_ref[...] = dnar_ref[...].astype(F32)
    settle(first)
    normal, scale1 = normal_of(h1_ref[...])
    moved = jnp.concatenate([nar_ref[9 - tap:9 - tap + rows, :].astype(BF) for tap in range(3)], 1)
    dn = jnp.zeros((rows, 512), F32)
    for side in range(2):
        copies[side].wait()
        weights = [w2_ref[side, :, :, 64 * j:64 * j + 64, :].reshape(512, 256) for j in range(4)]
        dn = dn + contract(dw_ref[:, 1024 * side:1024 * side + 1024], jnp.concatenate(weights, 1), 1, 1)
        if side == 0:
            weights = jnp.concatenate([narrow_block(w2_ref, tap) for tap in range(3)], 1)
            dn = dn + contract(moved, weights, 1, 1)
    settle(copies1)
    gains = gains_of(small_ref)
    dn = dn * valid
    gconv = column_sum(dn * normal)
    g1 = g2_ref[...] + back_of(dn, normal, scale1, gains[1:2])
    sg = sg_ref[...].astype(F32)
    da = (g1 * sg).astype(BF)
    db = (g1 * a_ref[...].astype(F32) * sg * (1.0 - sg)).astype(BF)
    dab_ref[:, 0:512] = da
    dab_ref[:, 512:1024] = db
    sums_ref[0:16, :] = table_ref[...]
    sums_ref[16:24, :] = jnp.zeros((8, 2048), F32)
    sums_ref[17:18, 0:512] = gconv
    sums_ref[18:19, 0:512] = gattn_ref[...]
    sums_ref[19:20, 0:512] = gffn_ref[...]
    dn = contract(da, glu_of(w1_ref, 0), 1, 1) + contract(db, glu_of(w1_ref, 1), 1, 1)
    normal, scale0 = normal_of(x_ref[...].astype(F32))
    sums_ref[16:17, 0:512] = column_sum(dn * normal)
    dx_ref[...] = g1 + back_of(dn, normal, scale0, gains[0:1])


def middle_kernel(info_ref, sp_ref, gs_ref, n3_ref, d_ref, sp2_ref, gs2_ref, n32_ref, d2_ref, out_ref):
    rows = gs_ref.shape[0]
    side = info_ref[0]
    gs = stack_rows(gs_ref[:, block_cols(side, 128)], gs2_ref[:, block_cols(side, 128)]).T
    for w in range(8):
        cols = slice(256 * w, 256 * w + 256)
        res = matmul(gs, stack_rows(sp_ref[:, cols], sp2_ref[:, cols])).reshape(8, 16, 256)
        for i in range(2):
            out_ref[:, w, 16 * i:16 * i + 16, :] = res[:, :, 128 * i:128 * i + 128].astype(BF)
    n3 = stack_rows(n3_ref[...], n32_ref[...]).T
    for part in range(3):
        d = [ref[pl.ds(side * 4, 4), 64 * part:64 * part + 64, :].reshape(256, rows) for ref in (d_ref, d2_ref)]
        packed = pair_rows(contract(n3, jnp.concatenate(d, 1), 1, 1)).astype(BF)
        for w in range(8):
            out_ref[:, w, 32 + 16 * part:48 + 16 * part, :] = packed[w]


def late_kernel(info_ref, n2_ref, dw_ref, dnar_ref, n1_ref, dab_ref, small_ref, n22_ref, dw2_ref,
                dnar2_ref, n12_ref, dab2_ref, small2_ref, out_ref, n2f_ref, narf_ref):
    rows = dw_ref.shape[0]
    side = info_ref[0]
    shifted = []
    dnar = []
    for n_ref, d_ref in ((n2_ref, dnar_ref), (n22_ref, dnar2_ref)):
        n2f_ref[...] = n_ref[...].astype(F32)
        narf_ref[...] = d_ref[...].astype(F32)
        shifted.append([n2f_ref[7 + tap:7 + tap + rows, :].astype(BF) for tap in range(3)])
        dnar.append(narf_ref[RIM:RIM + rows, block_cols(side, 128)].astype(BF))
    shifted = [stack_rows(*pair).T for pair in zip(*shifted)]
    dnar = stack_rows(*dnar)
    for j in range(4):
        cols = block_cols(side * 4 + j)
        res = matmul(shifted[1], stack_rows(dw_ref[:, cols], dw2_ref[:, cols]))
        for i in range(2):
            part = res[:, 128 * i:128 * i + 128].reshape(8, 64, 128)
            out_ref[2 * j + i, :, 0:64, :] = part.astype(BF)
    narrow = [matmul(piece, dnar) for piece in shifted]
    for w in range(8):
        lanes = pl.ds(pl.multiple_of(w * 256 + side * 128, 128), 128)
        pair = slice(128 * (w // 2), 128 * (w // 2) + 128)
        table = small_ref[0:16, lanes] + small2_ref[0:16, lanes]
        gains = small_ref[16:20, pair] + small2_ref[16:20, pair]
        table = jnp.concatenate([table[0:10], gains, table[14:16]], 0)
        for c in range(8):
            pieces = [n[64 * w + 8 * c:64 * w + 8 * c + 8] for n in narrow]
            pieces += [table[2 * c:2 * c + 2], jnp.zeros((6, 128), F32)]
            out_ref[c, w, 64:96, :] = jnp.concatenate(pieces, 0).astype(BF)
    n1 = stack_rows(n1_ref[...], n12_ref[...]).T
    for place in range(2):
        cols = block_cols(side + 2 * place)
        packed = pair_rows(matmul(n1, stack_rows(dab_ref[:, cols], dab2_ref[:, cols]))).astype(BF)
        for w in range(8):
            out_ref[:, w, 96 + 16 * place:112 + 16 * place, :] = packed[w]


def unpack_kernel(info_ref, near_ref, far_ref, gglu_ref, val_ref, gat_ref, gconv_ref, wid_ref, nar_ref,
                  gmid_ref, dep_ref, pnt_ref, gatt_ref, qry_ref, key_ref, vls_ref, outp_ref,
                  gffn_ref, upper_ref, lower_ref, fin_ref, low_ref, pt_ref, table_ref, sem):
    settle(fetch(info_ref[0], near_ref, far_ref, fin_ref, sem))
    for c in range(8):
        for k in range(2):
            fin = fin_ref[k, c].astype(F32)
            lanes = slice(k * 1024 + c * 128, k * 1024 + c * 128 + 128)
            upper_ref[:, lanes] = fin[0:64]
            wid_ref[:, lanes] = fin[EARLY + MIDDLE:EARLY + MIDDLE + 64]
            middle = EARLY
            late = EARLY + MIDDLE
            for i in range(2):
                low_ref[k * 256 + c * 32:k * 256 + c * 32 + 32, 128 * i:128 * i + 128] = (
                    fin[64 + 32 * i:96 + 32 * i]
                )
                pt_ref[k * 128 + c * 16:k * 128 + c * 16 + 16, 128 * i:128 * i + 128] = (
                    fin[middle + 16 * i:middle + 16 * i + 16]
                )
            for tap in range(3):
                nar_ref[tap, 8 * c:8 * c + 8, 128 * k:128 * k + 128] = (
                    fin[late + 64 + 8 * tap:late + 72 + 8 * tap]
                )
            table_ref[2 * c:2 * c + 2, 128 * k:128 * k + 128] = fin[late + 88:late + 90]
            bases = [128] + [middle + 32 + 16 * i for i in range(3)] + [late + 96, late + 112]
            targets = [outp_ref, qry_ref, key_ref, vls_ref, val_ref, gat_ref]
            for base, target in zip(bases, targets):
                for i in range(2):
                    target[8 * c:8 * c + 8, k * 256 + 128 * i:k * 256 + 128 * i + 128] = (
                        fin[base + 8 * i:base + 8 * i + 8]
                    )
    lower_ref[...] = low_ref[...].T
    pnt_ref[...] = pt_ref[...].T
    dep_ref[...] = table_ref[0:9, :]
    gmid_ref[...] = table_ref[9:10, :]
    even = info_ref[3] == 0
    gains = jnp.where(even, table_ref[10:14, 0:64], table_ref[10:14, 64:128])
    gglu_ref[...] = gains[0:1]
    gconv_ref[...] = gains[1:2]
    gatt_ref[...] = gains[2:3]
    gffn_ref[...] = gains[3:4]


def pack_ring_kernel(info_ref, wide_ref, narrow_ref, point_ref, out_ref, sem):
    core = info_ref[0]
    pairs = [
        (wide_ref.at[:, block_cols(core * 4 + j)], out_ref.at[64 * j:64 * j + 64, :]) for j in range(4)
    ]
    copies = launch(pairs, sem)

    @pl.when(core == 0)
    def _():
        settle(launch([(narrow_ref, out_ref.at[256:448, :]),
                       (narrow_ref.at[0:64, :], out_ref.at[448:512, :])], sem.at[4:6]))

    @pl.when(core == 1)
    def _():
        settle(launch([(point_ref, out_ref.at[256:512, :])], sem.at[4:5]))

    settle(copies)


def pack_rest_kernel(info_ref, value_ref, gate_ref, query_ref, key_ref, values_ref, g0_ref, g1_ref,
                     g2_ref, g3_ref, depth_ref, mid_ref, in_ref, out_ref, outw_ref, one_ref,
                     q_ref, three_ref, pack_ref, packq_ref, g0, g1, g2, g3, depth, mid, sem):
    core = info_ref[0]
    own = block_cols(core)
    small = [(g0_ref, g0), (g1_ref, g1), (g2_ref, g2), (g3_ref, g3), (depth_ref, depth), (mid_ref, mid)]
    small = launch(small, sem)
    weights = launch(
        [(ref.at[:, own], packq_ref.at[64 * i:64 * i + 64, :])
         for i, ref in enumerate((query_ref, key_ref, values_ref))], sem.at[6:9],
    )
    later = [(in_ref.at[:, block_cols(core * 4 + j)], three_ref.at[64 * j:64 * j + 64, :]) for j in range(4)]
    later += [(out_ref.at[:, own], three_ref.at[256:512, :]), (outw_ref.at[:, own], three_ref.at[512:576, :])]
    later = launch(later, sem.at[9:15])
    for index, ref in ((0, value_ref), (1, gate_ref)):
        @pl.when(core == index)
        def _():
            settle(launch([(ref.at[:, 256 * i:256 * i + 256], pack_ref.at[64 * i:64 * i + 64, :])
                           for i in range(2)], sem.at[15:17]))
    settle(small)
    gains = jnp.concatenate(
        [ref[...].astype(F32) for ref in (g0, g1, g2, g3)] + [jnp.zeros((4, 64), F32)], 0
    )
    gains = jnp.concatenate([gains] * 8, 1)
    place = lax.broadcasted_iota(jnp.int32, (8, 512), 1)
    start = (info_ref[5] * 4 + info_ref[4]) * 64
    gains = jnp.where((place >= start) & (place < start + 64), gains, 0.0)
    gains = jnp.concatenate([gains[:, 0:256], gains[:, 256:512]], 0)
    pack_ref[SMALL:SMALL + 16, :] = gains.astype(BF)
    taps = jnp.concatenate([depth[...].astype(F32), mid[...].astype(F32), jnp.zeros((6, 256), F32)], 0)
    pack_ref[SMALL + 16:SMALL + 32, :] = taps.astype(BF)
    settle(weights)
    for w in range(8):
        one_ref[w] = pack_ref[...]
        q_ref[w] = packq_ref[...]
    settle(later)


def fold_kernel(*refs):
    total = refs[0][...].astype(F32)
    for ref in refs[1:4]:
        total = total + ref[...].astype(F32)
    refs[4][...] = total.astype(BF)


def over_x(value):
    value = value.reshape((4,) + value.shape[2:])
    return lax.psum_scatter(value, ("xh", "xl"), scatter_dimension=0, tiled=True)[0]


def over_z(value):
    return lax.psum_scatter(value, "z", scatter_dimension=0, tiled=True)[0]


def spread_out(own, axes, count):
    copies = jnp.broadcast_to(own[None], (count,) + own.shape)
    return lax.all_to_all(copies, axes, 0, 0, tiled=True)


def shards(
    inputs, lengths, cotangent, glu_gain, glu_value, glu_gate, conv_gain, wide_weight,
    narrow_weight, mid_gain, depth_weight, point_weight, attn_gain, query_weight, key_weight,
    value_weight, output_weight, ffn_gain, ffn_in, ffn_out,
):
    rows, width = inputs.shape[1], inputs.shape[2]
    units = wide_weight.shape[1]
    rim_rows = rows + 2 * RIM
    core = lax.axis_index("core")
    shard = lax.axis_index("xl") * 4 + lax.axis_index("z")
    first = (lax.axis_index("y") * 4 + lax.axis_index("xh") * 2 + core) * rows
    xl, z = lax.axis_index("xl"), lax.axis_index("z")
    info = jnp.stack([core, first, lengths[0], shard % 2, z, xl]).astype(jnp.int32)
    flip = shift(dc=1)
    dma = pltpu.SemaphoreType.DMA

    pack2 = call(
        pack_ring_kernel, [((512, 256), BF, FREE)], [SMEM] + [HBM] * 3, [dma((6,))], "pack_ring", 1,
        info, wide_weight, narrow_weight.reshape(192, 256), point_weight,
    )[0]
    steps = [shift(dz=-1), shift(dz=2), shift(dz=1)]
    other = send(pack2, shift(dxl=1))
    own_pieces = [send(pack2, step) for step in steps]
    other_pieces = [send(other, step) for step in steps]

    line = lambda v: v.reshape(1, -1)
    pack1, packq, pack3 = call(
        pack_rest_kernel,
        [((8, SMALL + 32, 256), BF, FREE), ((8, 192, 256), BF, FREE), ((576, 256), BF, FREE)], [SMEM] + [HBM] * 14,
        [pltpu.VMEM((SMALL + 32, 256), BF), pltpu.VMEM((192, 256), BF)] + [pltpu.VMEM((1, 64), BF)] * 4
        + [pltpu.VMEM((9, 256), BF), pltpu.VMEM((1, 256), BF), dma((17,))],
        "pack_rest", 1, info, glu_value, glu_gate, query_weight, key_weight, value_weight,
        line(glu_gain), line(conv_gain), line(attn_gain), line(ffn_gain), depth_weight,
        line(mid_gain), ffn_in, ffn_out, output_weight,
    )

    pack1, *_ = lax.optimization_barrier((pack1, *own_pieces, other))
    near1 = lax.all_to_all(pack1, WT, 0, 0, tiled=True)
    packq, _ = lax.optimization_barrier((packq, near1))
    nearq = lax.all_to_all(packq, WT, 0, 0, tiled=True)
    x = inputs[0]
    low_x = send(x[rows - RIM:], along(1))
    high_x = send(x[:RIM], along(-1))
    other3 = send(pack3, shift(dxl=1))
    near1, pack3, other3, low_x, high_x, *ready = lax.optimization_barrier(
        (near1, pack3, other3, low_x, high_x, *own_pieces, *other_pieces)
    )
    near2 = [pack2] + ready[:3] + [other] + ready[3:]
    far2 = [send(piece, flip) for piece in near2]
    far1 = send(near1, flip)
    near3 = lax.all_gather(jnp.stack([pack3, other3]), "z", axis=0)

    tall, wide, narrow = (rows, width), (rows, units), (rows, 256)
    tiny = pltpu.VMEM((8, 32, 256), BF)
    ring = pltpu.VMEM((2, 2, 4) + pack2.shape, BF)
    n1, a, sg, h1, h1m = call(
        glu_kernel,
        [(tall, BF), (tall, BF), (tall, BF), ((rim_rows, width), F32, FREE), (tall, F32)],
        [SMEM] + [FREE] * 3 + [ANY] * 2, [pltpu.VMEM((2, 8, 128, 256), BF), tiny, dma((3,))], "glu", 3,
        info, low_x, x, high_x, near1, far1,
    )
    n2, wp, np_, nm, mean, scale, sp, h2, n3, two, one = call(
        conv_kernel,
        [((rim_rows, width), BF), ((rim_rows, units), F32, HBM), ((rim_rows, 256), F32),
         ((rim_rows, units), BF, HBM), ((rim_rows, 128), F32), ((rim_rows, 128), F32),
         (wide, BF, HBM), (tall, F32), (tall, BF),
         (ring.shape, BF, HBM), ((2,) + near1.shape, BF, HBM)],
        [SMEM, FREE] + [ANY] * 18,
        [ring, pltpu.VMEM((2,) + near1.shape, BF), pltpu.VMEM((rim_rows, units), F32),
         pltpu.VMEM((rim_rows, units), F32), pltpu.VMEM((rim_rows, units), BF), pltpu.VMEM(wide, BF),
         pltpu.VMEM((2, rim_rows, 128), F32), dma((16,)), dma((2,)), dma((3, 8))],
        "conv", 15, info, h1, *near2, *far2, near1, far1,
    )
    nearq, _ = lax.optimization_barrier((nearq, n3))
    qkv, wq = call(
        queries_kernel, [((HEADS, 3 * HEAD, rows), BF, FREE), ((2, 8, 192, 256), BF, HBM)],
        [SMEM, VMEM, ANY, ANY], [pltpu.VMEM((2, 8, 192, 256), BF), dma((2,))], "queries", 1,
        info, n3, nearq, send(nearq, flip),
    )
    near = lax.all_to_all(qkv, CHIPS, 0, 0, tiled=True)
    far = send(near[:, HEAD:], flip)
    head_out, expo, inverse, near, far = attend(near, far, lengths, info[:1])
    near3, _ = lax.optimization_barrier((near3, head_out))
    far3 = send(near3, flip)
    heads_in = lax.all_to_all(head_out, CHIPS, 0, 0, tiled=True)
    output, acts, g3, dob, d_gffn, heads_in = call(
        ffn_kernel,
        [(tall, BF), ((rows, 5632), BF, FREE), (tall, F32), ((HEADS, HEAD, rows), BF),
         ((1, width), F32), ((HEADS, HEAD, rows), BF, FREE)],
        [SMEM, VMEM, FREE, VMEM, HBM, HBM, ANY],
        [pltpu.VMEM((2, 2, 4) + pack3.shape, BF), tiny, pltpu.VMEM(tall, F32), pltpu.VMEM(tall, F32),
         dma((5,)), dma((4,))],
        "ffn", 11, info, h2, heads_in, cotangent[0], one, near3, far3,
    )

    d_near = lax.all_to_all(dob, CHIPS, 0, 0, tiled=True)
    early = call(
        early_kernel, [((2, 2, 4, 4, EARLY, 128), BF)], [SMEM] + [FREE] * 4, [], "early", 0.3,
        info, acts, heads_in, send(acts, flip), send(heads_in, flip),
    )[0]
    d_near, early = lax.optimization_barrier((d_near, early))
    early = over_x(early)
    keep, give = attend_back(near, far, expo, head_out, inverse, d_near)
    take = jnp.pad(send(give, flip), ((0, 0), (HEAD, 0), (0, 0)))
    d_qkv = (keep.astype(F32) + take.astype(F32)).astype(BF)
    d_qkv = lax.all_to_all(d_qkv, CHIPS, 0, 0, tiled=True)
    early = over_z(early)
    sp2, n32 = send(sp, flip), send(n3, flip)
    info_attn, _ = lax.optimization_barrier((info, sp2))
    g2, gs, lo, hi, d_gatt = call(
        attn_in_kernel,
        [(tall, F32), (narrow, BF, FREE), ((RIM, 256), BF), ((RIM, 256), BF), ((1, width), F32)],
        [SMEM, FREE] + [HBM] * 4,
        [pltpu.VMEM((2, 8, 192, 256), BF), tiny, pltpu.VMEM(tall, F32), pltpu.VMEM(tall, F32),
         dma((4,))],
        "attn_in", 0.5, info_attn, d_qkv, h2, g3, one, wq,
    )
    low_gs = send(hi, along(1))
    high_gs = send(lo, along(-1))
    info_mid, _, _ = lax.optimization_barrier((info, low_gs, high_gs))
    middle = call(
        middle_kernel, [((8, 8, MIDDLE, 128), BF)], [SMEM, VMEM, FREE, VMEM, FREE] + [FREE] * 4, [], "middle", 0.3,
        info_mid, sp, gs, n3, d_qkv, sp2, send(gs, flip), n32, send(d_qkv, flip),
    )[0]
    info_conv, middle = lax.optimization_barrier((info, middle))
    middle = lax.all_to_all(middle.reshape(64, MIDDLE, 128), CHIPS + WT, 0, 0, tiled=True)
    rim_narrow = ((rim_rows, 256), BF)
    dw, dnar, table = call(
        conv_back_kernel, [(wide, BF, FREE), ((rim_rows, 256), BF, FREE), ((16, units), F32, FREE)],
        [SMEM, FREE, FREE, FREE] + [VMEM] * 3 + [HBM] * 4,
        [pltpu.VMEM((2, 4, 256, 256), BF), tiny, pltpu.VMEM((2, rim_rows, 128), F32),
         pltpu.VMEM((2, rim_rows + 2 * RIM, 128), F32), pltpu.VMEM((rim_rows, units), F32),
         pltpu.VMEM((rim_rows, units), F32), pltpu.VMEM((rim_rows, units), BF),
         pltpu.VMEM((rim_rows, units), F32), dma((2,)), dma((2, 8))],
        "conv_back", 2, info_conv, low_gs, gs, high_gs, np_, mean, scale, nm, wp, two, one,
    )
    dw2, dnar2 = send(dw, flip), send(dnar, flip)
    info_glu, early = lax.optimization_barrier((info, early))
    dx, dab, sums = call(
        glu_back_kernel,
        [(tall, F32), ((rows, 2 * width), BF, FREE), ((24, units), F32, FREE)],
        [SMEM, FREE, FREE, HBM, HBM, HBM, VMEM, HBM, HBM, HBM, FREE, VMEM, VMEM],
        [pltpu.VMEM((2, 2, 4, 448, 256), BF), pltpu.VMEM((2, 8, 128, 256), BF), tiny,
         pltpu.VMEM((rim_rows, 256), F32), pltpu.VMEM(tall, F32), pltpu.VMEM(tall, BF),
         pltpu.VMEM(tall, BF), pltpu.VMEM(tall, BF), dma((8,))],
        "glu_back", 1, info_glu, dw, dnar, h1m, two, one, g2, a, sg, x, table, d_gatt, d_gffn,
    )
    dab2, sums2 = send(dab, flip), send(sums, flip)
    middle = jnp.sum(middle.astype(F32), 0).astype(BF)
    late = call(
        late_kernel, [((8, 8, LATE, 128), BF)], [SMEM, VMEM, FREE, FREE, VMEM, FREE, FREE] + [FREE] * 6,
        [pltpu.VMEM((rim_rows, width), F32), pltpu.VMEM((rim_rows, 256), F32)], "late", 0.5,
        info, n2, dw, dnar, n1, dab, sums, send(n2, flip), dw2, dnar2, send(n1, flip), dab2, sums2,
    )[0]
    _, early = lax.optimization_barrier((late, early))
    y = lax.axis_index("y")
    pick = lambda index: lax.dynamic_index_in_dim(early, index % 4, 0, keepdims=False)
    parts = [send(pick(y + d), shift(dy=d)) for d in (1, 2, 3)]
    early = call(
        fold_kernel, [((EARLY, 128), BF, FREE)], [FREE] * 4, [], "fold", FOLD, pick(y), *parts
    )[0]
    late = lax.all_to_all(late.reshape(64, LATE, 128), CHIPS + WT, 0, 0, tiled=True)
    late = jnp.sum(late.astype(F32), 0).astype(BF)
    final = spread_out(jnp.concatenate([early, middle, late], 0), CHIPS, 8)
    square, broad = ((64, 512), F32), ((64, 2048), F32)
    line = ((1, 64), F32)
    grads = call(
        unpack_kernel,
        [line, square, square, line, broad, ((3, 64, 256), F32), ((1, 256), F32),
         ((9, 256), F32), ((256, 256), F32), line, square, square, square, square, line, broad,
         ((256, 512), F32)],
        [SMEM, ANY, ANY],
        [pltpu.VMEM((2,) + final.shape, BF), pltpu.VMEM((512, 256), F32),
         pltpu.VMEM((256, 256), F32), pltpu.VMEM((16, 256), F32), dma((2,))],
        "unpack", 3, info, final, send(final, flip),
    )
    grads = [g[0] if g.shape[0] == 1 else g for g in grads]
    return (output[None], dx[None]) + tuple(grads)


def solution(mesh):
    fine = Mesh(mesh.devices.reshape(SIZES), AXES)
    flat, row, mid = P(WT), P(WT, None), P(None, WT, None)
    col = P(None, WT)
    tokens = P(WT, CTX, None)
    weights = (
        flat, row, row, flat, row, mid, flat, col, row, flat, row, row, row, row, flat, row, row,
    )
    return jax.shard_map(
        shards, mesh=fine, in_specs=(tokens, flat, tokens) + weights,
        out_specs=(tokens, tokens) + weights, check_vma=False,
    )
```

```python
import functools

import jax
import jax.numpy as jnp
import numpy as np
from jax import lax
from jax.experimental import pallas as pl
from jax.experimental.pallas import tpu as pltpu
from jax.sharding import Mesh
from jax.sharding import PartitionSpec as P

HEADS = 8
HEAD = 64
EPSILON = 1e-06
AXES = ("y", "xh", "core", "xl", "z")
SIZES = (4, 2, 2, 2, 4)
CTX = ("y", "xh", "core")
CHIPS = ("y", "xh")
WT = ("xl", "z")
BLOCK = 1024
LOG2E = 1.4426950408889634
BF = jnp.bfloat16
F32 = jnp.float32


def moves(target):
    pairs = []
    for source in range(int(np.prod(SIZES))):
        place = [int(v) for v in np.unravel_index(source, SIZES)]
        goal = target(*place)
        if goal is not None:
            pairs.append((source, int(np.ravel_multi_index(tuple(goal), SIZES))))
    return pairs


def shift(dy=0, dxh=0, dc=0, dxl=0, dz=0):
    return moves(
        lambda y, xh, c, xl, z: (
            (y + dy) % 4, (xh + dxh) % 2, (c + dc) % 2, (xl + dxl) % 2, (z + dz) % 4,
        )
    )


def along(step):
    def target(y, xh, c, xl, z):
        place = y * 4 + xh * 2 + c + step
        if place < 0 or place > 15:
            return None
        return (place // 4, place // 2 % 2, place % 2, xl, z)
    return moves(target)


def send(value, pairs):
    return lax.ppermute(value, AXES, pairs)


def matmul(left, right):
    return jnp.dot(left, right, preferred_element_type=F32)


def contract(left, right, ldim, rdim):
    return lax.dot_general(
        left, right, (((ldim,), (rdim,)), ((), ())), preferred_element_type=F32
    )


def smooth_unit(value):
    return value * jax.nn.sigmoid(value)


def smooth_slope(value):
    sigma = jax.nn.sigmoid(value)
    return sigma * (1.0 + value * (1.0 - sigma))


VMEM = pl.BlockSpec(memory_space=pltpu.VMEM)
SMEM = pl.BlockSpec(memory_space=pltpu.SMEM)
HBM = pl.BlockSpec(memory_space=pltpu.HBM)
ANY = pl.BlockSpec(memory_space=pl.ANY)
FREE = "free"


def attend_kernel(chips, rows, length_ref, core_ref, near_ref, far_ref, o_ref, e_ref, l_ref,
                  near_out, far_out, keys_ref, values_ref, sem):
    step = pl.program_id(0)
    span = chips * rows
    aug = 2 * HEAD
    pairs = [(near_ref, near_out), (far_ref, far_out)]

    @pl.when(step == chips - 1)
    def _():
        for i, (source, target) in enumerate(pairs):
            pltpu.make_async_copy(source, target, sem.at[i]).wait()

    @pl.when(step == 0)
    def _():
        launch(pairs, sem)
        length = length_ref[0]
        core = core_ref[0]
        ones = jnp.ones((16, rows), F32)
        for side in range(2):
            source = near_ref if side == 0 else far_ref
            base = HEAD if side == 0 else 0
            owner = core if side == 0 else 1 - core
            for chip in range(chips):
                cols = slice(side * span + chip * rows, side * span + (chip + 1) * rows)
                key = source[chip, base:base + HEAD, :]
                keys_ref[0:HEAD, cols] = key
                keys_ref[HEAD:aug, cols] = key
                place = (chip * 2 + owner) * rows + lax.broadcasted_iota(jnp.int32, (16, rows), 1)
                row = lax.broadcasted_iota(jnp.int32, (16, rows), 0)
                bias = jnp.where((place < length) | (row > 0), 0.0, -1e30)
                keys_ref[aug:aug + 16, cols] = bias.astype(BF)
                value = source[chip, base + HEAD:base + 2 * HEAD, :].astype(F32)
                stacked = jnp.concatenate([value, ones, jnp.zeros((48, rows), F32)], 0)
                values_ref[cols, :] = stacked.T.astype(BF)

    query = near_ref[step, 0:HEAD, :].astype(F32) * (LOG2E * HEAD ** -0.5)
    high = query.astype(BF)
    low = (query - high.astype(F32)).astype(BF)
    query = jnp.concatenate([high, low, jnp.ones((16, rows), BF)], 0)
    scores = contract(query, keys_ref[...], 0, 0)
    top = jnp.max(scores, 1, keepdims=True)
    expo = jnp.exp2(scores - top).astype(BF)
    e_ref[...] = expo
    out = matmul(expo, values_ref[...]).T
    inverse = 1.0 / out[HEAD:HEAD + 8]
    o_ref[0] = (out[0:HEAD] * inverse[0:1]).astype(BF)
    l_ref[0] = inverse


def attend(near, far, length, core):
    chips, _, rows = near.shape
    tokens = 2 * chips * rows
    return pl.pallas_call(
        functools.partial(attend_kernel, chips, rows),
        grid=(chips,),
        in_specs=[
            pl.BlockSpec(memory_space=pltpu.SMEM),
            pl.BlockSpec(memory_space=pltpu.SMEM),
            pl.BlockSpec(near.shape, lambda i: (0, 0, 0)),
            pl.BlockSpec(far.shape, lambda i: (0, 0, 0)),
        ],
        out_specs=[
            pl.BlockSpec((1, HEAD, rows), lambda i: (i, 0, 0)),
            pl.BlockSpec((rows, tokens), lambda i: (i, 0)),
            pl.BlockSpec((1, 8, rows), lambda i: (i, 0, 0)),
            HBM,
            HBM,
        ],
        out_shape=[
            pltpu.HBM((chips, HEAD, rows), BF),
            pltpu.HBM((chips * rows, tokens), BF),
            pltpu.HBM((chips, 8, rows), F32),
            pltpu.HBM(near.shape, BF),
            pltpu.HBM(far.shape, BF),
        ],
        scratch_shapes=[
            pltpu.VMEM((2 * HEAD + 16, tokens), BF),
            pltpu.VMEM((tokens, 2 * HEAD), BF),
            pltpu.SemaphoreType.DMA((2,)),
        ],
        compiler_params=pltpu.CompilerParams(vmem_limit_bytes=32 * 2**20),
        cost_estimate=cost(14),
        name="attend",
    )(length, core, near, far)


def attend_back_kernel(chips, rows, near_ref, far_ref, e_ref, o_ref, l_ref, do_ref,
                       keep_ref, give_ref, keys_ref, values_ref, dk_acc, dv_acc):
    step = pl.program_id(0)
    span = chips * rows

    @pl.when(step == 0)
    def _():
        row = lax.broadcasted_iota(jnp.int32, (16, rows), 0)
        ones = jnp.where(row < 3, 1.0, 0.0).astype(BF)
        for side in range(2):
            source = near_ref if side == 0 else far_ref
            base = HEAD if side == 0 else 0
            for chip in range(chips):
                cols = slice(side * span + chip * rows, side * span + (chip + 1) * rows)
                key = source[chip, base:base + HEAD, :].astype(F32)
                stacked = jnp.concatenate([key, jnp.zeros((HEAD, rows), F32)], 0)
                keys_ref[cols, :] = stacked.T.astype(BF)
                values_ref[0:HEAD, cols] = source[chip, base + HEAD:base + 2 * HEAD, :]
                values_ref[HEAD:HEAD + 16, cols] = ones
        dk_acc[...] = jnp.zeros_like(dk_acc)
        dv_acc[...] = jnp.zeros_like(dv_acc)

    inverse = l_ref[0, 0:1, :]
    grad = do_ref[0].astype(F32) * inverse
    total = -jnp.sum(grad * o_ref[0].astype(F32), 0, keepdims=True)
    high = total.astype(BF).astype(F32)
    mid = (total - high).astype(BF).astype(F32)
    low = total - high - mid
    grad_low = grad.astype(BF)
    row = lax.broadcasted_iota(jnp.int32, (16, rows), 0)
    extra = jnp.where(row == 0, high, jnp.where(row == 1, mid, jnp.where(row == 2, low, 0.0)))
    grads = jnp.concatenate([grad_low, extra.astype(BF)], 0)
    query = near_ref[step, 0:HEAD, :]
    grads = grads.T
    block = BLOCK
    dq = jnp.zeros((rows, 2 * HEAD), F32)
    for start in range(0, 2 * span, block):
        cols = slice(start, start + block)
        expo = e_ref[:, cols]
        d_scores = (expo.astype(F32) * matmul(grads, values_ref[:, cols])).astype(BF)
        dq = dq + matmul(d_scores, keys_ref[cols, :])
        dk_acc[:, cols] += matmul(query, d_scores)
        dv_acc[:, cols] += matmul(grad_low, expo)
    keep_ref[step, 0:HEAD, :] = (dq.T[0:HEAD] * HEAD ** -0.5).astype(BF)

    @pl.when(step == chips - 1)
    def _():
        for side in range(2):
            for chip in range(chips):
                cols = slice(side * span + chip * rows, side * span + (chip + 1) * rows)
                out_ref, base = (keep_ref, HEAD) if side == 0 else (give_ref, 0)
                out_ref[chip, base:base + HEAD, :] = (dk_acc[:, cols] * HEAD ** -0.5).astype(BF)
                out_ref[chip, base + HEAD:base + 2 * HEAD, :] = dv_acc[:, cols].astype(BF)


def attend_back(near, far, expo, out, inverse, d_out):
    chips, _, rows = near.shape
    tokens = 2 * chips * rows
    whole = lambda i: (0, 0, 0)
    one = lambda i: (i, 0, 0)
    return pl.pallas_call(
        functools.partial(attend_back_kernel, chips, rows),
        grid=(chips,),
        in_specs=[
            pl.BlockSpec(near.shape, whole),
            pl.BlockSpec(far.shape, whole),
            pl.BlockSpec((rows, tokens), lambda i: (i, 0)),
            pl.BlockSpec((1, HEAD, rows), one),
            pl.BlockSpec((1, 8, rows), one),
            pl.BlockSpec((1, HEAD, rows), one),
        ],
        out_specs=[pl.BlockSpec((chips, 3 * HEAD, rows), whole), pl.BlockSpec((chips, 2 * HEAD, rows), whole)],
        out_shape=[
            jax.ShapeDtypeStruct((chips, 3 * HEAD, rows), BF),
            jax.ShapeDtypeStruct((chips, 2 * HEAD, rows), BF),
        ],
        scratch_shapes=[
            pltpu.VMEM((tokens, 2 * HEAD), BF),
            pltpu.VMEM((HEAD + 16, tokens), BF),
            pltpu.VMEM((HEAD, tokens), F32),
            pltpu.VMEM((HEAD, tokens), F32),
        ],
        compiler_params=pltpu.CompilerParams(vmem_limit_bytes=32 * 2**20),
        cost_estimate=cost(3),
        name="attend_back",
    )(in_hbm(near), in_hbm(far), in_hbm(expo), in_hbm(out), in_hbm(inverse), d_out)


RIM = 8
FOLD = 0.3
ACT_N4 = slice(4096, 4608)
ACT_GY = slice(4608, 5120)
ACT_GA = slice(5120, 5632)
EARLY = 144
SMALL = 128
MIDDLE = 80
LATE = 128


def call(kernel, outs, specs, scratch, name, micros, *args):
    args = [arg if spec in (SMEM, FREE, ANY) else in_hbm(arg) for arg, spec in zip(args, specs)]
    kinds = [out[2] if len(out) > 2 else VMEM for out in outs]
    return pl.pallas_call(
        kernel,
        in_specs=[VMEM if spec is FREE else spec for spec in specs],
        out_specs=[VMEM if kind is FREE else kind for kind in kinds],
        out_shape=[
            (jax.ShapeDtypeStruct if kind is FREE else pltpu.HBM)(out[0], out[1])
            for kind, out in zip(kinds, outs)
        ],
        scratch_shapes=scratch,
        compiler_params=pltpu.CompilerParams(vmem_limit_bytes=32 * 2**20),
        cost_estimate=cost(micros),
        name=name,
    )(*args)


def in_hbm(value):
    return pltpu.with_memory_space_constraint(value, pltpu.HBM)


def cost(micros):
    return pl.CostEstimate(
        flops=int(micros * 1.0e9), bytes_accessed=int(micros * 3.0e6), transcendentals=0
    )


def launch(pairs, sems):
    copies = [
        pltpu.make_async_copy(source, target, sems.at[i]) for i, (source, target) in enumerate(pairs)
    ]
    for copy in copies:
        copy.start()
    return copies


def fetch(core, near_ref, far_ref, both_ref, sems):
    return launch([(near_ref, both_ref.at[core]), (far_ref, both_ref.at[1 - core])], sems)


def settle(copies):
    for copy in copies:
        copy.wait()


def gains_of(small_ref):
    total = small_ref[0, 0:16, :].astype(F32)
    for w in range(1, 8):
        total = total + small_ref[w, 0:16, :].astype(F32)
    return jnp.concatenate([total[0:8], total[8:16]], 1)


def taps_of(small_ref, index):
    small = small_ref[index, 16:32, :].astype(F32)
    return small[0:9], small[9:10]


def normal_of(value):
    average = jnp.mean(value, -1, keepdims=True)
    centred = value - average
    scale = lax.rsqrt(jnp.mean(centred * centred, -1, keepdims=True) + EPSILON)
    return centred * scale, scale


def back_of(incoming, normal, scale, gain):
    scaled = incoming * gain
    return scale * (
        scaled
        - jnp.mean(scaled, -1, keepdims=True)
        - normal * jnp.mean(scaled * normal, -1, keepdims=True)
    )


def column_sum(value):
    return jnp.sum(value, 0, keepdims=True)


def mask_of(info_ref, count, before):
    place = info_ref[1] - before + lax.broadcasted_iota(jnp.int32, (count, 1), 0)
    return jnp.where((place >= 0) & (place < info_ref[2]), 1.0, 0.0)


def block_cols(index, size=256):
    return pl.ds(pl.multiple_of(index * size, size), size)


def upper_block(both_ref, index):
    rows = pl.ds(pl.multiple_of(lax.rem(index, 4) * 64, 64), 64)
    if len(both_ref.shape) == 5:
        return both_ref[lax.div(index, 4), :, :, rows, :].reshape(512, 256)
    return both_ref[lax.div(index, 4), :, rows, :].reshape(512, 256)


def narrow_block(both_ref, tap):
    return both_ref[0, :, :, 256 + 64 * tap:320 + 64 * tap, :].reshape(512, 256)


def point_block(both_ref, index):
    return both_ref[1, lax.div(index, 4), lax.rem(index, 4), 256:512, :]


def collect(info_ref, near_refs, far_refs, both_ref, sems, rows=slice(0, 512)):
    core, x, z = info_ref[0], info_ref[5], info_ref[4]
    copies = []
    for side, refs in ((core, near_refs), (1 - core, far_refs)):
        for i, ref in enumerate(refs):
            place = x if i < 4 else 1 - x
            target = both_ref.at[side, place, lax.rem(z + i % 4, 4), rows]
            copies.append((ref.at[rows], target))
    return launch(copies, sems)


def glu_of(both_ref, side):
    return jnp.concatenate(
        [both_ref[side, :, 64 * i:64 * i + 64, :].reshape(512, 256) for i in range(2)], 1
    )


def queries_of(both_ref, side, part):
    return both_ref[side, :, 64 * part:64 * part + 64, :].reshape(512, 256)


def small_pair(one_ref, small_ref):
    return (one_ref.at[0, :, SMALL:SMALL + 32, :], small_ref)


def glu_kernel(info_ref, low_ref, x_ref, high_ref, near_ref, far_ref, n1_ref, a_ref, sg_ref, h1_ref,
               main_ref, w_ref, small_ref, sem):
    rows = x_ref.shape[0]
    main = slice(RIM, RIM + rows)
    core = info_ref[0]
    copies = launch(
        [(near_ref.at[:, SMALL:SMALL + 32, :], small_ref), (near_ref.at[:, 0:128, :], w_ref.at[core]),
         (far_ref.at[:, 0:128, :], w_ref.at[1 - core])], sem
    )
    x = jnp.concatenate(
        [low_ref[...].astype(F32), x_ref[...].astype(F32), high_ref[...].astype(F32)], 0
    )
    normal, _ = normal_of(x)
    settle(copies)
    normed = normal * gains_of(small_ref)[0:1]
    n1 = normed.astype(BF)
    n1_ref[...] = normed[main].astype(BF)
    a = matmul(n1, glu_of(w_ref, 0))
    sg = jax.nn.sigmoid(matmul(n1, glu_of(w_ref, 1)))
    a_ref[...] = a[main].astype(BF)
    sg_ref[...] = sg[main].astype(BF)
    h1 = x + a * sg
    h1_ref[...] = h1
    main_ref[...] = h1[main]


def conv_kernel(info_ref, h1_ref, *refs):
    near2, far2, rest = refs[0:8], refs[8:16], refs[16:]
    conv_body(info_ref, h1_ref, near2, far2, *rest)


def conv_body(info_ref, h1_ref, near2, far2, near1_ref, far1_ref,
              n2_ref, wp_out, np_ref, nm_out, mean_ref, scale_ref, sp_out, h2_ref, n3_ref,
              two_ref, one_ref, w2_ref, w1_ref, mix_ref, wp_ref, nm_ref, sp_ref, slab_ref,
              sem2, semq, sems):
    core = info_ref[0]
    rim_rows = h1_ref.shape[0]
    rows = rim_rows - 2 * RIM
    copiesq = fetch(core, near1_ref, far1_ref, w1_ref, semq)
    copies2 = collect(info_ref, near2, far2, w2_ref, sem2)
    small_ref = w1_ref.at[0, :, SMALL:SMALL + 32, :]
    settle(copiesq)
    copiesq = launch([(w1_ref, one_ref)], semq)

    def leaving(which, index):
        source, target = ((wp_ref, wp_out), (nm_ref, nm_out), (sp_ref, sp_out))[which]
        cols = block_cols(index)
        return pltpu.make_async_copy(source.at[:, cols], target.at[:, cols], sems.at[which, index])

    gains = gains_of(small_ref)
    valid = mask_of(info_ref, rim_rows, RIM)
    normal, _ = normal_of(h1_ref[...])
    n2f = normal * gains[1:2] * valid
    n2 = n2f.astype(BF)
    n2_ref[...] = n2
    n2f = n2.astype(F32)
    settle(copies2)
    copies2 = launch([(w2_ref, two_ref)], sem2)
    narrow = jnp.zeros((rim_rows, 256), F32)
    for tap in range(3):
        if tap == 1:
            moved = n2
        else:
            moved = pltpu.roll(n2f, 1 if tap == 0 else rim_rows - 1, 0).astype(BF)
        narrow = narrow + matmul(moved, narrow_block(w2_ref, tap))
    np_ref[...] = narrow
    narrow = smooth_unit(narrow)

    def first_pass(index, total):
        weights = jnp.concatenate([upper_block(w2_ref, 2 * index + i) for i in range(2)], 1)
        wide = matmul(n2_ref[...], weights)
        wp_ref[:, block_cols(index, 512)] = wide
        for i in range(2):
            leaving(0, 2 * index + i).start()
        mixed = smooth_unit(wide)
        head = mixed[:, 0:256] + narrow * jnp.where(index == 0, 1.0, 0.0)
        mixed = jnp.concatenate([head, mixed[:, 256:512]], 1)
        mix_ref[:, block_cols(index, 512)] = mixed
        return total + jnp.sum(mixed, -1, keepdims=True)

    total = lax.fori_loop(0, 4, first_pass, jnp.zeros((rim_rows, 1), F32))
    mean = total * (1.0 / 2048)

    total = jnp.zeros((rim_rows, 1), F32)
    for index in range(8):
        centred = mix_ref[:, 256 * index:256 * index + 256] - mean
        total = total + jnp.sum(centred * centred, -1, keepdims=True)
    scale = lax.rsqrt(total * (1.0 / 2048) + EPSILON)
    mean_ref[...] = jnp.broadcast_to(mean, mean_ref.shape)
    scale_ref[...] = jnp.broadcast_to(scale, scale_ref.shape)
    h2_ref[...] = h1_ref[RIM:RIM + rows, :]

    def third_pass(index, carry):
        cols = block_cols(index)
        taps, gain = taps_of(small_ref, index)
        nm = ((mix_ref[:, cols] - mean) * scale * gain * valid).astype(BF)
        nm_ref[:, cols] = nm
        leaving(1, index).start()
        nm = nm.astype(F32)
        halves = []
        for half in range(2):
            lanes = slice(128 * half, 128 * half + 128)
            slab_ref[half] = nm[:, lanes]
            spread = jnp.zeros((rows, 128), F32)
            for tap in range(9):
                spread = spread + slab_ref[half, 4 + tap:4 + tap + rows, :] * taps[tap:tap + 1, lanes]
            halves.append(spread)
        spread = jnp.concatenate(halves, 1).astype(BF)
        sp_ref[:, cols] = spread
        leaving(2, index).start()
        h2_ref[:, 0:256] += matmul(spread, point_block(w2_ref, index))
        return carry

    lax.fori_loop(0, 8, third_pass, 0, unroll=2)
    normal, _ = normal_of(h2_ref[...])
    n3 = (normal * gains[2:3]).astype(BF)
    n3_ref[...] = n3
    settle(copies2 + copiesq)
    for which in range(3):
        for index in range(8):
            leaving(which, index).wait()


def queries_kernel(info_ref, n3_ref, near_ref, far_ref, qkv_ref, wq_out, w_ref, sem):
    rows = n3_ref.shape[0]
    settle(fetch(info_ref[0], near_ref, far_ref, w_ref, sem))
    copies = launch([(w_ref, wq_out)], sem)
    for part in range(3):
        for side in range(2):
            block = matmul(n3_ref[...], queries_of(w_ref, side, part))
            qkv_ref[4 * side:4 * side + 4, 64 * part:64 * part + 64, :] = (
                block.T.astype(BF).reshape(4, 64, rows)
            )
    settle(copies)


def ffn_kernel(info_ref, h2_ref, o_ref, cot_ref, one_ref, near_ref, far_ref,
               out_ref, acts_ref, g3_ref, dob_ref, gain_ref, heads_ref,
               w_ref, small_ref, y_ref, dn_ref, sem, sem_later):
    rows = h2_ref.shape[0]
    core = info_ref[0]
    x = info_ref[5]
    pairs, later = [small_pair(one_ref, small_ref)], []
    for side, ref in ((core, near_ref), (1 - core, far_ref)):
        for rel, place in ((0, x), (1, 1 - x)):
            pairs.append((ref.at[:, rel, 512:576, :], w_ref.at[side, place, :, 512:576, :]))
            later.append((ref.at[:, rel, 0:512, :], w_ref.at[side, place, :, 0:512, :]))
    copies = launch(pairs, sem)
    later = launch(later, sem_later)
    valid = mask_of(info_ref, rows, 0)
    heads_ref[...] = o_ref[...]
    heads = o_ref[...].reshape(512, rows)
    gy = (cot_ref[...].astype(F32) * valid).astype(BF)
    acts_ref[:, ACT_GY] = gy
    settle(copies)
    gains = gains_of(small_ref)
    outs = [w_ref[side, :, :, 512:576, :].reshape(512, 256) for side in range(2)]
    h3 = h2_ref[...] + jnp.concatenate([contract(heads, outs[side], 0, 0) for side in range(2)], 1)
    normal, scale = normal_of(h3)
    acts_ref[:, ACT_N4] = (normal * gains[3:4]).astype(BF)
    y_ref[...] = h3
    dn_ref[...] = jnp.zeros_like(dn_ref)

    settle(later)
    gy0, gy1 = acts_ref[:, 4608:4864], acts_ref[:, 4864:5120]

    def step(index, carry):
        upper = jnp.concatenate([upper_block(w_ref, 2 * index + i) for i in range(2)], 1)
        lower = []
        for side in range(2):
            blocks = [2 * index + i for i in range(2)]
            blocks = [w_ref[side, lax.div(k, 4), lax.rem(k, 4), 256:512, :] for k in blocks]
            lower.append(jnp.concatenate(blocks, 0))
        u = matmul(acts_ref[:, ACT_N4], upper)
        sigma = jax.nn.sigmoid(u)
        r = (u * sigma).astype(BF)
        acts_ref[:, block_cols(index, 512)] = r
        dr = contract(gy0, lower[0], 1, 1) + contract(gy1, lower[1], 1, 1)
        du = (dr * (sigma * (1.0 + u * (1.0 - sigma)))).astype(BF)
        acts_ref[:, block_cols(index + 4, 512)] = du
        y_ref[:, 0:256] += matmul(r, lower[0])
        y_ref[:, 256:512] += matmul(r, lower[1])
        dn_ref[...] += contract(du, upper, 1, 1)
        return carry

    lax.fori_loop(0, 4, step, 0)
    out_ref[...] = (y_ref[...] * valid).astype(BF)
    dn = dn_ref[...]
    gain_ref[...] = column_sum(dn * normal)
    g3 = gy.astype(F32) + back_of(dn, normal, scale, gains[3:4])
    g3_ref[...] = g3
    ga = g3.astype(BF)
    acts_ref[:, ACT_GA] = ga
    dob = contract(outs[0], ga[:, 0:256], 1, 1) + contract(outs[1], ga[:, 256:512], 1, 1)
    dob_ref[...] = dob.astype(BF).reshape(HEADS, HEAD, rows)


def pair_rows(value):
    split = value.reshape(8, 8, 8, 256)
    return jnp.concatenate([split[..., 0:128], split[..., 128:256]], 2)


FULL = slice(None)


def by_chip(out_ref, c, rows, value):
    out_ref[c % 2, :, :, c // 2, rows, :] = value.astype(BF).reshape((2, 4) + value.shape[1:])


def by_shard(out_ref, w, rows, value):
    value = value.astype(BF).reshape((4, 2) + value.shape[1:])
    for xh in range(2):
        out_ref[xh, w // 4, w % 4, :, rows, :] = value[:, xh]


def stack_rows(*pieces):
    return jnp.concatenate(pieces, 0)


def early_kernel(info_ref, acts_ref, heads_ref, acts2_ref, heads2_ref, out_ref):
    rows = acts_ref.shape[0]
    side = info_ref[0]

    def tokens(cols):
        return stack_rows(acts_ref[:, cols], acts2_ref[:, cols])

    n4 = tokens(ACT_N4).T
    for j in range(4):
        res = matmul(n4, tokens(block_cols(side * 4 + j + 8)))
        for i in range(2):
            by_chip(out_ref, 2 * j + i, slice(0, 64), res[:, 128 * i:128 * i + 128].reshape(8, 64, 128))
    gy = tokens(block_cols(side + 18)).T
    for w in range(8):
        res = matmul(gy, tokens(slice(256 * w, 256 * w + 256))).reshape(8, 32, 256)
        for i in range(2):
            by_shard(out_ref, w, slice(64 + 32 * i, 96 + 32 * i), res[:, :, 128 * i:128 * i + 128])
    heads = jnp.concatenate([heads_ref[...].reshape(512, rows), heads2_ref[...].reshape(512, rows)], 1)
    packed = pair_rows(matmul(heads, tokens(block_cols(side + 20))))
    for c in range(8):
        by_chip(out_ref, c, slice(128, 144), packed[:, c])


def attn_in_kernel(info_ref, d_ref, h2_in, g3_in, one_ref, wq_ref,
                   g2_ref, gs_ref, lo_ref, hi_ref, gain_ref, w_ref, small_ref, h2_ref, g3_ref, sem):
    rows = h2_ref.shape[0]
    copies = launch(
        [(h2_in, h2_ref), small_pair(one_ref, small_ref), (wq_ref, w_ref),
         (g3_in, g3_ref)], sem
    )
    settle(copies[:1])
    normal, scale = normal_of(h2_ref[...])
    settle(copies[1:])
    gains = gains_of(small_ref)
    parts = [(part, side) for part in range(3) for side in range(2)]
    blocks = [
        d_ref[4 * side:4 * side + 4, 64 * part:64 * part + 64, :].reshape(256, rows) for part, side in parts
    ]
    weights = [queries_of(w_ref, side, part) for part, side in parts]
    dn = contract(stack_rows(*blocks).T, jnp.concatenate(weights, 1), 1, 1)
    gain_ref[...] = column_sum(dn * normal)
    g2 = g3_ref[...] + back_of(dn, normal, scale, gains[2:3])
    g2_ref[...] = g2
    gs = g2[:, 0:256]
    gs_ref[...] = gs.astype(BF)
    lo_ref[...] = gs[0:RIM].astype(BF)
    hi_ref[...] = gs[rows - RIM:rows].astype(BF)


def conv_back_kernel(info_ref, lo_ref, gs_ref, hi_ref, np_ref, mean_ref, scale_ref, nm_in, wp_in,
                     two_ref, one_ref, dw_ref, dnar_ref, table_ref, pt_ref, small_ref, nmf_ref,
                     dsp_ref, sc_ref, hat_ref, nm_ref, wp_ref, sem, sems):
    rim_rows = wp_ref.shape[0]
    rows = rim_rows - 2 * RIM
    main = slice(RIM, RIM + rows)
    copies = launch(
        [small_pair(one_ref, small_ref), (two_ref.at[1, :, :, 256:512, :], pt_ref)], sem
    )

    def arriving(which, index):
        source, target = ((nm_in, nm_ref), (wp_in, wp_ref))[which]
        cols = block_cols(index)
        return pltpu.make_async_copy(source.at[:, cols], target.at[:, cols], sems.at[which, index])

    for index in range(8):
        for which in range(2):
            arriving(which, index).start()
    valid = mask_of(info_ref, rim_rows, RIM)
    gs = jnp.concatenate(
        [lo_ref[...].astype(F32), gs_ref[...].astype(F32), hi_ref[...].astype(F32)], 0
    ).astype(BF)
    mean = mean_ref[:, 0:1]
    scale = scale_ref[:, 0:1]
    table_ref[...] = jnp.zeros_like(table_ref)
    dsp_ref[:, 0:RIM, :] = jnp.zeros((2, RIM, 128), F32)
    dsp_ref[:, RIM + rim_rows:, :] = jnp.zeros((2, RIM, 128), F32)
    settle(copies)

    def first_pass(index, carry):
        one, two = carry
        cols = block_cols(index)
        taps, gain = taps_of(small_ref, index)
        arriving(0, index).wait()
        arriving(1, index).wait()
        dsp = contract(gs, pt_ref[lax.div(index, 4), lax.rem(index, 4)], 1, 1).astype(BF).astype(F32)
        nm = nm_ref[:, cols].astype(F32)
        halves = []
        sums = []
        for half in range(2):
            lanes = slice(128 * half, 128 * half + 128)
            dsp_ref[half, RIM:RIM + rim_rows, :] = dsp[:, lanes]
            nmf_ref[half] = nm[:, lanes]
            inner = dsp[main, lanes]
            dn = jnp.zeros((rim_rows, 128), F32)
            parts = []
            for tap in range(9):
                dn = dn + dsp_ref[half, 12 - tap:12 - tap + rim_rows, :] * taps[tap:tap + 1, lanes]
                parts.append(column_sum(nmf_ref[half, 4 + tap:4 + tap + rows, :] * inner))
            halves.append(dn)
            sums.append(jnp.concatenate(parts, 0))
        table_ref[0:9, cols] = jnp.concatenate(sums, 1)
        dn = jnp.concatenate(halves, 1) * valid
        mixed = smooth_unit(wp_ref[:, cols]) + smooth_unit(np_ref[...]) * jnp.where(index == 0, 1.0, 0.0)
        hat = (mixed - mean) * scale
        hat_ref[:, cols] = hat
        table_ref[9:10, cols] = column_sum((dn * hat)[main])
        scaled = dn * gain
        sc_ref[:, cols] = scaled
        return (one + jnp.sum(scaled, -1, keepdims=True),
                two + jnp.sum(scaled * hat, -1, keepdims=True))

    zero = jnp.zeros((rim_rows, 1), F32)
    one, two = lax.fori_loop(0, 8, first_pass, (zero, zero))
    one = one * (1.0 / 2048)
    two = two * (1.0 / 2048)
    back = scale * (sc_ref[:, 0:256] - one - hat_ref[:, 0:256] * two)
    dnar_ref[...] = (back * smooth_slope(np_ref[...])).astype(BF)

    def second_pass(index, carry):
        cols = block_cols(index)
        back = scale[main] * (
            sc_ref[main, cols] - one[main] - hat_ref[main, cols] * two[main]
        )
        dw_ref[:, cols] = (back * smooth_slope(wp_ref[main, cols])).astype(BF)
        return carry

    lax.fori_loop(0, 8, second_pass, 0)


def glu_back_kernel(info_ref, dw_ref, dnar_ref, h1_in, two_ref, one_ref, g2_ref,
                    a_in, sg_in, x_in, table_ref, gattn_ref, gffn_ref, dx_ref, dab_ref, sums_ref,
                    w2_ref, w1_ref, small_ref, nar_ref, h1_ref, a_ref, sg_ref, x_ref, sem):
    rows = g2_ref.shape[0]
    first = launch([(h1_in, h1_ref)], sem)
    copies = launch(
        [(two_ref.at[0, :, :, 0:448, :], w2_ref.at[0]),
         (two_ref.at[1, :, :, 0:256, :], w2_ref.at[1, :, :, 0:256, :])], sem.at[1:3]
    )
    copies1 = launch(
        [small_pair(one_ref, small_ref), (one_ref.at[:, :, 0:128, :], w1_ref), (a_in, a_ref),
         (sg_in, sg_ref), (x_in, x_ref)], sem.at[3:8]
    )
    valid = mask_of(info_ref, rows, 0)
    nar_ref[...] = dnar_ref[...].astype(F32)
    settle(first)
    normal, scale1 = normal_of(h1_ref[...])
    moved = jnp.concatenate([nar_ref[9 - tap:9 - tap + rows, :].astype(BF) for tap in range(3)], 1)
    dn = jnp.zeros((rows, 512), F32)
    for side in range(2):
        copies[side].wait()
        weights = [w2_ref[side, :, :, 64 * j:64 * j + 64, :].reshape(512, 256) for j in range(4)]
        dn = dn + contract(dw_ref[:, 1024 * side:1024 * side + 1024], jnp.concatenate(weights, 1), 1, 1)
        if side == 0:
            weights = jnp.concatenate([narrow_block(w2_ref, tap) for tap in range(3)], 1)
            dn = dn + contract(moved, weights, 1, 1)
    settle(copies1)
    gains = gains_of(small_ref)
    dn = dn * valid
    gconv = column_sum(dn * normal)
    g1 = g2_ref[...] + back_of(dn, normal, scale1, gains[1:2])
    sg = sg_ref[...].astype(F32)
    da = (g1 * sg).astype(BF)
    db = (g1 * a_ref[...].astype(F32) * sg * (1.0 - sg)).astype(BF)
    dab_ref[:, 0:512] = da
    dab_ref[:, 512:1024] = db
    sums_ref[0:16, :] = table_ref[...]
    sums_ref[16:24, :] = jnp.zeros((8, 2048), F32)
    sums_ref[17:18, 0:512] = gconv
    sums_ref[18:19, 0:512] = gattn_ref[...]
    sums_ref[19:20, 0:512] = gffn_ref[...]
    dn = contract(da, glu_of(w1_ref, 0), 1, 1) + contract(db, glu_of(w1_ref, 1), 1, 1)
    normal, scale0 = normal_of(x_ref[...].astype(F32))
    sums_ref[16:17, 0:512] = column_sum(dn * normal)
    dx_ref[...] = g1 + back_of(dn, normal, scale0, gains[0:1])


def middle_kernel(info_ref, sp_ref, gs_ref, n3_ref, d_ref, sp2_ref, gs2_ref, n32_ref, d2_ref, out_ref):
    rows = gs_ref.shape[0]
    side = info_ref[0]
    gs = stack_rows(gs_ref[:, block_cols(side, 128)], gs2_ref[:, block_cols(side, 128)]).T
    for w in range(8):
        cols = slice(256 * w, 256 * w + 256)
        res = matmul(gs, stack_rows(sp_ref[:, cols], sp2_ref[:, cols])).reshape(8, 16, 256)
        for i in range(2):
            out_ref[:, w, 16 * i:16 * i + 16, :] = res[:, :, 128 * i:128 * i + 128].astype(BF)
    n3 = stack_rows(n3_ref[...], n32_ref[...]).T
    for part in range(3):
        d = [ref[pl.ds(side * 4, 4), 64 * part:64 * part + 64, :].reshape(256, rows) for ref in (d_ref, d2_ref)]
        packed = pair_rows(contract(n3, jnp.concatenate(d, 1), 1, 1)).astype(BF)
        for w in range(8):
            out_ref[:, w, 32 + 16 * part:48 + 16 * part, :] = packed[w]


def late_kernel(info_ref, n2_ref, dw_ref, dnar_ref, n1_ref, dab_ref, small_ref, n22_ref, dw2_ref,
                dnar2_ref, n12_ref, dab2_ref, small2_ref, out_ref, n2f_ref, narf_ref):
    rows = dw_ref.shape[0]
    side = info_ref[0]
    shifted = []
    dnar = []
    for n_ref, d_ref in ((n2_ref, dnar_ref), (n22_ref, dnar2_ref)):
        n2f_ref[...] = n_ref[...].astype(F32)
        narf_ref[...] = d_ref[...].astype(F32)
        shifted.append([n2f_ref[7 + tap:7 + tap + rows, :].astype(BF) for tap in range(3)])
        dnar.append(narf_ref[RIM:RIM + rows, block_cols(side, 128)].astype(BF))
    shifted = [stack_rows(*pair).T for pair in zip(*shifted)]
    dnar = stack_rows(*dnar)
    for j in range(4):
        cols = block_cols(side * 4 + j)
        res = matmul(shifted[1], stack_rows(dw_ref[:, cols], dw2_ref[:, cols]))
        for i in range(2):
            part = res[:, 128 * i:128 * i + 128].reshape(8, 64, 128)
            out_ref[2 * j + i, :, 0:64, :] = part.astype(BF)
    narrow = [matmul(piece, dnar) for piece in shifted]
    for w in range(8):
        lanes = pl.ds(pl.multiple_of(w * 256 + side * 128, 128), 128)
        pair = slice(128 * (w // 2), 128 * (w // 2) + 128)
        table = small_ref[0:16, lanes] + small2_ref[0:16, lanes]
        gains = small_ref[16:20, pair] + small2_ref[16:20, pair]
        table = jnp.concatenate([table[0:10], gains, table[14:16]], 0)
        for c in range(8):
            pieces = [n[64 * w + 8 * c:64 * w + 8 * c + 8] for n in narrow]
            pieces += [table[2 * c:2 * c + 2], jnp.zeros((6, 128), F32)]
            out_ref[c, w, 64:96, :] = jnp.concatenate(pieces, 0).astype(BF)
    n1 = stack_rows(n1_ref[...], n12_ref[...]).T
    for place in range(2):
        cols = block_cols(side + 2 * place)
        packed = pair_rows(matmul(n1, stack_rows(dab_ref[:, cols], dab2_ref[:, cols]))).astype(BF)
        for w in range(8):
            out_ref[:, w, 96 + 16 * place:112 + 16 * place, :] = packed[w]


def unpack_kernel(info_ref, near_ref, far_ref, gglu_ref, val_ref, gat_ref, gconv_ref, wid_ref, nar_ref,
                  gmid_ref, dep_ref, pnt_ref, gatt_ref, qry_ref, key_ref, vls_ref, outp_ref,
                  gffn_ref, upper_ref, lower_ref, fin_ref, low_ref, pt_ref, table_ref, sem):
    settle(fetch(info_ref[0], near_ref, far_ref, fin_ref, sem))
    for c in range(8):
        for k in range(2):
            fin = fin_ref[k, c].astype(F32)
            lanes = slice(k * 1024 + c * 128, k * 1024 + c * 128 + 128)
            upper_ref[:, lanes] = fin[0:64]
            wid_ref[:, lanes] = fin[EARLY + MIDDLE:EARLY + MIDDLE + 64]
            middle = EARLY
            late = EARLY + MIDDLE
            for i in range(2):
                low_ref[k * 256 + c * 32:k * 256 + c * 32 + 32, 128 * i:128 * i + 128] = (
                    fin[64 + 32 * i:96 + 32 * i]
                )
                pt_ref[k * 128 + c * 16:k * 128 + c * 16 + 16, 128 * i:128 * i + 128] = (
                    fin[middle + 16 * i:middle + 16 * i + 16]
                )
            for tap in range(3):
                nar_ref[tap, 8 * c:8 * c + 8, 128 * k:128 * k + 128] = (
                    fin[late + 64 + 8 * tap:late + 72 + 8 * tap]
                )
            table_ref[2 * c:2 * c + 2, 128 * k:128 * k + 128] = fin[late + 88:late + 90]
            bases = [128] + [middle + 32 + 16 * i for i in range(3)] + [late + 96, late + 112]
            targets = [outp_ref, qry_ref, key_ref, vls_ref, val_ref, gat_ref]
            for base, target in zip(bases, targets):
                for i in range(2):
                    target[8 * c:8 * c + 8, k * 256 + 128 * i:k * 256 + 128 * i + 128] = (
                        fin[base + 8 * i:base + 8 * i + 8]
                    )
    lower_ref[...] = low_ref[...].T
    pnt_ref[...] = pt_ref[...].T
    dep_ref[...] = table_ref[0:9, :]
    gmid_ref[...] = table_ref[9:10, :]
    even = info_ref[3] == 0
    gains = jnp.where(even, table_ref[10:14, 0:64], table_ref[10:14, 64:128])
    gglu_ref[...] = gains[0:1]
    gconv_ref[...] = gains[1:2]
    gatt_ref[...] = gains[2:3]
    gffn_ref[...] = gains[3:4]


def pack_ring_kernel(info_ref, wide_ref, narrow_ref, point_ref, out_ref, sem):
    core = info_ref[0]
    pairs = [
        (wide_ref.at[:, block_cols(core * 4 + j)], out_ref.at[64 * j:64 * j + 64, :]) for j in range(4)
    ]
    copies = launch(pairs, sem)

    @pl.when(core == 0)
    def _():
        settle(launch([(narrow_ref, out_ref.at[256:448, :]),
                       (narrow_ref.at[0:64, :], out_ref.at[448:512, :])], sem.at[4:6]))

    @pl.when(core == 1)
    def _():
        settle(launch([(point_ref, out_ref.at[256:512, :])], sem.at[4:5]))

    settle(copies)


def pack_rest_kernel(info_ref, value_ref, gate_ref, query_ref, key_ref, values_ref, g0_ref, g1_ref,
                     g2_ref, g3_ref, depth_ref, mid_ref, in_ref, out_ref, outw_ref, one_ref,
                     q_ref, three_ref, pack_ref, packq_ref, g0, g1, g2, g3, depth, mid, sem):
    core = info_ref[0]
    own = block_cols(core)
    small = [(g0_ref, g0), (g1_ref, g1), (g2_ref, g2), (g3_ref, g3), (depth_ref, depth), (mid_ref, mid)]
    small = launch(small, sem)
    weights = launch(
        [(ref.at[:, own], packq_ref.at[64 * i:64 * i + 64, :])
         for i, ref in enumerate((query_ref, key_ref, values_ref))], sem.at[6:9],
    )
    later = [(in_ref.at[:, block_cols(core * 4 + j)], three_ref.at[64 * j:64 * j + 64, :]) for j in range(4)]
    later += [(out_ref.at[:, own], three_ref.at[256:512, :]), (outw_ref.at[:, own], three_ref.at[512:576, :])]
    later = launch(later, sem.at[9:15])
    for index, ref in ((0, value_ref), (1, gate_ref)):
        @pl.when(core == index)
        def _():
            settle(launch([(ref.at[:, 256 * i:256 * i + 256], pack_ref.at[64 * i:64 * i + 64, :])
                           for i in range(2)], sem.at[15:17]))
    settle(small)
    gains = jnp.concatenate(
        [ref[...].astype(F32) for ref in (g0, g1, g2, g3)] + [jnp.zeros((4, 64), F32)], 0
    )
    gains = jnp.concatenate([gains] * 8, 1)
    place = lax.broadcasted_iota(jnp.int32, (8, 512), 1)
    start = (info_ref[5] * 4 + info_ref[4]) * 64
    gains = jnp.where((place >= start) & (place < start + 64), gains, 0.0)
    gains = jnp.concatenate([gains[:, 0:256], gains[:, 256:512]], 0)
    pack_ref[SMALL:SMALL + 16, :] = gains.astype(BF)
    taps = jnp.concatenate([depth[...].astype(F32), mid[...].astype(F32), jnp.zeros((6, 256), F32)], 0)
    pack_ref[SMALL + 16:SMALL + 32, :] = taps.astype(BF)
    settle(weights)
    for w in range(8):
        one_ref[w] = pack_ref[...]
        q_ref[w] = packq_ref[...]
    settle(later)


def fold_kernel(*refs):
    total = refs[0][...].astype(F32)
    for ref in refs[1:4]:
        total = total + ref[...].astype(F32)
    refs[4][...] = total.astype(BF)


def over_x(value):
    value = value.reshape((4,) + value.shape[2:])
    return lax.psum_scatter(value, ("xh", "xl"), scatter_dimension=0, tiled=True)[0]


def over_z(value):
    return lax.psum_scatter(value, "z", scatter_dimension=0, tiled=True)[0]


def spread_out(own, axes, count):
    copies = jnp.broadcast_to(own[None], (count,) + own.shape)
    return lax.all_to_all(copies, axes, 0, 0, tiled=True)


def shards(
    inputs, lengths, cotangent, glu_gain, glu_value, glu_gate, conv_gain, wide_weight,
    narrow_weight, mid_gain, depth_weight, point_weight, attn_gain, query_weight, key_weight,
    value_weight, output_weight, ffn_gain, ffn_in, ffn_out,
):
    rows, width = inputs.shape[1], inputs.shape[2]
    units = wide_weight.shape[1]
    rim_rows = rows + 2 * RIM
    core = lax.axis_index("core")
    shard = lax.axis_index("xl") * 4 + lax.axis_index("z")
    first = (lax.axis_index("y") * 4 + lax.axis_index("xh") * 2 + core) * rows
    xl, z = lax.axis_index("xl"), lax.axis_index("z")
    info = jnp.stack([core, first, lengths[0], shard % 2, z, xl]).astype(jnp.int32)
    flip = shift(dc=1)
    dma = pltpu.SemaphoreType.DMA

    pack2 = call(
        pack_ring_kernel, [((512, 256), BF, FREE)], [SMEM] + [HBM] * 3, [dma((6,))], "pack_ring", 1,
        info, wide_weight, narrow_weight.reshape(192, 256), point_weight,
    )[0]
    steps = [shift(dz=-1), shift(dz=2), shift(dz=1)]
    other = send(pack2, shift(dxl=1))
    own_pieces = [send(pack2, step) for step in steps]
    other_pieces = [send(other, step) for step in steps]

    line = lambda v: v.reshape(1, -1)
    pack1, packq, pack3 = call(
        pack_rest_kernel,
        [((8, SMALL + 32, 256), BF, FREE), ((8, 192, 256), BF, FREE), ((576, 256), BF, FREE)], [SMEM] + [HBM] * 14,
        [pltpu.VMEM((SMALL + 32, 256), BF), pltpu.VMEM((192, 256), BF)] + [pltpu.VMEM((1, 64), BF)] * 4
        + [pltpu.VMEM((9, 256), BF), pltpu.VMEM((1, 256), BF), dma((17,))],
        "pack_rest", 1, info, glu_value, glu_gate, query_weight, key_weight, value_weight,
        line(glu_gain), line(conv_gain), line(attn_gain), line(ffn_gain), depth_weight,
        line(mid_gain), ffn_in, ffn_out, output_weight,
    )

    pack1, *_ = lax.optimization_barrier((pack1, *own_pieces, other))
    near1 = lax.all_to_all(pack1, WT, 0, 0, tiled=True)
    packq, _ = lax.optimization_barrier((packq, near1))
    nearq = lax.all_to_all(packq, WT, 0, 0, tiled=True)
    x = inputs[0]
    low_x = send(x[rows - RIM:], along(1))
    high_x = send(x[:RIM], along(-1))
    other3 = send(pack3, shift(dxl=1))
    near1, shards3, low_x, high_x, *ready = lax.optimization_barrier(
        (near1, jnp.stack([pack3, other3]), low_x, high_x, *own_pieces, *other_pieces)
    )
    near2 = [pack2] + ready[:3] + [other] + ready[3:]
    far2 = [send(piece, flip) for piece in near2]
    far1 = send(near1, flip)
    near3 = lax.all_gather(shards3, "z", axis=0)

    tall, wide, narrow = (rows, width), (rows, units), (rows, 256)
    tiny = pltpu.VMEM((8, 32, 256), BF)
    ring = pltpu.VMEM((2, 2, 4) + pack2.shape, BF)
    n1, a, sg, h1, h1m = call(
        glu_kernel,
        [(tall, BF), (tall, BF), (tall, BF), ((rim_rows, width), F32, FREE), (tall, F32)],
        [SMEM] + [FREE] * 3 + [ANY] * 2, [pltpu.VMEM((2, 8, 128, 256), BF), tiny, dma((3,))], "glu", 3,
        info, low_x, x, high_x, near1, far1,
    )
    n2, wp, np_, nm, mean, scale, sp, h2, n3, two, one = call(
        conv_kernel,
        [((rim_rows, width), BF), ((rim_rows, units), F32, HBM), ((rim_rows, 256), F32),
         ((rim_rows, units), BF, HBM), ((rim_rows, 128), F32), ((rim_rows, 128), F32),
         (wide, BF, HBM), (tall, F32), (tall, BF),
         (ring.shape, BF, HBM), ((2,) + near1.shape, BF, HBM)],
        [SMEM, FREE] + [ANY] * 18,
        [ring, pltpu.VMEM((2,) + near1.shape, BF), pltpu.VMEM((rim_rows, units), F32),
         pltpu.VMEM((rim_rows, units), F32), pltpu.VMEM((rim_rows, units), BF), pltpu.VMEM(wide, BF),
         pltpu.VMEM((2, rim_rows, 128), F32), dma((16,)), dma((2,)), dma((3, 8))],
        "conv", 15, info, h1, *near2, *far2, near1, far1,
    )
    nearq, _ = lax.optimization_barrier((nearq, n3))
    qkv, wq = call(
        queries_kernel, [((HEADS, 3 * HEAD, rows), BF, FREE), ((2, 8, 192, 256), BF, HBM)],
        [SMEM, VMEM, ANY, ANY], [pltpu.VMEM((2, 8, 192, 256), BF), dma((2,))], "queries", 1,
        info, n3, nearq, send(nearq, flip),
    )
    near = lax.all_to_all(qkv, CHIPS, 0, 0, tiled=True)
    far = send(near[:, HEAD:], flip)
    head_out, expo, inverse, near, far = attend(near, far, lengths, info[:1])
    near3, _ = lax.optimization_barrier((near3, head_out))
    far3 = send(near3, flip)
    heads_in = lax.all_to_all(head_out, CHIPS, 0, 0, tiled=True)
    output, acts, g3, dob, d_gffn, heads_in = call(
        ffn_kernel,
        [(tall, BF), ((rows, 5632), BF, FREE), (tall, F32), ((HEADS, HEAD, rows), BF),
         ((1, width), F32), ((HEADS, HEAD, rows), BF, FREE)],
        [SMEM, VMEM, FREE, VMEM, HBM, HBM, ANY],
        [pltpu.VMEM((2, 2, 4) + pack3.shape, BF), tiny, pltpu.VMEM(tall, F32), pltpu.VMEM(tall, F32),
         dma((5,)), dma((4,))],
        "ffn", 11, info, h2, heads_in, cotangent[0], one, near3, far3,
    )

    d_near = lax.all_to_all(dob, CHIPS, 0, 0, tiled=True)
    early = call(
        early_kernel, [((2, 2, 4, 4, EARLY, 128), BF)], [SMEM] + [FREE] * 4, [], "early", 0.3,
        info, acts, heads_in, send(acts, flip), send(heads_in, flip),
    )[0]
    d_near, early = lax.optimization_barrier((d_near, early))
    early = over_x(early)
    keep, give = attend_back(near, far, expo, head_out, inverse, d_near)
    take = jnp.pad(send(give, flip), ((0, 0), (HEAD, 0), (0, 0)))
    d_qkv = (keep.astype(F32) + take.astype(F32)).astype(BF)
    d_qkv = lax.all_to_all(d_qkv, CHIPS, 0, 0, tiled=True)
    early = over_z(early)
    sp2, n32 = send(sp, flip), send(n3, flip)
    info_attn, _ = lax.optimization_barrier((info, sp2))
    g2, gs, lo, hi, d_gatt = call(
        attn_in_kernel,
        [(tall, F32), (narrow, BF, FREE), ((RIM, 256), BF), ((RIM, 256), BF), ((1, width), F32)],
        [SMEM, FREE] + [HBM] * 4,
        [pltpu.VMEM((2, 8, 192, 256), BF), tiny, pltpu.VMEM(tall, F32), pltpu.VMEM(tall, F32),
         dma((4,))],
        "attn_in", 0.5, info_attn, d_qkv, h2, g3, one, wq,
    )
    low_gs = send(hi, along(1))
    high_gs = send(lo, along(-1))
    info_mid, _, _ = lax.optimization_barrier((info, low_gs, high_gs))
    middle = call(
        middle_kernel, [((8, 8, MIDDLE, 128), BF)], [SMEM, VMEM, FREE, VMEM, FREE] + [FREE] * 4, [], "middle", 0.3,
        info_mid, sp, gs, n3, d_qkv, sp2, send(gs, flip), n32, send(d_qkv, flip),
    )[0]
    info_conv, middle = lax.optimization_barrier((info, middle))
    middle = lax.all_to_all(middle.reshape(64, MIDDLE, 128), CHIPS + WT, 0, 0, tiled=True)
    rim_narrow = ((rim_rows, 256), BF)
    dw, dnar, table = call(
        conv_back_kernel, [(wide, BF, FREE), ((rim_rows, 256), BF, FREE), ((16, units), F32, FREE)],
        [SMEM, FREE, FREE, FREE] + [VMEM] * 3 + [HBM] * 4,
        [pltpu.VMEM((2, 4, 256, 256), BF), tiny, pltpu.VMEM((2, rim_rows, 128), F32),
         pltpu.VMEM((2, rim_rows + 2 * RIM, 128), F32), pltpu.VMEM((rim_rows, units), F32),
         pltpu.VMEM((rim_rows, units), F32), pltpu.VMEM((rim_rows, units), BF),
         pltpu.VMEM((rim_rows, units), F32), dma((2,)), dma((2, 8))],
        "conv_back", 2, info_conv, low_gs, gs, high_gs, np_, mean, scale, nm, wp, two, one,
    )
    dw2, dnar2 = send(dw, flip), send(dnar, flip)
    info_glu, early = lax.optimization_barrier((info, early))
    dx, dab, sums = call(
        glu_back_kernel,
        [(tall, F32), ((rows, 2 * width), BF, FREE), ((24, units), F32, FREE)],
        [SMEM, FREE, FREE, HBM, HBM, HBM, VMEM, HBM, HBM, HBM, FREE, VMEM, VMEM],
        [pltpu.VMEM((2, 2, 4, 448, 256), BF), pltpu.VMEM((2, 8, 128, 256), BF), tiny,
         pltpu.VMEM((rim_rows, 256), F32), pltpu.VMEM(tall, F32), pltpu.VMEM(tall, BF),
         pltpu.VMEM(tall, BF), pltpu.VMEM(tall, BF), dma((8,))],
        "glu_back", 1, info_glu, dw, dnar, h1m, two, one, g2, a, sg, x, table, d_gatt, d_gffn,
    )
    dab2, sums2 = send(dab, flip), send(sums, flip)
    middle = jnp.sum(middle.astype(F32), 0).astype(BF)
    late = call(
        late_kernel, [((8, 8, LATE, 128), BF)], [SMEM, VMEM, FREE, FREE, VMEM, FREE, FREE] + [FREE] * 6,
        [pltpu.VMEM((rim_rows, width), F32), pltpu.VMEM((rim_rows, 256), F32)], "late", 0.5,
        info, n2, dw, dnar, n1, dab, sums, send(n2, flip), dw2, dnar2, send(n1, flip), dab2, sums2,
    )[0]
    _, early = lax.optimization_barrier((late, early))
    y = lax.axis_index("y")
    pick = lambda index: lax.dynamic_index_in_dim(early, index % 4, 0, keepdims=False)
    parts = [send(pick(y + d), shift(dy=d)) for d in (1, 2, 3)]
    early = call(
        fold_kernel, [((EARLY, 128), BF, FREE)], [FREE] * 4, [], "fold", FOLD, pick(y), *parts
    )[0]
    late = lax.all_to_all(late.reshape(64, LATE, 128), CHIPS + WT, 0, 0, tiled=True)
    late = jnp.sum(late.astype(F32), 0).astype(BF)
    final = spread_out(jnp.concatenate([early, middle, late], 0), CHIPS, 8)
    square, broad = ((64, 512), F32), ((64, 2048), F32)
    line = ((1, 64), F32)
    grads = call(
        unpack_kernel,
        [line, square, square, line, broad, ((3, 64, 256), F32), ((1, 256), F32),
         ((9, 256), F32), ((256, 256), F32), line, square, square, square, square, line, broad,
         ((256, 512), F32)],
        [SMEM, ANY, ANY],
        [pltpu.VMEM((2,) + final.shape, BF), pltpu.VMEM((512, 256), F32),
         pltpu.VMEM((256, 256), F32), pltpu.VMEM((16, 256), F32), dma((2,))],
        "unpack", 3, info, final, send(final, flip),
    )
    grads = [g[0] if g.shape[0] == 1 else g for g in grads]
    return (output[None], dx[None]) + tuple(grads)


def solution(mesh):
    fine = Mesh(mesh.devices.reshape(SIZES), AXES)
    flat, row, mid = P(WT), P(WT, None), P(None, WT, None)
    col = P(None, WT)
    tokens = P(WT, CTX, None)
    weights = (
        flat, row, row, flat, row, mid, flat, col, row, flat, row, row, row, row, flat, row, row,
    )
    return jax.shard_map(
        shards, mesh=fine, in_specs=(tokens, flat, tokens) + weights,
        out_specs=(tokens, tokens) + weights, check_vma=False,
    )
```
